32 devices in a mesh: scen: 4 (over y, core), vox: 8 (over z, x).
Axes of the slice: x: 2, y: 2, z: 4, core: 2. Of those that a mesh axis runs over, the one named last changes fastest.
Arguments:
- dose_blocks: float32 [8, 640, 128, 128], P('scen', 'vox'), may hold values from 0 to 0.046875
- block_map: int32 [640, 2], P('vox'), may hold values from 0 to 127, as said below
- block_counts: int32 [8], P('vox'), may hold values from 10 to 80, as said below
- target: float32 [131072], P('vox'), may hold values from 0.5 to 15
- fluence_init: float32 [16384], P('vox'), may hold values from 0.5 to 1.5
Outputs:
- fluence: float32 [16384], P('vox')
- weights: float32 [8, 131072], P('scen', 'vox')
The draws below stay inside these ranges and needn't reach their ends.
Inputs may be any that keep to these rules, and one draw needn't show every extreme that they name: `block_map`: column 0 is a row block of the slot's voxel group, 0 to 127; column 1 a beamlet block, 0 to 127; pairs may repeat. `block_counts`: the slots in use are the first ones of their group; some group uses all 80.
All inputs are finite; a program needn't handle non-finite values.
Results may differ from the reference program's by a relative error of at most 0.0003.
Values sent between devices are 32-bit elements; how exact they have to be, the bound alone decides.
No kernel may reach another device: no remote copies, remote signals or barrier semaphores. Data moves between devices by JAX's collectives and lax.ppermute only.
A program may use at most 64 MiB of HBM per device.

```python
import jax
import jax.numpy as jnp
from jax import lax

BS = 128
BEAMLETS = 16384
VOX_DEV = 16384
NB = 80
ROUNDS = 2
ITERS = 2
SCEN = 8
VOXELS = 131072
NBLK = 640
N_VOX = 8


def draw_block_map(key, part):
    first_key, second_key = jax.random.split(jax.random.fold_in(key, 11))
    row_ids = jax.random.randint(first_key, (NB * N_VOX,), 0, VOX_DEV // BS)
    col_ids = jax.random.randint(second_key, (NB * N_VOX,), 0, BEAMLETS // BS)
    row_ids = row_ids.at[0].set(VOX_DEV // BS - 1)
    col_ids = col_ids.at[0].set(BEAMLETS // BS - 1)
    return jnp.stack([row_ids, col_ids], axis=1).astype(jnp.int32)


def draw_block_counts(key, part):
    first_key, second_key = jax.random.split(jax.random.fold_in(key, 23))
    counts = jax.random.randint(first_key, (N_VOX,), max(1, NB // 8), NB // 2 + 1)
    chosen = jax.random.randint(second_key, (), 0, N_VOX)
    counts = jnp.where(jnp.arange(N_VOX) == chosen, NB, counts)
    return counts.astype(jnp.int32)


def draw_target(key, part):
    mapping = draw_block_map(key, part)
    first_rows = mapping[jnp.arange(N_VOX) * NB, 0]
    base_key, plant_key = jax.random.split(jax.random.fold_in(key, 37))
    voxel = jnp.arange(VOXELS)
    group = voxel // VOX_DEV
    local = voxel % VOX_DEV
    planted = (local // BS == first_rows[group]) & (local % BS % 16 == 0)
    drawn = jax.random.uniform(base_key, (VOXELS,), jnp.float32, 0.5, 1.5)
    strength = jax.random.uniform(plant_key, (VOXELS,), jnp.float32, 4.0, 15.0)
    strength = jnp.where(voxel == VOX_DEV - BS, 15.0, strength)
    return jnp.where(planted, strength, drawn).astype(jnp.float32)


def shard_levels(own_key, dims, cuts, least, top_value):
    def one(dim, shards_of):
        steps = jax.random.uniform(jax.random.fold_in(jax.random.fold_in(own_key, 6), dim), (shards_of,), jnp.float32, least / len(cuts), top_value / len(cuts))
        return jnp.repeat(jnp.exp(steps), dims[dim] // shards_of).reshape((-1,) + (1,) * (len(dims) - dim - 1))

    loudness = one(*cuts[0])
    for cut in cuts[1:]:
        loudness = loudness * one(*cut)
    return loudness


def setup_inputs(seed: int = 0) -> dict:
    keys = jax.random.split(jax.random.key(seed), 6)
    return {
        "dose_blocks": jnp.clip(0.046875 * jax.random.uniform(keys[0], (SCEN, NBLK, BS, BS), jnp.float32) ** shard_levels(keys[0], (SCEN, NBLK, BS, BS), ((0, 4), (1, 8)), -0.2, 0.2), 0.0, 0.046875),
        "block_map": draw_block_map(jax.random.fold_in(keys[5], 71), 0),
        "block_counts": draw_block_counts(jax.random.fold_in(keys[5], 71), 0),
        "target": draw_target(jax.random.fold_in(keys[5], 71), 0),
        "fluence_init": jnp.clip(0.5 + 1.0 * jax.random.uniform(keys[4], (BEAMLETS,), jnp.float32) ** shard_levels(keys[4], (BEAMLETS,), ((0, 8),), -0.2, 0.2), 0.5, 1.5),
    }


HIGHEST = lax.Precision.HIGHEST
SHARPNESS = 2.0
STEP_SIZE = 0.5


def reference(dose_blocks, block_map, block_counts, target, fluence_init):
    slots = jnp.arange(NBLK).astype(jnp.int32)
    groups = (slots // NB).astype(jnp.int32)
    usable = ((slots - groups * NB) < block_counts[groups]).astype(jnp.float32)
    row_ids = (groups * (VOX_DEV // BS) + block_map[:, 0]).astype(jnp.int32)
    row_hot = (row_ids[:, None] == jnp.arange(VOXELS // BS).astype(jnp.int32)[None, :]).astype(jnp.float32) * usable[:, None]
    col_hot = (block_map[:, 1][:, None] == jnp.arange(BEAMLETS // BS).astype(jnp.int32)[None, :]).astype(jnp.float32)

    def forward(copies):
        pieces = copies.reshape(SCEN, BEAMLETS // BS, BS)
        picked = jnp.einsum("nb,sbj->snj", col_hot, pieces, precision=HIGHEST)
        products = jnp.einsum("snij,snj->sni", dose_blocks, picked, precision=HIGHEST)
        summed = jnp.einsum("nr,sni->sri", row_hot, products, precision=HIGHEST)
        return summed.reshape(SCEN, VOXELS)

    def backward(weighted):
        pieces = weighted.reshape(SCEN, VOXELS // BS, BS)
        picked = jnp.einsum("nr,sri->sni", row_hot, pieces, precision=HIGHEST)
        products = jnp.einsum("snij,sni->snj", dose_blocks, picked, precision=HIGHEST)
        summed = jnp.einsum("nb,snj->sbj", col_hot, products, precision=HIGHEST)
        return summed.reshape(SCEN, BEAMLETS)

    fluence = fluence_init
    weights = jnp.zeros((SCEN, VOXELS), jnp.float32)
    for outer_round in range(ROUNDS):
        copies = jnp.broadcast_to(fluence[None, :], (SCEN, BEAMLETS))
        for inner_step in range(ITERS):
            dose = forward(copies)
            excess = dose - target[None, :]
            if inner_step == 0:
                weights = jax.nn.softmax(SHARPNESS * excess * excess, axis=0)
            gradient = backward(2.0 * weights * excess)
            copies = jnp.maximum(copies - STEP_SIZE * gradient, 0.0)
        fluence = jnp.mean(copies, axis=0)
    return fluence, weights
```

```python
import functools

import jax
import jax.numpy as jnp
from jax import lax
from jax.experimental import pallas as pl
from jax.experimental.pallas import tpu as pltpu
from jax.sharding import PartitionSpec as P

ROUNDS = 2
SHARPNESS = 2.0
STEP_SIZE = 0.5
F32 = jnp.float32
BF16 = jnp.bfloat16
VMEM = pl.BlockSpec(memory_space=pltpu.VMEM)


def split3(x):
    high = x.astype(BF16)
    rest = x - high.astype(F32)
    mid = rest.astype(BF16)
    low = (rest - mid.astype(F32)).astype(BF16)
    return jnp.concatenate([high, mid, low], axis=-1)


def exact(hot, x):
    n = x.shape[1]
    y = jnp.dot(hot, split3(x), preferred_element_type=F32)
    return y[:, :n] + y[:, n : 2 * n] + y[:, 2 * n :]


def columns(x):
    pad = -x.shape[0] % 128
    if pad:
        x = jnp.concatenate([x, jnp.zeros((pad, x.shape[1]), x.dtype)], axis=0)
    return x.T


def products(blocks, vectors, rows):
    scen, slots, side, _ = blocks.shape
    for k in range(slots):
        for s in range(scen):
            if s == 0 or vectors[s] is not vectors[0]:
                wide = jnp.broadcast_to(vectors[s][:, k : k + 1], (side, side))
            rows[s, k : k + 1, :] = jnp.sum(blocks[s, k] * wide, axis=0, keepdims=True)


def merge(a, b):
    top = jnp.maximum(a, b)
    return top + jnp.log(jnp.exp(a - top) + jnp.exp(b - top))


def prepare_kernel(blocks, block_map, counts, flipped, row_hot, row_hot_t, col_hot, col_hot_t):
    scen, slots, side, _ = blocks.shape
    row_blocks, beam_blocks = row_hot.shape[1], col_hot.shape[1]
    slot = lax.broadcasted_iota(jnp.int32, (slots, row_blocks), 0)
    usable = slot < counts[0]
    rows = lax.broadcasted_iota(jnp.int32, (slots, row_blocks), 1) == block_map[:, 0:1]
    cols = lax.broadcasted_iota(jnp.int32, (slots, beam_blocks), 1) == block_map[:, 1:2]
    row = jnp.where(rows & usable, 1.0, 0.0).astype(F32)
    col = jnp.where(cols, 1.0, 0.0).astype(F32)
    row_hot[...] = row.astype(BF16)
    col_hot[...] = col.astype(BF16)
    row_hot_t[...] = columns(row)[:, :slots].astype(BF16)
    col_hot_t[...] = columns(col)[:, :slots].astype(BF16)

    def flip(k, _):
        for s in range(scen):
            flipped[s, k] = blocks[s, k].T
        return 0

    lax.fori_loop(0, slots, flip, 0)


def first_kernel(flipped, fluence, target, col_hot, row_hot_t, excess, score_sum, rows):
    scen = flipped.shape[0]
    vector = columns(exact(col_hot[...], fluence[...]))
    products(flipped, [vector] * scen, rows)
    scores = []
    for s in range(scen):
        e = exact(row_hot_t[...], rows[s]) - target[...]
        excess[s] = e
        scores.append(SHARPNESS * e * e)
    top = functools.reduce(jnp.maximum, scores)
    total = functools.reduce(jnp.add, [jnp.exp(score - top) for score in scores])
    score_sum[...] = top + jnp.log(total)


def second_kernel(blocks, excess, sum_a, sum_b, row_hot, col_hot_t, weights, gradient, rows):
    scen = blocks.shape[0]
    total = merge(sum_a[...], sum_b[...])
    vectors = []
    for s in range(scen):
        e = excess[s]
        w = jnp.exp(SHARPNESS * e * e - total)
        weights[s] = w
        vectors.append(columns(exact(row_hot[...], 2.0 * w * e)))
    products(blocks, vectors, rows)
    for s in range(scen):
        gradient[s] = exact(col_hot_t[...], rows[s])


def third_kernel(
    blocks, flipped, fluence, grad_a, grad_b, weights, target,
    col_hot, col_hot_t, row_hot, row_hot_t, copies, gradient, rows
):
    scen = blocks.shape[0]
    vectors = []
    for s in range(scen):
        c = jnp.maximum(fluence[...] - STEP_SIZE * (grad_a[s] + grad_b[s]), 0.0)
        copies[s] = c
        vectors.append(columns(exact(col_hot[...], c)))
    products(flipped, vectors, rows)
    vectors = []
    for s in range(scen):
        e = exact(row_hot_t[...], rows[s]) - target[...]
        vectors.append(columns(exact(row_hot[...], 2.0 * weights[s] * e)))
    products(blocks, vectors, rows)
    for s in range(scen):
        gradient[s] = exact(col_hot_t[...], rows[s])


def near(x):
    return pltpu.with_memory_space_constraint(x, pltpu.VMEM)


def swap(x, axis, bit):
    return lax.ppermute(x, axis, [(i, i ^ bit) for i in range(lax.axis_size(axis))])


def bits(axis):
    size = lax.axis_size(axis)
    if size & (size - 1) or size < 2:
        raise ValueError("axis size")
    return [1 << b for b in range(size.bit_length() - 1)]


def reduce_but_last(x, axis, combine):
    steps = bits(axis)
    for bit in steps[:-1]:
        x = combine(x, swap(x, axis, bit))
    return x, swap(x, axis, steps[-1])


def gather(x, axis):
    me = lax.axis_index(axis)
    for bit in bits(axis):
        other = swap(x, axis, bit)
        x = jnp.where(
            me & bit == 0, jnp.concatenate([x, other], axis=0), jnp.concatenate([other, x], axis=0)
        )
    return x


def body(dose_blocks, block_map, block_counts, target, fluence_init):
    scen, slots, side, _ = dose_blocks.shape
    share = fluence_init.shape[0]
    parts = lax.axis_size("vox")
    beam_blocks = share * parts // side
    row_blocks = target.shape[0] // side
    scen_total = scen * lax.axis_size("scen")
    params = pltpu.CompilerParams(vmem_limit_bytes=16 * 2**20)
    passes = scen * slots * side * side
    dense = lambda *shape: jax.ShapeDtypeStruct(shape, F32)
    scratch = [pltpu.VMEM((scen, slots, side), F32)]

    blocks = near(dose_blocks)
    target = target.reshape(row_blocks, side)
    flipped, row_hot, row_hot_t, col_hot, col_hot_t = pl.pallas_call(
        prepare_kernel,
        name="prepare",
        out_shape=(
            pltpu.VMEM((scen, slots, side, side), F32),
            jax.ShapeDtypeStruct((slots, row_blocks), BF16),
            jax.ShapeDtypeStruct((row_blocks, slots), BF16),
            jax.ShapeDtypeStruct((slots, beam_blocks), BF16),
            jax.ShapeDtypeStruct((beam_blocks, slots), BF16),
        ),
        in_specs=[VMEM, VMEM, pl.BlockSpec(memory_space=pltpu.SMEM)],
        out_specs=(VMEM,) * 5,
        compiler_params=params,
        cost_estimate=pl.CostEstimate(flops=passes, bytes_accessed=8 * passes, transcendentals=0),
    )(blocks, block_map, block_counts)
    flipped = near(flipped)

    fluence = gather(fluence_init.reshape(share // side, side), "vox")
    for outer_round in range(ROUNDS):
        excess, score_sum = pl.pallas_call(
            first_kernel,
            name="first",
            out_shape=(dense(scen, row_blocks, side), dense(row_blocks, side)),
            in_specs=[VMEM] * 5,
            out_specs=(VMEM,) * 2,
            scratch_shapes=scratch,
            compiler_params=params,
        )(flipped, fluence, target, col_hot, row_hot_t)
        sum_a, sum_b = reduce_but_last(score_sum, "scen", merge)
        weights, gradient = pl.pallas_call(
            second_kernel,
            name="second",
            out_shape=(dense(scen, row_blocks, side), dense(scen, beam_blocks, side)),
            in_specs=[VMEM] * 6,
            out_specs=(VMEM,) * 2,
            scratch_shapes=scratch,
            compiler_params=params,
        )(blocks, excess, sum_a, sum_b, row_hot, col_hot_t)
        grad_a, grad_b = reduce_but_last(gradient, "vox", jnp.add)
        copies, gradient = pl.pallas_call(
            third_kernel,
            name="third",
            out_shape=(dense(scen, beam_blocks, side), dense(scen, beam_blocks, side)),
            in_specs=[VMEM] * 11,
            out_specs=(VMEM,) * 2,
            scratch_shapes=scratch,
            compiler_params=params,
        )(
            blocks, flipped, fluence, grad_a, grad_b, weights, target,
            col_hot, col_hot_t, row_hot, row_hot_t,
        )
        if outer_round < ROUNDS - 1:
            grad_a, grad_b = reduce_but_last(gradient, "vox", jnp.add)
        else:
            pieces = gradient.reshape(scen, parts, share // side, side)
            pieces = lax.all_to_all(pieces, "vox", split_axis=1, concat_axis=1, tiled=True)
            grad_a, grad_b = jnp.sum(pieces, axis=1), 0.0
            start = lax.axis_index("vox") * (share // side)
            copies = lax.dynamic_slice_in_dim(copies, start, share // side, 1)
        copies = jnp.maximum(copies - STEP_SIZE * (grad_a + grad_b), 0.0)
        mean_a, mean_b = reduce_but_last(jnp.sum(copies, axis=0), "scen", jnp.add)
        fluence = (mean_a + mean_b) / scen_total
    return fluence.reshape(share), weights.reshape(scen, row_blocks * side)


def solution(mesh):
    placed = (P("scen", "vox", None, None), P("vox", None), P("vox"), P("vox"), P("vox"))
    return jax.shard_map(
        body, mesh=mesh, in_specs=placed, out_specs=(P("vox"), P("scen", "vox")), check_vma=False
    )
```

```python
import functools

import jax
import jax.numpy as jnp
from jax import lax
from jax.experimental import pallas as pl
from jax.experimental.pallas import tpu as pltpu
from jax.sharding import PartitionSpec as P

ROUNDS = 2
SHARPNESS = 2.0
STEP_SIZE = 0.5
F32 = jnp.float32
BF16 = jnp.bfloat16
VMEM = pl.BlockSpec(memory_space=pltpu.VMEM)


def split3(x):
    high = x.astype(BF16)
    rest = x - high.astype(F32)
    mid = rest.astype(BF16)
    low = (rest - mid.astype(F32)).astype(BF16)
    return jnp.concatenate([high, mid, low], axis=-1)


def exact(hot, x):
    n = x.shape[1]
    y = jnp.dot(hot, split3(x), preferred_element_type=F32)
    return y[:, :n] + y[:, n : 2 * n] + y[:, 2 * n :]


def columns(x):
    pad = -x.shape[0] % 128
    if pad:
        x = jnp.concatenate([x, jnp.zeros((pad, x.shape[1]), x.dtype)], axis=0)
    return x.T


def flat(x):
    pad = -x.shape[1] % 128
    slots = x.shape[1]
    if pad:
        x = jnp.concatenate([x, jnp.zeros((x.shape[0], pad), x.dtype)], axis=1)
    return x.T[:slots]


def products(blocks, vectors, rows):
    scen, slots, side, _ = blocks.shape
    for k in range(slots):
        for s in range(scen):
            if s == 0 or vectors[s] is not vectors[0]:
                wide = jnp.broadcast_to(vectors[s][:, k : k + 1], (side, side))
            rows[s, k : k + 1, :] = jnp.sum(blocks[s, k] * wide, axis=0, keepdims=True)


def merge(a, b):
    top = jnp.maximum(a, b)
    return top + jnp.log(jnp.exp(a - top) + jnp.exp(b - top))


def flip_kernel(blocks, flipped):
    scen, slots, _, _ = blocks.shape
    group = next(n for n in (8, 4, 2, 1) if slots % n == 0)

    def flip(t, _):
        for u in range(group):
            for s in range(scen):
                flipped[s, t * group + u] = blocks[s, t * group + u].T
        return 0

    lax.fori_loop(0, slots // group, flip, 0)


def hot_kernel(block_map, counts, row_hot, row_hot_t, col_hot, col_hot_t):
    row_blocks, slots = row_hot_t.shape
    usable = lax.broadcasted_iota(jnp.int32, (row_blocks, slots), 1) < counts[0]
    rows = lax.broadcasted_iota(jnp.int32, (row_blocks, slots), 0) == block_map[0:1, :]
    row = jnp.where(rows & usable, 1.0, 0.0).astype(F32)
    beam_blocks = col_hot_t.shape[0]
    cols = lax.broadcasted_iota(jnp.int32, (beam_blocks, slots), 0) == block_map[1:2, :]
    col = jnp.where(cols, 1.0, 0.0).astype(F32)
    row_hot_t[...] = row.astype(BF16)
    col_hot_t[...] = col.astype(BF16)
    row_hot[...] = flat(row).astype(BF16)
    col_hot[...] = flat(col).astype(BF16)


def finish_first(rows, target, row_hot_t, excess, score_sum):
    scores = []
    for s in range(len(rows)):
        e = exact(row_hot_t[...], rows[s]) - target[...]
        excess[s] = e
        scores.append(SHARPNESS * e * e)
    top = functools.reduce(jnp.maximum, scores)
    total = functools.reduce(jnp.add, [jnp.exp(score - top) for score in scores])
    score_sum[...] = top + jnp.log(total)


def first_kernel(flipped, fluence, target, col_hot, row_hot_t, excess, score_sum, rows):
    scen = flipped.shape[0]
    vector = columns(exact(col_hot[...], fluence[...]))
    products(flipped, [vector] * scen, rows)
    finish_first([rows[s] for s in range(scen)], target, row_hot_t, excess, score_sum)


def open_kernel(sizes, source, fluence, target, col_hot, row_hot_t, blocks, excess, score_sum, sems):
    scen, slots, side, _ = source.shape
    copies, first = [], 0
    for n, size in enumerate(sizes):
        part = pl.ds(first, size)
        copies.append(pltpu.make_async_copy(source.at[:, part], blocks.at[:, part], sems.at[n]))
        first += size
    for copy in copies:
        copy.start()
    picked = exact(col_hot[...], fluence[...])
    lane = lax.broadcasted_iota(jnp.int32, (side, -(-slots // 128) * 128), 1)
    sums = [jnp.zeros(lane.shape, F32) for _ in range(scen)]
    first = 0
    for copy, size in zip(copies, sizes):
        copy.wait()
        for k in range(first, first + size):
            for s in range(scen):
                total = jnp.sum(blocks[s, k] * picked[k : k + 1, :], axis=1, keepdims=True)
                sums[s] = jnp.where(lane == k, total, sums[s])
        first += size
    finish_first([x.T[:slots] for x in sums], target, row_hot_t, excess, score_sum)


def second_kernel(blocks, excess, sum_a, sum_b, row_hot, col_hot_t, weights, gradient, rows):
    scen = excess.shape[0]
    total = merge(sum_a[...], sum_b[...])
    vectors = []
    for s in range(scen):
        e = excess[s]
        w = jnp.exp(SHARPNESS * e * e - total)
        weights[s] = w
        vectors.append(columns(exact(row_hot[...], 2.0 * w * e)))
    products(blocks, vectors, rows)
    for s in range(scen):
        gradient[s] = exact(col_hot_t[...], rows[s])


def third_kernel(
    blocks, flipped, fluence, grad_a, grad_b, weights, target,
    col_hot, col_hot_t, row_hot, row_hot_t, copies, gradient, rows
):
    scen = weights.shape[0]
    vectors = []
    for s in range(scen):
        c = jnp.maximum(fluence[...] - STEP_SIZE * (grad_a[s] + grad_b[s]), 0.0)
        copies[s] = c
        vectors.append(columns(exact(col_hot[...], c)))
    products(flipped, vectors, rows)
    vectors = []
    for s in range(scen):
        e = exact(row_hot_t[...], rows[s]) - target[...]
        vectors.append(columns(exact(row_hot[...], 2.0 * weights[s] * e)))
    products(blocks, vectors, rows)
    for s in range(scen):
        gradient[s] = exact(col_hot_t[...], rows[s])


def near(x):
    return pltpu.with_memory_space_constraint(x, pltpu.VMEM)


def swap(x, axis, bit):
    return lax.ppermute(x, axis, [(i, i ^ bit) for i in range(lax.axis_size(axis))])


def bits(axis):
    size = lax.axis_size(axis)
    if size & (size - 1) or size < 2:
        raise ValueError("axis size")
    return [1 << b for b in range(size.bit_length() - 1)]


def reduce_vox(x):
    steps = bits("vox")
    for bit in steps[:-1]:
        x = x + swap(x, "vox", bit)
    return x, swap(x, "vox", steps[-1])


def reduce_scen(x, combine):
    steps = bits("scen")
    x = [x, swap(x, "scen", steps[0])]
    for bit in steps[1:]:
        both = combine(*x)
        x = [both, swap(both, "scen", bit ^ 1)]
    return x


def swap_both(x, bit):
    scen, vox = lax.axis_size("scen"), lax.axis_size("vox")
    pairs = [(s * vox + v, (s ^ 1) * vox + (v ^ bit)) for s in range(scen) for v in range(vox)]
    return lax.ppermute(x, ("scen", "vox"), pairs)


def split(total, parts):
    return [total * (n + 1) // parts - total * n // parts for n in range(parts)]


def body(dose_blocks, block_map, block_counts, target, fluence_init):
    scen, slots, side, _ = dose_blocks.shape
    share = fluence_init.shape[0]
    parts = lax.axis_size("vox")
    beam_blocks = share * parts // side
    row_blocks = target.shape[0] // side
    scen_total = scen * lax.axis_size("scen")
    params = pltpu.CompilerParams(vmem_limit_bytes=16 * 2**20)
    passes = scen * slots * side * side
    dense = lambda *shape: jax.ShapeDtypeStruct(shape, F32)
    scratch = [pltpu.VMEM((scen, slots, side), F32)]

    target = target.reshape(row_blocks, side)
    row_hot, row_hot_t, col_hot, col_hot_t = pl.pallas_call(
        hot_kernel,
        name="hot",
        out_shape=(
            jax.ShapeDtypeStruct((slots, row_blocks), BF16),
            jax.ShapeDtypeStruct((row_blocks, slots), BF16),
            jax.ShapeDtypeStruct((slots, beam_blocks), BF16),
            jax.ShapeDtypeStruct((beam_blocks, slots), BF16),
        ),
        in_specs=[VMEM, pl.BlockSpec(memory_space=pltpu.SMEM)],
        out_specs=(VMEM,) * 4,
        compiler_params=params,
    )(block_map.T, block_counts)

    fluence = fluence_init.reshape(share // side, side)
    me = lax.axis_index("vox")
    for bit in bits("vox"):
        other = swap_both(fluence, bit)
        fluence = jnp.where(
            me & bit == 0,
            jnp.concatenate([fluence, other], axis=0),
            jnp.concatenate([other, fluence], axis=0),
        )

    whole = pltpu.VMEM((scen, slots, side, side), F32)
    for outer_round in range(ROUNDS):
        if outer_round == 0:
            sizes = split(slots, 10)
            blocks, excess, score_sum = pl.pallas_call(
                functools.partial(open_kernel, sizes),
                name="open",
                out_shape=(whole, dense(scen, row_blocks, side), dense(row_blocks, side)),
                in_specs=[pl.BlockSpec(memory_space=pltpu.HBM)] + [VMEM] * 4,
                out_specs=(VMEM,) * 3,
                scratch_shapes=[pltpu.SemaphoreType.DMA((len(sizes),))],
                compiler_params=params,
            )(
                pltpu.with_memory_space_constraint(dose_blocks, pltpu.HBM),
                fluence, target, col_hot, row_hot_t,
            )
            blocks = near(blocks)
            flipped = pl.pallas_call(
                flip_kernel,
                name="flip",
                out_shape=whole,
                in_specs=[VMEM],
                out_specs=VMEM,
                compiler_params=params,
                cost_estimate=pl.CostEstimate(
                    flops=0, bytes_accessed=8 * passes, transcendentals=0
                ),
            )(blocks)
            flipped = near(flipped)
        else:
            excess, score_sum = pl.pallas_call(
                first_kernel,
                name="first",
                out_shape=(dense(scen, row_blocks, side), dense(row_blocks, side)),
                in_specs=[VMEM] * 5,
                out_specs=(VMEM,) * 2,
                scratch_shapes=scratch,
                compiler_params=params,
            )(flipped, fluence, target, col_hot, row_hot_t)
        sum_a, sum_b = reduce_scen(score_sum, merge)
        weights, gradient = pl.pallas_call(
            second_kernel,
            name="second",
            out_shape=(dense(scen, row_blocks, side), dense(scen, beam_blocks, side)),
            in_specs=[VMEM] * 6,
            out_specs=(VMEM,) * 2,
            scratch_shapes=scratch,
            compiler_params=params,
        )(blocks, excess, sum_a, sum_b, row_hot, col_hot_t)
        grad_a, grad_b = reduce_vox(gradient)
        copies, gradient = pl.pallas_call(
            third_kernel,
            name="third",
            out_shape=(dense(scen, beam_blocks, side), dense(scen, beam_blocks, side)),
            in_specs=[VMEM] * 11,
            out_specs=(VMEM,) * 2,
            scratch_shapes=scratch,
            compiler_params=params,
        )(
            blocks, flipped, fluence, grad_a, grad_b, weights, target,
            col_hot, col_hot_t, row_hot, row_hot_t,
        )
        if outer_round < ROUNDS - 1:
            grad_a, grad_b = reduce_vox(gradient)
        else:
            pieces = gradient.reshape(scen, parts, share // side, side)
            pieces = lax.all_to_all(pieces, "vox", split_axis=1, concat_axis=1, tiled=True)
            grad_a, grad_b = jnp.sum(pieces, axis=1), 0.0
            start = lax.axis_index("vox") * (share // side)
            copies = lax.dynamic_slice_in_dim(copies, start, share // side, 1)
        copies = jnp.maximum(copies - STEP_SIZE * (grad_a + grad_b), 0.0)
        mean_a, mean_b = reduce_scen(jnp.sum(copies, axis=0), jnp.add)
        fluence = (mean_a + mean_b) / scen_total
    return fluence.reshape(share), weights.reshape(scen, row_blocks * side)


def solution(mesh):
    placed = (P("scen", "vox", None, None), P("vox", None), P("vox"), P("vox"), P("vox"))
    return jax.shard_map(
        body, mesh=mesh, in_specs=placed, out_specs=(P("vox"), P("scen", "vox")), check_vma=False
    )
```

```python
import functools

import jax
import jax.numpy as jnp
from jax import lax
from jax.experimental import pallas as pl
from jax.experimental.pallas import tpu as pltpu
from jax.sharding import PartitionSpec as P

ROUNDS = 2
SHARPNESS = 2.0
STEP_SIZE = 0.5
F32 = jnp.float32
BF16 = jnp.bfloat16
VMEM = pl.BlockSpec(memory_space=pltpu.VMEM)


def split3(x):
    return jnp.concatenate(pieces(x), axis=-1)


def exact(hot, x):
    n = x.shape[1]
    y = jnp.dot(hot, split3(x), preferred_element_type=F32)
    return y[:, :n] + y[:, n : 2 * n] + y[:, 2 * n :]


def columns(x):
    pad = -x.shape[0] % 128
    if pad:
        x = jnp.concatenate([x, jnp.zeros((pad, x.shape[1]), x.dtype)], axis=0)
    return x.T


def flat(x):
    pad = -x.shape[1] % 128
    slots = x.shape[1]
    if pad:
        x = jnp.concatenate([x, jnp.zeros((x.shape[0], pad), x.dtype)], axis=1)
    return x.T[:slots]


def pieces(x):
    high = x.astype(BF16)
    rest = x - high.astype(F32)
    mid = rest.astype(BF16)
    return high, mid, (rest - mid.astype(F32)).astype(BF16)


def products(blocks, picked, rows):
    scen, slots, side, _ = blocks.shape
    index = [lax.broadcasted_iota(jnp.int32, (side, side), n) for n in range(2)]
    eye = jnp.where(index[0] == index[1], 1.0, 0.0).astype(BF16)
    ones = jnp.ones((3 * side, side), BF16)
    turned = {id(x): columns(x) for x in picked}
    parts = {id(x): pieces(x) for x in picked}
    count = 0
    for k in range(slots):
        wide = {}
        for s in range(scen):
            key = id(picked[s])
            if key not in wide:
                if count % 2:
                    wide[key] = jnp.broadcast_to(turned[key][:, k : k + 1], (side, side))
                else:
                    diagonals = [eye * x[k : k + 1, :] for x in parts[key]]
                    wide[key] = jnp.dot(
                        jnp.concatenate(diagonals, axis=1), ones, preferred_element_type=F32
                    )
                count += 1
            rows[s, k : k + 1, :] = jnp.sum(blocks[s, k] * wide[key], axis=0, keepdims=True)


def merge(a, b):
    top = jnp.maximum(a, b)
    return top + jnp.log(jnp.exp(a - top) + jnp.exp(b - top))


def load_kernel(sizes, source, blocks, flipped, sems):
    scen = source.shape[0]
    copies, first = [], 0
    for n, size in enumerate(sizes):
        part = pl.ds(first, size)
        copies.append(pltpu.make_async_copy(source.at[:, part], blocks.at[:, part], sems.at[n]))
        first += size
    for copy in copies:
        copy.start()
    first = 0
    for copy, size in zip(copies, sizes):
        copy.wait()
        for k in range(first, first + size):
            for s in range(scen):
                flipped[s, k] = blocks[s, k].T
        first += size


def hot_kernel(block_map, counts, row_hot, row_hot_t, col_hot, col_hot_t):
    row_blocks, slots = row_hot_t.shape
    usable = lax.broadcasted_iota(jnp.int32, (row_blocks, slots), 1) < counts[0]
    rows = lax.broadcasted_iota(jnp.int32, (row_blocks, slots), 0) == block_map[0:1, :]
    row = jnp.where(rows & usable, 1.0, 0.0).astype(F32)
    beam_blocks = col_hot_t.shape[0]
    cols = lax.broadcasted_iota(jnp.int32, (beam_blocks, slots), 0) == block_map[1:2, :]
    col = jnp.where(cols, 1.0, 0.0).astype(F32)
    row_hot_t[...] = row.astype(BF16)
    col_hot_t[...] = col.astype(BF16)
    row_hot[...] = flat(row).astype(BF16)
    col_hot[...] = flat(col).astype(BF16)


def first_kernel(flipped, fluence, target, col_hot, row_hot_t, excess, score_sum, rows):
    scen = flipped.shape[0]
    picked = exact(col_hot[...], fluence[...])
    products(flipped, [picked] * scen, rows)
    scores = []
    for s in range(scen):
        e = exact(row_hot_t[...], rows[s]) - target[...]
        excess[s] = e
        scores.append(SHARPNESS * e * e)
    top = functools.reduce(jnp.maximum, scores)
    total = functools.reduce(jnp.add, [jnp.exp(score - top) for score in scores])
    score_sum[...] = top + jnp.log(total)


def second_kernel(blocks, excess, sum_a, sum_b, row_hot, col_hot_t, weights, gradient, rows):
    scen = excess.shape[0]
    total = merge(sum_a[...], sum_b[...])
    picked = []
    for s in range(scen):
        e = excess[s]
        w = jnp.exp(SHARPNESS * e * e - total)
        weights[s] = w
        picked.append(exact(row_hot[...], 2.0 * w * e))
    products(blocks, picked, rows)
    for s in range(scen):
        gradient[s] = exact(col_hot_t[...], rows[s])


def third_kernel(
    blocks, flipped, fluence, grad_a, grad_b, weights, target,
    col_hot, col_hot_t, row_hot, row_hot_t, copies, gradient, rows
):
    scen = weights.shape[0]
    picked = []
    for s in range(scen):
        c = jnp.maximum(fluence[...] - STEP_SIZE * (grad_a[s] + grad_b[s]), 0.0)
        copies[s] = c
        picked.append(exact(col_hot[...], c))
    products(flipped, picked, rows)
    picked = []
    for s in range(scen):
        e = exact(row_hot_t[...], rows[s]) - target[...]
        picked.append(exact(row_hot[...], 2.0 * weights[s] * e))
    products(blocks, picked, rows)
    for s in range(scen):
        gradient[s] = exact(col_hot_t[...], rows[s])


def near(x):
    return pltpu.with_memory_space_constraint(x, pltpu.VMEM)


def swap(x, axis, bit):
    return lax.ppermute(x, axis, [(i, i ^ bit) for i in range(lax.axis_size(axis))])


def bits(axis):
    size = lax.axis_size(axis)
    if size & (size - 1) or size < 2:
        raise ValueError("axis size")
    return [1 << b for b in range(size.bit_length() - 1)]


def reduce_vox(x):
    steps = bits("vox")
    for bit in steps[:-1]:
        x = x + swap(x, "vox", bit)
    return x, swap(x, "vox", steps[-1])


def reduce_scen(x, combine):
    steps = bits("scen")
    x = [x, swap(x, "scen", steps[0])]
    for bit in steps[1:]:
        both = combine(*x)
        x = [both, swap(both, "scen", bit ^ 1)]
    return x


def swap_both(x, bit):
    scen, vox = lax.axis_size("scen"), lax.axis_size("vox")
    pairs = [(s * vox + v, (s ^ 1) * vox + (v ^ bit)) for s in range(scen) for v in range(vox)]
    return lax.ppermute(x, ("scen", "vox"), pairs)


def split(total, parts):
    return [total * (n + 1) // parts - total * n // parts for n in range(parts)]


def body(dose_blocks, block_map, block_counts, target, fluence_init):
    scen, slots, side, _ = dose_blocks.shape
    share = fluence_init.shape[0]
    parts = lax.axis_size("vox")
    beam_blocks = share * parts // side
    row_blocks = target.shape[0] // side
    scen_total = scen * lax.axis_size("scen")
    params = pltpu.CompilerParams(vmem_limit_bytes=16 * 2**20)
    passes = scen * slots * side * side
    dense = lambda *shape: jax.ShapeDtypeStruct(shape, F32)
    scratch = [pltpu.VMEM((scen, slots, side), F32)]

    target = target.reshape(row_blocks, side)
    row_hot, row_hot_t, col_hot, col_hot_t = pl.pallas_call(
        hot_kernel,
        name="hot",
        out_shape=(
            jax.ShapeDtypeStruct((slots, row_blocks), BF16),
            jax.ShapeDtypeStruct((row_blocks, slots), BF16),
            jax.ShapeDtypeStruct((slots, beam_blocks), BF16),
            jax.ShapeDtypeStruct((beam_blocks, slots), BF16),
        ),
        in_specs=[VMEM, pl.BlockSpec(memory_space=pltpu.SMEM)],
        out_specs=(VMEM,) * 4,
        compiler_params=params,
    )(block_map.T, block_counts)

    fluence = fluence_init.reshape(share // side, side)
    me = lax.axis_index("vox")
    for bit in bits("vox"):
        other = swap_both(fluence, bit)
        fluence = jnp.where(
            me & bit == 0,
            jnp.concatenate([fluence, other], axis=0),
            jnp.concatenate([other, fluence], axis=0),
        )

    sizes = split(slots, 10)
    whole = pltpu.VMEM((scen, slots, side, side), F32)
    blocks, flipped = pl.pallas_call(
        functools.partial(load_kernel, sizes),
        name="load",
        out_shape=(whole, whole),
        in_specs=[pl.BlockSpec(memory_space=pltpu.HBM)],
        out_specs=(VMEM,) * 2,
        scratch_shapes=[pltpu.SemaphoreType.DMA((len(sizes),))],
        compiler_params=params,
        cost_estimate=pl.CostEstimate(flops=0, bytes_accessed=8 * passes, transcendentals=0),
    )(pltpu.with_memory_space_constraint(dose_blocks, pltpu.HBM))
    blocks, flipped = near(blocks), near(flipped)

    for outer_round in range(ROUNDS):
        excess, score_sum = pl.pallas_call(
            first_kernel,
            name="first",
            out_shape=(dense(scen, row_blocks, side), dense(row_blocks, side)),
            in_specs=[VMEM] * 5,
            out_specs=(VMEM,) * 2,
            scratch_shapes=scratch,
            compiler_params=params,
        )(flipped, fluence, target, col_hot, row_hot_t)
        sum_a, sum_b = reduce_scen(score_sum, merge)
        weights, gradient = pl.pallas_call(
            second_kernel,
            name="second",
            out_shape=(dense(scen, row_blocks, side), dense(scen, beam_blocks, side)),
            in_specs=[VMEM] * 6,
            out_specs=(VMEM,) * 2,
            scratch_shapes=scratch,
            compiler_params=params,
        )(blocks, excess, sum_a, sum_b, row_hot, col_hot_t)
        grad_a, grad_b = reduce_vox(gradient)
        copies, gradient = pl.pallas_call(
            third_kernel,
            name="third",
            out_shape=(dense(scen, beam_blocks, side), dense(scen, beam_blocks, side)),
            in_specs=[VMEM] * 11,
            out_specs=(VMEM,) * 2,
            scratch_shapes=scratch,
            compiler_params=params,
        )(
            blocks, flipped, fluence, grad_a, grad_b, weights, target,
            col_hot, col_hot_t, row_hot, row_hot_t,
        )
        if outer_round < ROUNDS - 1:
            grad_a, grad_b = reduce_vox(gradient)
        else:
            pieces = gradient.reshape(scen, parts, share // side, side)
            pieces = lax.all_to_all(pieces, "vox", split_axis=1, concat_axis=1, tiled=True)
            grad_a, grad_b = jnp.sum(pieces, axis=1), 0.0
            start = lax.axis_index("vox") * (share // side)
            copies = lax.dynamic_slice_in_dim(copies, start, share // side, 1)
        copies = jnp.maximum(copies - STEP_SIZE * (grad_a + grad_b), 0.0)
        mean_a, mean_b = reduce_scen(jnp.sum(copies, axis=0), jnp.add)
        fluence = (mean_a + mean_b) / scen_total
    return fluence.reshape(share), weights.reshape(scen, row_blocks * side)


def solution(mesh):
    placed = (P("scen", "vox", None, None), P("vox", None), P("vox"), P("vox"), P("vox"))
    return jax.shard_map(
        body, mesh=mesh, in_specs=placed, out_specs=(P("vox"), P("scen", "vox")), check_vma=False
    )
```

```python
import functools

import jax
import jax.numpy as jnp
from jax import lax
from jax.experimental import pallas as pl
from jax.experimental.pallas import tpu as pltpu
from jax.sharding import PartitionSpec as P

ROUNDS = 2
SHARPNESS = 2.0
STEP_SIZE = 0.5
F32 = jnp.float32
BF16 = jnp.bfloat16
VMEM = pl.BlockSpec(memory_space=pltpu.VMEM)
FAR = pl.BlockSpec(memory_space=pltpu.HBM)


def split3(x):
    return jnp.concatenate(pieces(x), axis=-1)


def exact(hot, x):
    n = x.shape[1]
    y = jnp.dot(hot, split3(x), preferred_element_type=F32)
    return y[:, :n] + y[:, n : 2 * n] + y[:, 2 * n :]


def columns(x):
    pad = -x.shape[0] % 128
    if pad:
        x = jnp.concatenate([x, jnp.zeros((pad, x.shape[1]), x.dtype)], axis=0)
    return x.T


def flat(x):
    pad = -x.shape[1] % 128
    slots = x.shape[1]
    if pad:
        x = jnp.concatenate([x, jnp.zeros((x.shape[0], pad), x.dtype)], axis=1)
    return x.T[:slots]


def pieces(x):
    high = x.astype(BF16)
    rest = x - high.astype(F32)
    mid = rest.astype(BF16)
    return high, mid, (rest - mid.astype(F32)).astype(BF16)


def products(whole, upper, lower, picked, rows):
    scen, kept, side, _ = whole.shape
    split_slots = upper.shape[1]
    turned, parts = {}, {}
    for x in picked:
        if id(x) not in turned:
            turned[id(x)] = columns(x[:kept])
            parts[id(x)] = [y.astype(F32) for y in pieces(x)]
    depth = max(16, 8 * scen)
    sub = lax.broadcasted_iota(jnp.int32, (depth, side), 0)
    order = [(k + 0.5) / kept for k in range(kept)]
    order += [(m + 0.5) / split_slots for m in range(split_slots)]
    for k in sorted(range(kept + split_slots), key=lambda k: (order[k], k)):
        if k < kept:
            wide = {}
            for s in range(scen):
                key = id(picked[s])
                if key not in wide:
                    wide[key] = jnp.broadcast_to(turned[key][:, k : k + 1], (side, side))
                rows[s, k : k + 1, :] = jnp.sum(whole[s, k] * wide[key], axis=0, keepdims=True)
            continue
        m = k - kept
        firsts, stacks = [], {}
        for s in range(scen):
            key = id(picked[s])
            high, mid, low = [x[k : k + 1, :] for x in parts[key]]
            firsts.append(jnp.where(sub == 8 * s, high, 0.0).astype(BF16))
            if key not in stacks:
                stack = jnp.where(sub == 0, high, jnp.where(sub == 1, mid, jnp.where(sub == 2, low, 0.0)))
                stacks[key] = jnp.concatenate([stack.astype(BF16)] * 2, axis=1)
        rest = jnp.dot(jnp.concatenate(firsts, axis=1), lower[m], preferred_element_type=F32)
        for s in range(scen):
            main = jnp.dot(stacks[id(picked[s])], upper[s, m], preferred_element_type=F32)
            total = main[:8] + rest[8 * s : 8 * s + 8]
            rows[s, k : k + 1, :] = jnp.sum(total, axis=0, keepdims=True)


def merge(a, b):
    top = jnp.maximum(a, b)
    return top + jnp.log(jnp.exp(a - top) + jnp.exp(b - top))


def load_kernel(chunks, source, whole, whole_t, upper, upper_t, lower, lower_t, held, sems):
    scen, _, side, _ = source.shape
    kept = whole.shape[1]
    copies = []
    for n, (first, size) in enumerate(chunks):
        part = pl.ds(first, size)
        to = whole.at[:, part] if first < kept else held.at[:, pl.ds(first - kept, size)]
        copies.append(pltpu.make_async_copy(source.at[:, part], to, sems.at[n]))
    for copy in copies:
        copy.start()
    for copy, (first, size) in zip(copies, chunks):
        copy.wait()
        for k in range(first, first + size):
            for s in range(scen):
                if k < kept:
                    whole_t[s, k] = whole[s, k].T
                    continue
                m = k - kept
                block = held[s, m]
                for x, up, low in ((block, upper, lower), (block.T, upper_t, lower_t)):
                    high, mid, rest = pieces(x)
                    up[s, m, :side] = high
                    up[s, m, side:] = mid
                    low[m, s * side : (s + 1) * side] = rest


def hot_kernel(
    map_far, fluence, counts, row_hot, row_hot_t, col_hot, col_hot_t, mine, block_map, sems
):
    copies = [
        pltpu.make_async_copy(map_far, block_map, sems.at[0]),
        pltpu.make_async_copy(fluence, mine, sems.at[1]),
    ]
    for copy in copies:
        copy.start()
    for copy in copies:
        copy.wait()
    row_blocks, slots = row_hot_t.shape
    usable = lax.broadcasted_iota(jnp.int32, (row_blocks, slots), 1) < counts[...]
    rows = lax.broadcasted_iota(jnp.int32, (row_blocks, slots), 0) == block_map[0:1, :]
    row = jnp.where(rows & usable, 1.0, 0.0).astype(F32)
    beam_blocks = col_hot_t.shape[0]
    cols = lax.broadcasted_iota(jnp.int32, (beam_blocks, slots), 0) == block_map[1:2, :]
    col = jnp.where(cols, 1.0, 0.0).astype(F32)
    row_hot_t[...] = row.astype(BF16)
    col_hot_t[...] = col.astype(BF16)
    row_hot[...] = flat(row).astype(BF16)
    col_hot[...] = flat(col).astype(BF16)


def join_kernel(bit, mine, other, joined):
    size = mine.shape[0]
    low = lax.axis_index("vox") & bit == 0
    joined[:size] = jnp.where(low, mine[...], other[...])
    joined[size:] = jnp.where(low, other[...], mine[...])


def first_kernel(
    whole, upper, lower, fluence, target, col_hot, row_hot_t, excess, score_sum, rows
):
    scen = whole.shape[0]
    picked = exact(col_hot[...], fluence[...])
    products(whole, upper, lower, [picked] * scen, rows)
    scores = []
    for s in range(scen):
        e = exact(row_hot_t[...], rows[s]) - target[...]
        excess[s] = e
        scores.append(SHARPNESS * e * e)
    top = functools.reduce(jnp.maximum, scores)
    total = functools.reduce(jnp.add, [jnp.exp(score - top) for score in scores])
    score_sum[...] = top + jnp.log(total)


def second_kernel(
    whole, upper, lower, excess, sum_a, sum_b, row_hot, col_hot_t, weights, gradient, rows
):
    scen = excess.shape[0]
    total = merge(sum_a[...], sum_b[...])
    picked = []
    for s in range(scen):
        e = excess[s]
        w = jnp.exp(SHARPNESS * e * e - total)
        weights[s] = w
        picked.append(exact(row_hot[...], 2.0 * w * e))
    products(whole, upper, lower, picked, rows)
    for s in range(scen):
        gradient[s] = exact(col_hot_t[...], rows[s])


def third_kernel(
    whole, upper, lower, whole_t, upper_t, lower_t, fluence, grad_a, grad_b, weights, target,
    col_hot, col_hot_t, row_hot, row_hot_t, copies, gradient, rows
):
    scen = weights.shape[0]
    picked = []
    for s in range(scen):
        c = jnp.maximum(fluence[...] - STEP_SIZE * (grad_a[s] + grad_b[s]), 0.0)
        copies[s] = c
        picked.append(exact(col_hot[...], c))
    products(whole_t, upper_t, lower_t, picked, rows)
    picked = []
    for s in range(scen):
        e = exact(row_hot_t[...], rows[s]) - target[...]
        picked.append(exact(row_hot[...], 2.0 * weights[s] * e))
    products(whole, upper, lower, picked, rows)
    for s in range(scen):
        g = exact(col_hot_t[...], rows[s])
        if len(gradient.shape) == 3:
            gradient[s] = g
        else:
            gradient[:, s] = g.reshape(gradient.shape[0], *gradient.shape[2:])


def near(x):
    return pltpu.with_memory_space_constraint(x, pltpu.VMEM)


def far(x):
    return pltpu.with_memory_space_constraint(x, pltpu.HBM)


def swap(x, axis, bit):
    return lax.ppermute(x, axis, [(i, i ^ bit) for i in range(lax.axis_size(axis))])


def bits(axis):
    size = lax.axis_size(axis)
    if size & (size - 1) or size < 2:
        raise ValueError("axis size")
    return [1 << b for b in range(size.bit_length() - 1)]


def reduce_vox(x):
    steps = bits("vox")
    orders = [steps, steps]
    if len(steps) > 2:
        first, far, *between = steps[0], steps[-1], *steps[1:-1]
        orders = [[far, first, *between], [first, far, *between]]
    other = None
    for pair in zip(*orders):
        if other is not None:
            x = x + other
        other = lax.ppermute(
            x,
            "vox",
            [(v, v ^ pair[(v & steps[-2]) // steps[-2]]) for v in range(lax.axis_size("vox"))],
        )
    return x, other


def reduce_scen(x, combine):
    steps = bits("scen")
    x = [x, swap(x, "scen", steps[0])]
    for bit in steps[1:]:
        both = combine(*x)
        x = [both, swap(both, "scen", bit ^ 1)]
    return x


def swap_both(x, bit):
    scen, vox = lax.axis_size("scen"), lax.axis_size("vox")
    pairs = [(s * vox + v, (s ^ 1) * vox + (v ^ bit)) for s in range(scen) for v in range(vox)]
    return lax.ppermute(x, ("scen", "vox"), pairs)


def split(total, parts):
    return [total * (n + 1) // parts - total * n // parts for n in range(parts)]


def body(dose_blocks, block_map, block_counts, target, fluence_init):
    scen, slots, side, _ = dose_blocks.shape
    share = fluence_init.shape[0]
    parts = lax.axis_size("vox")
    beam_blocks = share * parts // side
    row_blocks = target.shape[0] // side
    scen_total = scen * lax.axis_size("scen")
    params = pltpu.CompilerParams(vmem_limit_bytes=16 * 2**20)
    passes = scen * slots * side * side
    dense = lambda *shape: jax.ShapeDtypeStruct(shape, F32)
    scratch = [pltpu.VMEM((scen, slots, side), F32)]

    target = target.reshape(row_blocks, side)
    fluence = fluence_init.reshape(share // side, side)
    row_hot, row_hot_t, col_hot, col_hot_t, mine = pl.pallas_call(
        hot_kernel,
        name="hot",
        out_shape=(
            jax.ShapeDtypeStruct((slots, row_blocks), BF16),
            jax.ShapeDtypeStruct((row_blocks, slots), BF16),
            jax.ShapeDtypeStruct((slots, beam_blocks), BF16),
            jax.ShapeDtypeStruct((beam_blocks, slots), BF16),
            dense(*fluence.shape),
        ),
        in_specs=[FAR, FAR, VMEM],
        out_specs=(VMEM,) * 5,
        scratch_shapes=[pltpu.VMEM((2, slots), jnp.int32), pltpu.SemaphoreType.DMA((2,))],
        compiler_params=params,
    )(far(block_map.T), far(fluence), block_counts.reshape(1, 1))

    for bit in bits("vox"):
        other = swap_both(fluence, bit)
        if bit == 1:
            fluence = mine
        rows_here = fluence.shape[0]
        fluence = pl.pallas_call(
            functools.partial(join_kernel, bit),
            name="join",
            out_shape=dense(2 * rows_here, side),
            in_specs=[VMEM] * 2,
            out_specs=VMEM,
            compiler_params=params,
        )(fluence, other)

    kept = slots * 2 // 5
    rest = slots - kept
    chunks = [(n * kept // 4, kept) for n in range(4)] + [(kept + n * rest // 6, rest) for n in range(6)]
    ends = [first for first, _ in chunks[1:]] + [slots]
    chunks = [(first, end - first, of) for (first, of), end in zip(chunks, ends) if end > first]
    chunks.sort(key=lambda chunk: (chunk[0] % kept if chunk[0] < kept else chunk[0] - kept) / chunk[2])
    chunks = [(first, size) for first, size, _ in chunks]
    near_blocks = pl.pallas_call(
        functools.partial(load_kernel, chunks),
        name="load",
        out_shape=(pltpu.VMEM((scen, kept, side, side), F32),) * 2
        + (pltpu.VMEM((scen, rest, 2 * side, side), BF16),) * 2
        + (pltpu.VMEM((rest, scen * side, side), BF16),) * 2,
        in_specs=[FAR],
        out_specs=(VMEM,) * 6,
        scratch_shapes=[
            pltpu.VMEM((scen, rest, side, side), F32),
            pltpu.SemaphoreType.DMA((len(chunks),)),
        ],
        compiler_params=params,
        cost_estimate=pl.CostEstimate(flops=0, bytes_accessed=8 * passes, transcendentals=0),
    )(far(dose_blocks))
    blocks = [near(x) for x in near_blocks[0::2]]
    flipped = [near(x) for x in near_blocks[1::2]]

    for outer_round in range(ROUNDS):
        excess, score_sum = pl.pallas_call(
            first_kernel,
            name="first",
            out_shape=(dense(scen, row_blocks, side), dense(row_blocks, side)),
            in_specs=[VMEM] * 7,
            out_specs=(VMEM,) * 2,
            scratch_shapes=scratch,
            compiler_params=params,
        )(*flipped, fluence, target, col_hot, row_hot_t)
        sum_a, sum_b = reduce_scen(score_sum, merge)
        weights, gradient = pl.pallas_call(
            second_kernel,
            name="second",
            out_shape=(dense(scen, row_blocks, side), dense(scen, beam_blocks, side)),
            in_specs=[VMEM] * 8,
            out_specs=(VMEM,) * 2,
            scratch_shapes=scratch,
            compiler_params=params,
        )(*blocks, excess, sum_a, sum_b, row_hot, col_hot_t)
        grad_a, grad_b = reduce_vox(gradient)
        last = outer_round == ROUNDS - 1
        form = (parts, scen, share // side, side) if last else (scen, beam_blocks, side)
        copies, gradient = pl.pallas_call(
            third_kernel,
            name="third",
            out_shape=(dense(scen, beam_blocks, side), dense(*form)),
            in_specs=[VMEM] * 15,
            out_specs=(VMEM,) * 2,
            scratch_shapes=scratch,
            compiler_params=params,
        )(
            *blocks, *flipped, fluence, grad_a, grad_b, weights, target,
            col_hot, col_hot_t, row_hot, row_hot_t,
        )
        if not last:
            grad_a, grad_b = reduce_vox(gradient)
        else:
            gradient = lax.all_to_all(gradient, "vox", split_axis=0, concat_axis=0, tiled=True)
            grad_a, grad_b = jnp.sum(gradient, axis=0), 0.0
            start = lax.axis_index("vox") * (share // side)
            copies = lax.dynamic_slice_in_dim(copies, start, share // side, 1)
        copies = jnp.maximum(copies - STEP_SIZE * (grad_a + grad_b), 0.0)
        mean_a, mean_b = reduce_scen(jnp.sum(copies, axis=0), jnp.add)
        fluence = (mean_a + mean_b) / scen_total
    return fluence.reshape(share), weights.reshape(scen, row_blocks * side)


def solution(mesh):
    placed = (P("scen", "vox", None, None), P("vox", None), P("vox"), P("vox"), P("vox"))
    return jax.shard_map(
        body, mesh=mesh, in_specs=placed, out_specs=(P("vox"), P("scen", "vox")), check_vma=False
    )
```

```python
import functools

import jax
import jax.numpy as jnp
from jax import lax
from jax.experimental import pallas as pl
from jax.experimental.pallas import tpu as pltpu
from jax.sharding import PartitionSpec as P

ROUNDS = 2
SHARPNESS = 2.0
STEP_SIZE = 0.5
F32 = jnp.float32
BF16 = jnp.bfloat16
VMEM = pl.BlockSpec(memory_space=pltpu.VMEM)
FAR = pl.BlockSpec(memory_space=pltpu.HBM)


def split3(x):
    return jnp.concatenate(pieces(x), axis=-1)


def exact(hot, x):
    n = x.shape[1]
    y = jnp.dot(hot, split3(x), preferred_element_type=F32)
    return y[:, :n] + y[:, n : 2 * n] + y[:, 2 * n :]


def columns(x):
    pad = -x.shape[0] % 128
    if pad:
        x = jnp.concatenate([x, jnp.zeros((pad, x.shape[1]), x.dtype)], axis=0)
    return x.T


def flat(x):
    pad = -x.shape[1] % 128
    slots = x.shape[1]
    if pad:
        x = jnp.concatenate([x, jnp.zeros((x.shape[0], pad), x.dtype)], axis=1)
    return x.T[:slots]


def pieces(x):
    high = x.astype(BF16)
    rest = x - high.astype(F32)
    mid = rest.astype(BF16)
    return high, mid, (rest - mid.astype(F32)).astype(BF16)


def products(whole, upper, lower, picked, rows):
    scen, kept, side, _ = whole.shape
    split_slots = upper.shape[1]
    turned, parts = {}, {}
    for x in picked:
        if id(x) not in turned:
            turned[id(x)] = columns(x[:kept])
            parts[id(x)] = [y.astype(F32) for y in pieces(x)]
    depth = max(16, 8 * scen)
    sub = lax.broadcasted_iota(jnp.int32, (depth, side), 0)
    order = [(k + 0.5) / kept for k in range(kept)]
    order += [(m + 0.5) / split_slots for m in range(split_slots)]
    for k in sorted(range(kept + split_slots), key=lambda k: (order[k], k)):
        if k < kept:
            wide = {}
            for s in range(scen):
                key = id(picked[s])
                if key not in wide:
                    wide[key] = jnp.broadcast_to(turned[key][:, k : k + 1], (side, side))
                rows[s, k : k + 1, :] = jnp.sum(whole[s, k] * wide[key], axis=0, keepdims=True)
            continue
        m = k - kept
        firsts, stacks = [], {}
        for s in range(scen):
            key = id(picked[s])
            high, mid, low = [x[k : k + 1, :] for x in parts[key]]
            firsts.append(jnp.where(sub == 8 * s, high, 0.0).astype(BF16))
            if key not in stacks:
                stack = jnp.where(sub == 0, high, jnp.where(sub == 1, mid, jnp.where(sub == 2, low, 0.0)))
                stacks[key] = jnp.concatenate([stack.astype(BF16)] * 2, axis=1)
        rest = jnp.dot(jnp.concatenate(firsts, axis=1), lower[m], preferred_element_type=F32)
        for s in range(scen):
            main = jnp.dot(stacks[id(picked[s])], upper[s, m], preferred_element_type=F32)
            total = main[:8] + rest[8 * s : 8 * s + 8]
            rows[s, k : k + 1, :] = jnp.sum(total, axis=0, keepdims=True)


def merge(a, b):
    top = jnp.maximum(a, b)
    return top + jnp.log(jnp.exp(a - top) + jnp.exp(b - top))


def bring(source, first, sizes, to, sems):
    copies, done = [], 0
    for n, size in enumerate(sizes):
        copy = pltpu.make_async_copy(
            source.at[:, pl.ds(first + done, size)], to.at[:, pl.ds(done, size)], sems.at[n]
        )
        copy.start()
        copies.append((copy, range(done, done + size)))
        done += size
    for copy, slots in copies:
        copy.wait()
        yield slots


def whole_kernel(sizes, source, order, whole, whole_t, token, sems):
    del order
    token[...] = jnp.zeros_like(token)
    for slots in bring(source, 0, sizes, whole, sems):
        for k in slots:
            for s in range(source.shape[0]):
                whole_t[s, k] = whole[s, k].T


def split_kernel(sizes, source, order, upper, upper_t, lower, lower_t, held, sems):
    del order
    scen, slots, side, _ = source.shape
    for brought in bring(source, slots - held.shape[1], sizes, held, sems):
        for k in brought:
            for s in range(scen):
                block = held[s, k]
                for x, up, low in ((block, upper, lower), (block.T, upper_t, lower_t)):
                    high, mid, rest = pieces(x)
                    up[s, k, :side] = high
                    up[s, k, side:] = mid
                    low[k, s * side : (s + 1) * side] = rest


def hot_kernel(
    map_far, fluence, counts, row_hot, row_hot_t, col_hot, col_hot_t, mine, block_map, sems
):
    copies = [
        pltpu.make_async_copy(map_far, block_map, sems.at[0]),
        pltpu.make_async_copy(fluence, mine, sems.at[1]),
    ]
    for copy in copies:
        copy.start()
    for copy in copies:
        copy.wait()
    row_blocks, slots = row_hot_t.shape
    usable = lax.broadcasted_iota(jnp.int32, (row_blocks, slots), 1) < counts[...]
    rows = lax.broadcasted_iota(jnp.int32, (row_blocks, slots), 0) == block_map[0:1, :]
    row = jnp.where(rows & usable, 1.0, 0.0).astype(F32)
    beam_blocks = col_hot_t.shape[0]
    cols = lax.broadcasted_iota(jnp.int32, (beam_blocks, slots), 0) == block_map[1:2, :]
    col = jnp.where(cols, 1.0, 0.0).astype(F32)
    row_hot_t[...] = row.astype(BF16)
    col_hot_t[...] = col.astype(BF16)
    row_hot[...] = flat(row).astype(BF16)
    col_hot[...] = flat(col).astype(BF16)


def join_kernel(bit, mine, other, order, joined):
    del order
    size = mine.shape[0]
    low = lax.axis_index("vox") & bit == 0
    joined[:size] = jnp.where(low, mine[...], other[...])
    joined[size:] = jnp.where(low, other[...], mine[...])


def first_kernel(
    whole, upper, lower, fluence, target, col_hot, row_hot_t, excess, score_sum, rows
):
    scen = whole.shape[0]
    picked = exact(col_hot[...], fluence[...])
    products(whole, upper, lower, [picked] * scen, rows)
    scores = []
    for s in range(scen):
        e = exact(row_hot_t[...], rows[s]) - target[...]
        excess[s] = e
        scores.append(SHARPNESS * e * e)
    top = functools.reduce(jnp.maximum, scores)
    total = functools.reduce(jnp.add, [jnp.exp(score - top) for score in scores])
    score_sum[...] = top + jnp.log(total)


def second_kernel(
    whole, upper, lower, excess, sum_a, sum_b, row_hot, col_hot_t, weights, gradient, rows
):
    scen = excess.shape[0]
    total = merge(sum_a[...], sum_b[...])
    picked = []
    for s in range(scen):
        e = excess[s]
        w = jnp.exp(SHARPNESS * e * e - total)
        weights[s] = w
        picked.append(exact(row_hot[...], 2.0 * w * e))
    products(whole, upper, lower, picked, rows)
    for s in range(scen):
        gradient[s] = exact(col_hot_t[...], rows[s])


def third_kernel(
    whole, upper, lower, whole_t, upper_t, lower_t, fluence, grad_a, grad_b, weights, target,
    col_hot, col_hot_t, row_hot, row_hot_t, copies, gradient, rows, held
):
    scen = weights.shape[0]
    share = copies.shape[1]
    mine = pl.ds(0 if share == held.shape[1] else lax.axis_index("vox") * share, share)
    picked = []
    for s in range(scen):
        c = jnp.maximum(fluence[...] - STEP_SIZE * (grad_a[s] + grad_b[s]), 0.0)
        held[s] = c
        copies[s] = held[s, mine]
        picked.append(exact(col_hot[...], c))
    products(whole_t, upper_t, lower_t, picked, rows)
    picked = []
    for s in range(scen):
        e = exact(row_hot_t[...], rows[s]) - target[...]
        picked.append(exact(row_hot[...], 2.0 * weights[s] * e))
    products(whole, upper, lower, picked, rows)
    for s in range(scen):
        g = exact(col_hot_t[...], rows[s])
        if len(gradient.shape) == 3:
            gradient[s] = g
        else:
            gradient[:, s] = g.reshape(gradient.shape[0], *gradient.shape[2:])


def place_kernel(weights, placed):
    for s in range(weights.shape[0]):
        placed[:, s] = weights[s]


def near(x):
    return pltpu.with_memory_space_constraint(x, pltpu.VMEM)


def far(x):
    return pltpu.with_memory_space_constraint(x, pltpu.HBM)


def swap(x, axis, bit):
    return lax.ppermute(x, axis, [(i, i ^ bit) for i in range(lax.axis_size(axis))])


def bits(axis):
    size = lax.axis_size(axis)
    if size & (size - 1) or size < 2:
        raise ValueError("axis size")
    return [1 << b for b in range(size.bit_length() - 1)]


def reduce_vox(x):
    steps = bits("vox")
    orders = [steps, steps]
    if len(steps) > 2:
        first, far, *between = steps[0], steps[-1], *steps[1:-1]
        orders = [[far, first, *between], [first, far, *between]]
    other = None
    for pair in zip(*orders):
        if other is not None:
            x = x + other
        other = lax.ppermute(
            x,
            "vox",
            [(v, v ^ pair[(v & steps[-2]) // steps[-2]]) for v in range(lax.axis_size("vox"))],
        )
    return x, other


def reduce_scen(x, combine):
    steps = bits("scen")
    x = [x, swap(x, "scen", steps[0])]
    for bit in steps[1:]:
        both = combine(*x)
        x = [both, swap(both, "scen", bit ^ 1)]
    return x


def swap_both(x, bit):
    scen, vox = lax.axis_size("scen"), lax.axis_size("vox")
    pairs = [(s * vox + v, (s ^ 1) * vox + (v ^ bit)) for s in range(scen) for v in range(vox)]
    return lax.ppermute(x, ("scen", "vox"), pairs)


def split(total, parts):
    return [total * (n + 1) // parts - total * n // parts for n in range(parts)]


def body(dose_blocks, block_map, block_counts, target, fluence_init):
    scen, slots, side, _ = dose_blocks.shape
    share = fluence_init.shape[0]
    parts = lax.axis_size("vox")
    beam_blocks = share * parts // side
    row_blocks = target.shape[0] // side
    scen_total = scen * lax.axis_size("scen")
    params = pltpu.CompilerParams(vmem_limit_bytes=16 * 2**20)
    passes = scen * slots * side * side
    dense = lambda *shape: jax.ShapeDtypeStruct(shape, F32)
    scratch = [pltpu.VMEM((scen, slots, side), F32)]

    target = target.reshape(row_blocks, side)
    fluence = fluence_init.reshape(share // side, side)
    row_hot, row_hot_t, col_hot, col_hot_t, mine = pl.pallas_call(
        hot_kernel,
        name="hot",
        out_shape=(
            jax.ShapeDtypeStruct((slots, row_blocks), BF16),
            jax.ShapeDtypeStruct((row_blocks, slots), BF16),
            jax.ShapeDtypeStruct((slots, beam_blocks), BF16),
            jax.ShapeDtypeStruct((beam_blocks, slots), BF16),
            dense(*fluence.shape),
        ),
        in_specs=[FAR, FAR, VMEM],
        out_specs=(VMEM,) * 5,
        scratch_shapes=[pltpu.VMEM((2, slots), jnp.int32), pltpu.SemaphoreType.DMA((2,))],
        compiler_params=params,
    )(far(block_map.T), far(fluence), block_counts.reshape(1, 1))

    kept = slots * 2 // 5
    rest = slots - kept
    steps = bits("vox")
    for n, bit in enumerate(steps):
        other = swap_both(fluence, bit)
        if n == 0:
            fluence = mine
        token = fluence
        if n == max(len(steps) - 2, 0):
            sizes = split(kept, 4)
            whole, whole_t, token = pl.pallas_call(
                functools.partial(whole_kernel, sizes),
                name="whole",
                out_shape=(pltpu.VMEM((scen, kept, side, side), F32),) * 2 + (dense(8, 128),),
                in_specs=[FAR, VMEM],
                out_specs=(VMEM,) * 3,
                scratch_shapes=[pltpu.SemaphoreType.DMA((len(sizes),))],
                compiler_params=params,
                cost_estimate=pl.CostEstimate(
                    flops=0, bytes_accessed=3 * passes, transcendentals=0
                ),
            )(far(dose_blocks), token)
        if n == len(steps) - 1:
            sizes = split(rest, 6)
            upper, upper_t, lower, lower_t = pl.pallas_call(
                functools.partial(split_kernel, sizes),
                name="split",
                out_shape=(pltpu.VMEM((scen, rest, 2 * side, side), BF16),) * 2
                + (pltpu.VMEM((rest, scen * side, side), BF16),) * 2,
                in_specs=[FAR, VMEM],
                out_specs=(VMEM,) * 4,
                scratch_shapes=[
                    pltpu.VMEM((scen, rest, side, side), F32),
                    pltpu.SemaphoreType.DMA((len(sizes),)),
                ],
                compiler_params=params,
                cost_estimate=pl.CostEstimate(
                    flops=0, bytes_accessed=5 * passes, transcendentals=0
                ),
            )(far(dose_blocks), fluence)
        fluence = pl.pallas_call(
            functools.partial(join_kernel, bit),
            name="join",
            out_shape=dense(2 * fluence.shape[0], side),
            in_specs=[VMEM] * 3,
            out_specs=VMEM,
            compiler_params=params,
        )(fluence, other, token)
    blocks = [near(x) for x in (whole, upper, lower)]
    flipped = [near(x) for x in (whole_t, upper_t, lower_t)]

    for outer_round in range(ROUNDS):
        excess, score_sum = pl.pallas_call(
            first_kernel,
            name="first",
            out_shape=(dense(scen, row_blocks, side), dense(row_blocks, side)),
            in_specs=[VMEM] * 7,
            out_specs=(VMEM,) * 2,
            scratch_shapes=scratch,
            compiler_params=params,
        )(*flipped, fluence, target, col_hot, row_hot_t)
        sum_a, sum_b = reduce_scen(score_sum, merge)
        last = outer_round == ROUNDS - 1
        weights, gradient = pl.pallas_call(
            second_kernel,
            name="second",
            out_shape=(dense(scen, row_blocks, side), dense(scen, beam_blocks, side)),
            in_specs=[VMEM] * 8,
            out_specs=(VMEM,) * 2,
            scratch_shapes=scratch,
            compiler_params=params,
        )(*blocks, excess, sum_a, sum_b, row_hot, col_hot_t)
        grad_a, grad_b = reduce_vox(gradient)
        form = (parts, scen, share // side, side) if last else (scen, beam_blocks, side)
        copies, gradient = pl.pallas_call(
            third_kernel,
            name="third",
            out_shape=(dense(scen, share // side if last else beam_blocks, side), dense(*form)),
            in_specs=[VMEM] * 15,
            out_specs=(VMEM,) * 2,
            scratch_shapes=scratch + [pltpu.VMEM((scen, beam_blocks, side), F32)],
            compiler_params=params,
        )(
            *blocks, *flipped, fluence, grad_a, grad_b, weights, target,
            col_hot, col_hot_t, row_hot, row_hot_t,
        )
        if not last:
            grad_a, grad_b = reduce_vox(gradient)
        else:
            weights = pl.pallas_call(
                place_kernel,
                name="place",
                out_shape=dense(row_blocks, scen, side),
                in_specs=[VMEM],
                out_specs=VMEM,
                compiler_params=params,
                cost_estimate=pl.CostEstimate(
                    flops=0, bytes_accessed=8 * weights.size, transcendentals=0
                ),
            )(near(weights))
            weights = jnp.swapaxes(weights, 0, 1).reshape(scen, row_blocks * side)
            gradient, copies, weights = lax.optimization_barrier((gradient, copies, weights))
            gradient = lax.all_to_all(gradient, "vox", split_axis=0, concat_axis=0, tiled=True)
            grad_a, grad_b = jnp.sum(gradient, axis=0), 0.0
        copies = jnp.maximum(copies - STEP_SIZE * (grad_a + grad_b), 0.0)
        mean_a, mean_b = reduce_scen(jnp.sum(copies, axis=0), jnp.add)
        fluence = (mean_a + mean_b) / scen_total
    return fluence.reshape(share), weights


def solution(mesh):
    placed = (P("scen", "vox", None, None), P("vox", None), P("vox"), P("vox"), P("vox"))
    return jax.shard_map(
        body, mesh=mesh, in_specs=placed, out_specs=(P("vox"), P("scen", "vox")), check_vma=False
    )
```

```python
import functools

import jax
import jax.numpy as jnp
from jax import lax
from jax.experimental import pallas as pl
from jax.experimental.pallas import tpu as pltpu
from jax.sharding import PartitionSpec as P

ROUNDS = 2
SHARPNESS = 2.0
STEP_SIZE = 0.5
F32 = jnp.float32
BF16 = jnp.bfloat16
VMEM = pl.BlockSpec(memory_space=pltpu.VMEM)
FAR = pl.BlockSpec(memory_space=pltpu.HBM)


def exact(hot, xs):
    n = xs[0].shape[1]
    every = jnp.concatenate([y for x in xs for y in pieces(x)], axis=1)
    y = jnp.dot(hot, every, preferred_element_type=F32)
    parts = [y[:, m * n : (m + 1) * n] for m in range(3 * len(xs))]
    return [parts[m] + parts[m + 1] + parts[m + 2] for m in range(0, len(parts), 3)]


def columns(x):
    pad = -x.shape[0] % 128
    if pad:
        x = jnp.concatenate([x, jnp.zeros((pad, x.shape[1]), x.dtype)], axis=0)
    return x.T


def flat(x):
    pad = -x.shape[1] % 128
    slots = x.shape[1]
    if pad:
        x = jnp.concatenate([x, jnp.zeros((x.shape[0], pad), x.dtype)], axis=1)
    return x.T[:slots]


def pieces(x):
    high = x.astype(BF16)
    rest = x - high.astype(F32)
    mid = rest.astype(BF16)
    return high, mid, (rest - mid.astype(F32)).astype(BF16)


def products(whole, upper, lower, picked, rows):
    scen, kept, side, _ = whole.shape
    split_slots = upper.shape[1]
    turned, parts = {}, {}
    for x in picked:
        if id(x) not in turned:
            turned[id(x)] = columns(x[:kept])
            parts[id(x)] = [y.astype(F32) for y in pieces(x)]
    depth = max(16, 8 * scen)
    sub = lax.broadcasted_iota(jnp.int32, (depth, side), 0)
    order = [(k + 0.5) / kept for k in range(kept)]
    order += [(m + 0.5) / split_slots for m in range(split_slots)]
    for k in sorted(range(kept + split_slots), key=lambda k: (order[k], k)):
        if k < kept:
            wide = {}
            for s in range(scen):
                key = id(picked[s])
                if key not in wide:
                    wide[key] = jnp.broadcast_to(turned[key][:, k : k + 1], (side, side))
                rows[s, k : k + 1, :] = jnp.sum(whole[s, k] * wide[key], axis=0, keepdims=True)
            continue
        m = k - kept
        firsts, stacks = [], {}
        for s in range(scen):
            key = id(picked[s])
            high, mid, low = [x[k : k + 1, :] for x in parts[key]]
            firsts.append(jnp.where(sub == 8 * s, high, 0.0).astype(BF16))
            if key not in stacks:
                stack = jnp.where(sub == 0, high, jnp.where(sub == 1, mid, jnp.where(sub == 2, low, 0.0)))
                stacks[key] = jnp.concatenate([stack.astype(BF16)] * 2, axis=1)
        rest = jnp.dot(jnp.concatenate(firsts, axis=1), lower[m], preferred_element_type=F32)
        for s in range(scen):
            main = jnp.dot(stacks[id(picked[s])], upper[s, m], preferred_element_type=F32)
            total = main[:8] + rest[8 * s : 8 * s + 8]
            rows[s, k : k + 1, :] = jnp.sum(total, axis=0, keepdims=True)


def merge(a, b):
    top = jnp.maximum(a, b)
    return top + jnp.log(jnp.exp(a - top) + jnp.exp(b - top))


def bring(source, first, sizes, to, sems):
    copies, done = [], 0
    for n, size in enumerate(sizes):
        copy = pltpu.make_async_copy(
            source.at[:, pl.ds(first + done, size)], to.at[:, pl.ds(done, size)], sems.at[n]
        )
        copy.start()
        copies.append((copy, range(done, done + size)))
        done += size
    for copy, slots in copies:
        copy.wait()
        yield slots


def whole_kernel(sizes, source, order, whole, whole_t, token, sems):
    del order
    token[...] = jnp.zeros_like(token)
    for slots in bring(source, 0, sizes, whole, sems):
        for k in slots:
            for s in range(source.shape[0]):
                whole_t[s, k] = whole[s, k].T


def split_kernel(sizes, source, order, upper, upper_t, lower, lower_t, held, sems):
    del order
    scen, slots, side, _ = source.shape
    for brought in bring(source, slots - held.shape[1], sizes, held, sems):
        for k in brought:
            for s in range(scen):
                block = held[s, k]
                for x, up, low in ((block, upper, lower), (block.T, upper_t, lower_t)):
                    high, mid, rest = pieces(x)
                    up[s, k, :side] = high
                    up[s, k, side:] = mid
                    low[k, s * side : (s + 1) * side] = rest


def hot_kernel(
    map_far, fluence, target_far, counts,
    col_hot, col_hot_t, same, leads, target, mine, block_map, target_rows, sems
):
    copies = [
        pltpu.make_async_copy(x, y, sems.at[n])
        for n, (x, y) in enumerate(
            [(map_far, block_map), (fluence, mine), (target_far, target_rows)]
        )
    ]
    for copy in copies:
        copy.start()
    for copy in copies:
        copy.wait()
    row_blocks, slots = leads.shape
    usable = lax.broadcasted_iota(jnp.int32, (row_blocks, slots), 1) < counts[...]
    rows = lax.broadcasted_iota(jnp.int32, (row_blocks, slots), 0) == block_map[0:1, :]
    row = jnp.where(rows & usable, 1.0, 0.0).astype(F32)
    beam_blocks = col_hot_t.shape[0]
    cols = lax.broadcasted_iota(jnp.int32, (beam_blocks, slots), 0) == block_map[1:2, :]
    col = jnp.where(cols, 1.0, 0.0).astype(F32)
    col_hot_t[...] = col.astype(BF16)
    col_hot[...] = flat(col).astype(BF16)
    row_hot = flat(row).astype(BF16)
    shared = jnp.dot(row_hot, row.astype(BF16), preferred_element_type=F32)
    same[...] = shared.astype(BF16)
    before = lax.broadcasted_iota(jnp.int32, (slots, slots), 0) < lax.broadcasted_iota(
        jnp.int32, (slots, slots), 1
    )
    earlier = jnp.sum(jnp.where(before, shared, 0.0), axis=0, keepdims=True)
    leads[...] = jnp.where(earlier == 0.0, row, 0.0).astype(BF16)
    target[...] = exact(row_hot, [target_rows[...]])[0]


def join_kernel(bit, mine, other, order, joined):
    del order
    size = mine.shape[0]
    low = lax.axis_index("vox") & bit == 0
    joined[:size] = jnp.where(low, mine[...], other[...])
    joined[size:] = jnp.where(low, other[...], mine[...])


def first_kernel(whole, upper, lower, fluence, target, col_hot, same, excess, score_sum, rows):
    scen = whole.shape[0]
    picked = exact(col_hot[...], [fluence[...]])
    products(whole, upper, lower, picked * scen, rows)
    scores = []
    for s, dose in enumerate(exact(same[...], [rows[s] for s in range(scen)])):
        e = dose - target[...]
        excess[s] = e
        scores.append(SHARPNESS * e * e)
    top = functools.reduce(jnp.maximum, scores)
    total = functools.reduce(jnp.add, [jnp.exp(score - top) for score in scores])
    score_sum[...] = top + jnp.log(total)


def second_kernel(whole, upper, lower, excess, sum_a, sum_b, col_hot_t, weights, gradient, rows):
    scen = excess.shape[0]
    total = merge(sum_a[...], sum_b[...])
    picked = []
    for s in range(scen):
        e = excess[s]
        w = jnp.exp(SHARPNESS * e * e - total)
        weights[s] = w
        picked.append(2.0 * w * e)
    products(whole, upper, lower, picked, rows)
    put_gradient(col_hot_t, rows, gradient)


def third_kernel(
    whole, upper, lower, whole_t, upper_t, lower_t, fluence, grad_a, grad_b, weights, target,
    col_hot, col_hot_t, same, copies, gradient, rows, held
):
    scen = weights.shape[0]
    share = copies.shape[1]
    mine = pl.ds(0 if share == held.shape[1] else lax.axis_index("vox") * share, share)
    for s in range(scen):
        held[s] = jnp.maximum(fluence[...] - STEP_SIZE * (grad_a[s] + grad_b[s]), 0.0)
        copies[s] = held[s, mine]
    picked = exact(col_hot[...], [held[s] for s in range(scen)])
    products(whole_t, upper_t, lower_t, picked, rows)
    doses = exact(same[...], [rows[s] for s in range(scen)])
    picked = [2.0 * weights[s] * (doses[s] - target[...]) for s in range(scen)]
    products(whole, upper, lower, picked, rows)
    put_gradient(col_hot_t, rows, gradient)


def put_gradient(col_hot_t, rows, gradient):
    for s, g in enumerate(exact(col_hot_t[...], [rows[s] for s in range(rows.shape[0])])):
        if len(gradient.shape) == 3:
            gradient[s] = g
        else:
            gradient[:, s] = g.reshape(gradient.shape[0], *gradient.shape[2:])


def place_kernel(scen_total, weights, leads, placed):
    used = jnp.sum(leads[...].astype(F32), axis=1, keepdims=True)
    scen = weights.shape[0]
    for s, w in enumerate(exact(leads[...], [weights[s] for s in range(scen)])):
        placed[:, s] = jnp.where(used == 0.0, 1.0 / scen_total, w)


def near(x):
    return pltpu.with_memory_space_constraint(x, pltpu.VMEM)


def far(x):
    return pltpu.with_memory_space_constraint(x, pltpu.HBM)


def swap(x, axis, bit):
    return lax.ppermute(x, axis, [(i, i ^ bit) for i in range(lax.axis_size(axis))])


def bits(axis):
    size = lax.axis_size(axis)
    if size & (size - 1) or size < 2:
        raise ValueError("axis size")
    return [1 << b for b in range(size.bit_length() - 1)]


def reduce_vox(x):
    steps = bits("vox")
    orders = [steps, steps]
    if len(steps) > 2:
        first, far, *between = steps[0], steps[-1], *steps[1:-1]
        orders = [[far, first, *between], [first, far, *between]]
    other = None
    for pair in zip(*orders):
        if other is not None:
            x = x + other
        other = lax.ppermute(
            x,
            "vox",
            [(v, v ^ pair[(v & steps[-2]) // steps[-2]]) for v in range(lax.axis_size("vox"))],
        )
    return x, other


def reduce_scen(x, combine):
    steps = bits("scen")
    x = [x, swap(x, "scen", steps[0])]
    for bit in steps[1:]:
        both = combine(*x)
        x = [both, swap(both, "scen", bit ^ 1)]
    return x


def swap_both(x, bit):
    scen, vox = lax.axis_size("scen"), lax.axis_size("vox")
    pairs = [(s * vox + v, (s ^ 1) * vox + (v ^ bit)) for s in range(scen) for v in range(vox)]
    return lax.ppermute(x, ("scen", "vox"), pairs)


def split(total, parts):
    return [total * (n + 1) // parts - total * n // parts for n in range(parts)]


def body(dose_blocks, block_map, block_counts, target, fluence_init):
    scen, slots, side, _ = dose_blocks.shape
    share = fluence_init.shape[0]
    parts = lax.axis_size("vox")
    beam_blocks = share * parts // side
    row_blocks = target.shape[0] // side
    scen_total = scen * lax.axis_size("scen")
    params = pltpu.CompilerParams(vmem_limit_bytes=16 * 2**20)
    passes = scen * slots * side * side
    dense = lambda *shape: jax.ShapeDtypeStruct(shape, F32)
    scratch = [pltpu.VMEM((scen, slots, side), F32)]

    fluence = fluence_init.reshape(share // side, side)
    half = lambda *shape: jax.ShapeDtypeStruct(shape, BF16)
    col_hot, col_hot_t, same, leads, target, mine = pl.pallas_call(
        hot_kernel,
        name="hot",
        out_shape=(
            half(slots, beam_blocks),
            half(beam_blocks, slots),
            half(slots, slots),
            half(row_blocks, slots),
            dense(slots, side),
            dense(*fluence.shape),
        ),
        in_specs=[FAR] * 3 + [VMEM],
        out_specs=(VMEM,) * 6,
        scratch_shapes=[
            pltpu.VMEM((2, slots), jnp.int32),
            pltpu.VMEM((row_blocks, side), F32),
            pltpu.SemaphoreType.DMA((3,)),
        ],
        compiler_params=params,
    )(
        far(block_map.T),
        far(fluence),
        far(target.reshape(row_blocks, side)),
        block_counts.reshape(1, 1),
    )

    kept = slots * 2 // 5
    rest = slots - kept
    steps = bits("vox")
    for n, bit in enumerate(steps):
        other = swap_both(fluence, bit)
        if n == 0:
            fluence = mine
        token = fluence
        if n == max(len(steps) - 2, 0):
            sizes = split(kept, 4)
            whole, whole_t, token = pl.pallas_call(
                functools.partial(whole_kernel, sizes),
                name="whole",
                out_shape=(pltpu.VMEM((scen, kept, side, side), F32),) * 2 + (dense(8, 128),),
                in_specs=[FAR, VMEM],
                out_specs=(VMEM,) * 3,
                scratch_shapes=[pltpu.SemaphoreType.DMA((len(sizes),))],
                compiler_params=params,
                cost_estimate=pl.CostEstimate(
                    flops=0, bytes_accessed=3 * passes, transcendentals=0
                ),
            )(far(dose_blocks), token)
        if n == len(steps) - 1:
            sizes = split(rest, 6)
            upper, upper_t, lower, lower_t = pl.pallas_call(
                functools.partial(split_kernel, sizes),
                name="split",
                out_shape=(pltpu.VMEM((scen, rest, 2 * side, side), BF16),) * 2
                + (pltpu.VMEM((rest, scen * side, side), BF16),) * 2,
                in_specs=[FAR, VMEM],
                out_specs=(VMEM,) * 4,
                scratch_shapes=[
                    pltpu.VMEM((scen, rest, side, side), F32),
                    pltpu.SemaphoreType.DMA((len(sizes),)),
                ],
                compiler_params=params,
                cost_estimate=pl.CostEstimate(
                    flops=0, bytes_accessed=5 * passes, transcendentals=0
                ),
            )(far(dose_blocks), fluence)
        fluence = pl.pallas_call(
            functools.partial(join_kernel, bit),
            name="join",
            out_shape=dense(2 * fluence.shape[0], side),
            in_specs=[VMEM] * 3,
            out_specs=VMEM,
            compiler_params=params,
        )(fluence, other, token)
    blocks = [near(x) for x in (whole, upper, lower)]
    flipped = [near(x) for x in (whole_t, upper_t, lower_t)]

    for outer_round in range(ROUNDS):
        excess, score_sum = pl.pallas_call(
            first_kernel,
            name="first",
            out_shape=(dense(scen, slots, side), dense(slots, side)),
            in_specs=[VMEM] * 7,
            out_specs=(VMEM,) * 2,
            scratch_shapes=scratch,
            compiler_params=params,
        )(*flipped, fluence, target, col_hot, same)
        sum_a, sum_b = reduce_scen(score_sum, merge)
        last = outer_round == ROUNDS - 1
        weights, gradient = pl.pallas_call(
            second_kernel,
            name="second",
            out_shape=(dense(scen, slots, side), dense(scen, beam_blocks, side)),
            in_specs=[VMEM] * 7,
            out_specs=(VMEM,) * 2,
            scratch_shapes=scratch,
            compiler_params=params,
        )(*blocks, excess, sum_a, sum_b, col_hot_t)
        grad_a, grad_b = reduce_vox(gradient)
        form = (parts, scen, share // side, side) if last else (scen, beam_blocks, side)
        copies, gradient = pl.pallas_call(
            third_kernel,
            name="third",
            out_shape=(dense(scen, share // side if last else beam_blocks, side), dense(*form)),
            in_specs=[VMEM] * 14,
            out_specs=(VMEM,) * 2,
            scratch_shapes=scratch + [pltpu.VMEM((scen, beam_blocks, side), F32)],
            compiler_params=params,
        )(
            *blocks, *flipped, fluence, grad_a, grad_b, weights, target,
            col_hot, col_hot_t, same,
        )
        if not last:
            grad_a, grad_b = reduce_vox(gradient)
        else:
            weights = pl.pallas_call(
                functools.partial(place_kernel, scen_total),
                name="place",
                out_shape=dense(row_blocks, scen, side),
                in_specs=[VMEM] * 2,
                out_specs=VMEM,
                compiler_params=params,
                cost_estimate=pl.CostEstimate(
                    flops=0, bytes_accessed=8 * weights.size, transcendentals=0
                ),
            )(near(weights), leads)
            weights = jnp.swapaxes(weights, 0, 1).reshape(scen, row_blocks * side)
            gradient, copies, weights = lax.optimization_barrier((gradient, copies, weights))
            gradient = lax.all_to_all(gradient, "vox", split_axis=0, concat_axis=0, tiled=True)
            grad_a, grad_b = jnp.sum(gradient, axis=0), 0.0
        copies = jnp.maximum(copies - STEP_SIZE * (grad_a + grad_b), 0.0)
        mean_a, mean_b = reduce_scen(jnp.sum(copies, axis=0), jnp.add)
        fluence = (mean_a + mean_b) / scen_total
    return fluence.reshape(share), weights


def solution(mesh):
    placed = (P("scen", "vox", None, None), P("vox", None), P("vox"), P("vox"), P("vox"))
    return jax.shard_map(
        body, mesh=mesh, in_specs=placed, out_specs=(P("vox"), P("scen", "vox")), check_vma=False
    )
```

```python
import functools

import jax
import jax.numpy as jnp
from jax import lax
from jax.experimental import pallas as pl
from jax.experimental.pallas import tpu as pltpu
from jax.sharding import PartitionSpec as P

ROUNDS = 2
SHARPNESS = 2.0
STEP_SIZE = 0.5
F32 = jnp.float32
BF16 = jnp.bfloat16
VMEM = pl.BlockSpec(memory_space=pltpu.VMEM)
FAR = pl.BlockSpec(memory_space=pltpu.HBM)


def exact(hot, xs):
    n = xs[0].shape[1]
    every = jnp.concatenate([y for x in xs for y in pieces(x)], axis=1)
    y = jnp.dot(hot, every, preferred_element_type=F32)
    parts = [y[:, m * n : (m + 1) * n] for m in range(3 * len(xs))]
    return [parts[m] + parts[m + 1] + parts[m + 2] for m in range(0, len(parts), 3)]


def columns(x):
    pad = -x.shape[0] % 128
    if pad:
        x = jnp.concatenate([x, jnp.zeros((pad, x.shape[1]), x.dtype)], axis=0)
    return x.T


def flat(x):
    pad = -x.shape[1] % 128
    slots = x.shape[1]
    if pad:
        x = jnp.concatenate([x, jnp.zeros((x.shape[0], pad), x.dtype)], axis=1)
    return x.T[:slots]


def pieces(x):
    high = x.astype(BF16)
    rest = x - high.astype(F32)
    mid = rest.astype(BF16)
    return high, mid, (rest - mid.astype(F32)).astype(BF16)


def products(whole, upper, lower, picked, rows):
    _, kept, side, _ = whole.shape
    pairs = lower.shape[1]
    turned, parts = {}, {}
    for _, x in picked:
        if id(x) not in turned:
            turned[id(x)] = columns(x[:kept])
            parts[id(x)] = [y.astype(F32) for y in pieces(x)]
    sub = lax.broadcasted_iota(jnp.int32, (16, side), 0)

    def on_vector_unit(k):
        wide = {}
        for n, (s, x) in enumerate(picked):
            if id(x) not in wide:
                wide[id(x)] = jnp.broadcast_to(turned[id(x)][:, k : k + 1], (side, side))
            rows[n, k : k + 1, :] = jnp.sum(whole[s, k] * wide[id(x)], axis=0, keepdims=True)

    def on_matrix_unit(m):
        left = {}
        for n, (s, x) in enumerate(picked):
            if id(x) not in left:
                stacks, firsts = [], []
                for u in range(2):
                    k = kept + 2 * m + u
                    high, mid, low = [y[k : k + 1, :] for y in parts[id(x)]]
                    stack = jnp.where(sub == 1, mid, jnp.where(sub == 2, low, 0.0))
                    stack = jnp.where(sub == 0, high, stack).astype(BF16)
                    stacks.append(jnp.concatenate([stack] * 2, axis=1))
                    firsts.append(jnp.where(sub == 8 * u, high, 0.0).astype(BF16))
                left[id(x)] = stacks, jnp.concatenate(firsts, axis=1)
            stacks, firsts = left[id(x)]
            rest = jnp.dot(firsts, lower[s, m], preferred_element_type=F32)
            for u in range(2):
                k = kept + 2 * m + u
                main = jnp.dot(stacks[u], upper[s, 2 * m + u], preferred_element_type=F32)
                total = main[:8] + rest[8 * u : 8 * u + 8]
                rows[n, k : k + 1, :] = jnp.sum(total, axis=0, keepdims=True)

    order = [((k + 0.5) / kept, on_vector_unit, k) for k in range(kept)]
    order += [((m + 0.5) / pairs, on_matrix_unit, m) for m in range(pairs)]
    for _, work, k in sorted(order, key=lambda entry: entry[0]):
        work(k)


def merge(a, b):
    top = jnp.maximum(a, b)
    return top + jnp.log(jnp.exp(a - top) + jnp.exp(b - top))


def bring(source, first, sizes, to, sems):
    copies, done = [], 0
    for n, size in enumerate(sizes):
        copy = pltpu.make_async_copy(
            source.at[:, pl.ds(first + done, size)], to.at[:, pl.ds(done, size)], sems.at[n]
        )
        copy.start()
        copies.append((copy, range(done, done + size)))
        done += size
    for copy, slots in copies:
        copy.wait()
        yield slots


def whole_kernel(sizes, source, order, whole, whole_t, token, sems):
    del order
    token[...] = jnp.zeros_like(token)
    for slots in bring(source, 0, sizes, whole, sems):
        for k in slots:
            for s in range(source.shape[0]):
                whole_t[s, k] = whole[s, k].T


def split_kernel(sizes, source, order, upper, upper_t, lower, lower_t, held, sems):
    del order
    scen, slots, side, _ = source.shape
    for brought in bring(source, slots - held.shape[1], sizes, held, sems):
        for k in brought:
            for s in range(scen):
                block = held[s, k]
                for x, up, low in ((block, upper, lower), (block.T, upper_t, lower_t)):
                    high, mid, rest = pieces(x)
                    up[s, k, :side] = high
                    up[s, k, side:] = mid
                    low[s, k // 2, k % 2 * side : (k % 2 + 1) * side] = rest


def hot_kernel(
    map_far, fluence, target_far, counts,
    col_hot, col_hot_t, same, leads, target, mine, block_map, target_rows, sems
):
    copies = [
        pltpu.make_async_copy(x, y, sems.at[n])
        for n, (x, y) in enumerate(
            [(map_far, block_map), (fluence, mine), (target_far, target_rows)]
        )
    ]
    for copy in copies:
        copy.start()
    for copy in copies:
        copy.wait()
    row_blocks, slots = leads.shape
    usable = lax.broadcasted_iota(jnp.int32, (row_blocks, slots), 1) < counts[...]
    rows = lax.broadcasted_iota(jnp.int32, (row_blocks, slots), 0) == block_map[0:1, :]
    row = jnp.where(rows & usable, 1.0, 0.0).astype(F32)
    beam_blocks = col_hot_t.shape[0]
    cols = lax.broadcasted_iota(jnp.int32, (beam_blocks, slots), 0) == block_map[1:2, :]
    col = jnp.where(cols, 1.0, 0.0).astype(F32)
    col_hot_t[...] = col.astype(BF16)
    col_hot[...] = flat(col).astype(BF16)
    row_hot = flat(row).astype(BF16)
    shared = jnp.dot(row_hot, row.astype(BF16), preferred_element_type=F32)
    same[...] = shared.astype(BF16)
    before = lax.broadcasted_iota(jnp.int32, (slots, slots), 0) < lax.broadcasted_iota(
        jnp.int32, (slots, slots), 1
    )
    earlier = jnp.sum(jnp.where(before, shared, 0.0), axis=0, keepdims=True)
    leads[...] = jnp.where(earlier == 0.0, row, 0.0).astype(BF16)
    target[...] = exact(row_hot, [target_rows[...]])[0]


def join_kernel(bit, mine, other, order, joined):
    del order
    size = mine.shape[0]
    low = lax.axis_index("vox") & bit == 0
    joined[:size] = jnp.where(low, mine[...], other[...])
    joined[size:] = jnp.where(low, other[...], mine[...])


def first_kernel(whole, upper, lower, fluence, target, col_hot, same, *refs):
    *excess, score_sum, rows = refs
    scen = len(excess)
    picked = exact(col_hot[...], [fluence[...]])[0]
    products(whole, upper, lower, [(s, picked) for s in range(scen)], rows)
    scores = []
    for s, dose in enumerate(exact(same[...], [rows[s] for s in range(scen)])):
        e = dose - target[...]
        excess[s][...] = e
        scores.append(SHARPNESS * e * e)
    top = functools.reduce(jnp.maximum, scores)
    total = functools.reduce(jnp.add, [jnp.exp(score - top) for score in scores])
    score_sum[...] = top + jnp.log(total)


def second_kernel(scens, whole, upper, lower, sum_a, sum_b, col_hot_t, order, *refs):
    del order
    *refs, rows = refs
    n = len(scens)
    excess, weights, gradient = refs[:n], refs[n : 2 * n], refs[2 * n :]
    total = merge(sum_a[...], sum_b[...])
    picked = []
    for m, s in enumerate(scens):
        e = excess[m][...]
        w = jnp.exp(SHARPNESS * e * e - total)
        weights[m][...] = w
        picked.append((s, 2.0 * w * e))
    products(whole, upper, lower, picked, rows)
    for m, g in enumerate(exact(col_hot_t[...], [rows[m] for m in range(n)])):
        gradient[m][...] = g


def third_kernel(
    scens, whole, upper, lower, whole_t, upper_t, lower_t, fluence, target,
    col_hot, col_hot_t, same, *refs
):
    *refs, rows, held = refs
    n = len(scens)
    grad_a, grad_b, weights, refs = refs[:n], refs[n : 2 * n], refs[2 * n : 3 * n], refs[3 * n :]
    together = len(refs[-1].shape) == 4
    others = refs[: len(refs) - n - (1 if together else n)]
    copies = refs[len(others) : len(others) + n]
    gradient = refs[len(others) + n :]
    share = copies[0].shape[0]
    mine = pl.ds(0 if share == held.shape[1] else lax.axis_index("vox") * share, share)
    for m in range(n):
        step = STEP_SIZE * (grad_a[m][...] + grad_b[m][...])
        held[m] = jnp.maximum(fluence[...] - step, 0.0)
        copies[m][...] = held[m, mine]
    picked = exact(col_hot[...], [held[m] for m in range(n)])
    products(whole_t, upper_t, lower_t, list(zip(scens, picked)), rows)
    doses = exact(same[...], [rows[m] for m in range(n)])
    picked = [2.0 * weights[m][...] * (doses[m] - target[...]) for m in range(n)]
    products(whole, upper, lower, list(zip(scens, picked)), rows)
    found = exact(col_hot_t[...], [rows[m] for m in range(n)])
    if not together:
        for m, g in enumerate(found):
            gradient[m][...] = g
        return
    parts, _, *piece = gradient[0].shape
    for m, g in enumerate([*(x[...] for x in others), *found]):
        gradient[0][:, m] = g.reshape(parts, *piece)


def place_kernel(scen_total, leads, order, *refs):
    del order
    used = jnp.sum(leads[...].astype(F32), axis=1, keepdims=True)
    *weights, placed = refs
    for s, w in enumerate(exact(leads[...], [x[...] for x in weights])):
        placed[:, s] = jnp.where(used == 0.0, 1.0 / scen_total, w)


def near(x):
    return pltpu.with_memory_space_constraint(x, pltpu.VMEM)


def far(x):
    return pltpu.with_memory_space_constraint(x, pltpu.HBM)


def swap(x, axis, bit):
    return lax.ppermute(x, axis, [(i, i ^ bit) for i in range(lax.axis_size(axis))])


def bits(axis):
    size = lax.axis_size(axis)
    if size & (size - 1) or size < 2:
        raise ValueError("axis size")
    return [1 << b for b in range(size.bit_length() - 1)]


def reduce_vox(x):
    steps = bits("vox")
    orders = [steps, steps]
    if len(steps) > 2:
        first, far, *between = steps[0], steps[-1], *steps[1:-1]
        orders = [[far, first, *between], [first, far, *between]]
    other = None
    for pair in zip(*orders):
        if other is not None:
            x = x + other
        other = lax.ppermute(
            x,
            "vox",
            [(v, v ^ pair[(v & steps[-2]) // steps[-2]]) for v in range(lax.axis_size("vox"))],
        )
    return x, other


def reduce_scen(x, combine):
    steps = bits("scen")
    x = [x, swap(x, "scen", steps[0])]
    for bit in steps[1:]:
        both = combine(*x)
        x = [both, swap(both, "scen", bit ^ 1)]
    return x


def swap_both(x, bit):
    scen, vox = lax.axis_size("scen"), lax.axis_size("vox")
    pairs = [(s * vox + v, (s ^ 1) * vox + (v ^ bit)) for s in range(scen) for v in range(vox)]
    return lax.ppermute(x, ("scen", "vox"), pairs)


def split(total, parts):
    return [total * (n + 1) // parts - total * n // parts for n in range(parts)]


def body(dose_blocks, block_map, block_counts, target, fluence_init):
    scen, slots, side, _ = dose_blocks.shape
    share = fluence_init.shape[0]
    parts = lax.axis_size("vox")
    beam_blocks = share * parts // side
    row_blocks = target.shape[0] // side
    scen_total = scen * lax.axis_size("scen")
    params = pltpu.CompilerParams(vmem_limit_bytes=16 * 2**20)
    passes = scen * slots * side * side
    dense = lambda *shape: jax.ShapeDtypeStruct(shape, F32)

    fluence = fluence_init.reshape(share // side, side)
    half = lambda *shape: jax.ShapeDtypeStruct(shape, BF16)
    col_hot, col_hot_t, same, leads, target, mine = pl.pallas_call(
        hot_kernel,
        name="hot",
        out_shape=(
            half(slots, beam_blocks),
            half(beam_blocks, slots),
            half(slots, slots),
            half(row_blocks, slots),
            dense(slots, side),
            dense(*fluence.shape),
        ),
        in_specs=[FAR] * 3 + [VMEM],
        out_specs=(VMEM,) * 6,
        scratch_shapes=[
            pltpu.VMEM((2, slots), jnp.int32),
            pltpu.VMEM((row_blocks, side), F32),
            pltpu.SemaphoreType.DMA((3,)),
        ],
        compiler_params=params,
    )(
        far(block_map.T),
        far(fluence),
        far(target.reshape(row_blocks, side)),
        block_counts.reshape(1, 1),
    )

    kept = slots * 2 // 5
    kept += (slots - kept) % 2
    rest = slots - kept
    steps = bits("vox")
    for n, bit in enumerate(steps):
        other = swap_both(fluence, bit)
        if n == 0:
            fluence = mine
        token = fluence
        if n == max(len(steps) - 2, 0):
            sizes = split(kept, 4)
            whole, whole_t, token = pl.pallas_call(
                functools.partial(whole_kernel, sizes),
                name="whole",
                out_shape=(pltpu.VMEM((scen, kept, side, side), F32),) * 2 + (dense(8, 128),),
                in_specs=[FAR, VMEM],
                out_specs=(VMEM,) * 3,
                scratch_shapes=[pltpu.SemaphoreType.DMA((len(sizes),))],
                compiler_params=params,
                cost_estimate=pl.CostEstimate(
                    flops=0, bytes_accessed=3 * passes, transcendentals=0
                ),
            )(far(dose_blocks), token)
        if n == len(steps) - 1:
            sizes = split(rest, 6)
            upper, upper_t, lower, lower_t = pl.pallas_call(
                functools.partial(split_kernel, sizes),
                name="split",
                out_shape=(pltpu.VMEM((scen, rest, 2 * side, side), BF16),) * 2
                + (pltpu.VMEM((scen, rest // 2, 2 * side, side), BF16),) * 2,
                in_specs=[FAR, VMEM],
                out_specs=(VMEM,) * 4,
                scratch_shapes=[
                    pltpu.VMEM((scen, rest, side, side), F32),
                    pltpu.SemaphoreType.DMA((len(sizes),)),
                ],
                compiler_params=params,
                cost_estimate=pl.CostEstimate(
                    flops=0, bytes_accessed=5 * passes, transcendentals=0
                ),
            )(far(dose_blocks), fluence)
        fluence = pl.pallas_call(
            functools.partial(join_kernel, bit),
            name="join",
            out_shape=dense(2 * fluence.shape[0], side),
            in_specs=[VMEM] * 3,
            out_specs=VMEM,
            compiler_params=params,
        )(fluence, other, token)
    blocks = [near(x) for x in (whole, upper, lower)]
    flipped = [near(x) for x in (whole_t, upper_t, lower_t)]

    for outer_round in range(ROUNDS):
        last = outer_round == ROUNDS - 1
        *excess, score_sum = pl.pallas_call(
            first_kernel,
            name="first",
            out_shape=(dense(slots, side),) * (scen + 1),
            in_specs=[VMEM] * 7,
            out_specs=(VMEM,) * (scen + 1),
            scratch_shapes=[pltpu.VMEM((scen, slots, side), F32)],
            compiler_params=params,
        )(*flipped, fluence, target, col_hot, same)
        sum_a, sum_b = reduce_scen(score_sum, merge)

        groups = [[s] for s in range(scen)] if last else [list(range(scen))]
        weights, gradients, order = [], [], score_sum
        for group in groups:
            n = len(group)
            found = pl.pallas_call(
                functools.partial(second_kernel, group),
                name="second",
                out_shape=(dense(slots, side),) * n + (dense(beam_blocks, side),) * n,
                in_specs=[VMEM] * (7 + n),
                out_specs=(VMEM,) * (2 * n),
                scratch_shapes=[pltpu.VMEM((n, slots, side), F32)],
                compiler_params=params,
            )(*blocks, sum_a, sum_b, col_hot_t, order, *[excess[s] for s in group])
            order = found[-1]
            weights += found[:n]
            gradients += found[n:]
        sums = [reduce_vox(gradient) for gradient in gradients]
        copies, gradients = [], []
        for group in groups:
            n = len(group)
            together = last and group is groups[-1]
            others = gradients if together else []
            form = [(parts, scen, share // side, side)] if together else [(beam_blocks, side)] * n
            found = pl.pallas_call(
                functools.partial(third_kernel, group),
                name="third",
                out_shape=(dense(share // side if last else beam_blocks, side),) * n
                + tuple(dense(*shape) for shape in form),
                in_specs=[VMEM] * (11 + 3 * n + len(others)),
                out_specs=(VMEM,) * (n + len(form)),
                scratch_shapes=[
                    pltpu.VMEM((n, slots, side), F32),
                    pltpu.VMEM((n, beam_blocks, side), F32),
                ],
                compiler_params=params,
            )(
                *blocks, *flipped, fluence, target, col_hot, col_hot_t, same,
                *[sums[s][0] for s in group], *[sums[s][1] for s in group],
                *[weights[s] for s in group], *others,
            )
            copies += found[:n]
            gradients += found[n:]
        if not last:
            sums = [reduce_vox(gradient) for gradient in gradients]
            gradients = [a + b for a, b in sums]
        else:
            gradient, copies = lax.optimization_barrier((gradients[-1], copies))
            gradient = lax.all_to_all(gradient, "vox", split_axis=0, concat_axis=0, tiled=True)
            gradient = jnp.sum(gradient, axis=0)
            gradients = [gradient[s] for s in range(scen)]
        copies = [jnp.maximum(c - STEP_SIZE * g, 0.0) for c, g in zip(copies, gradients)]
        total = functools.reduce(jnp.add, copies)
        if last:
            others = [swap(total, "scen", n) for n in range(1, lax.axis_size("scen"))]
            placed = pl.pallas_call(
                functools.partial(place_kernel, scen_total),
                name="place",
                out_shape=dense(row_blocks, scen, side),
                in_specs=[VMEM] * (2 + scen),
                out_specs=VMEM,
                compiler_params=params,
                cost_estimate=pl.CostEstimate(
                    flops=0, bytes_accessed=8 * scen * row_blocks * side, transcendentals=0
                ),
            )(leads, total, *weights)
            weights = jnp.swapaxes(placed, 0, 1).reshape(scen, row_blocks * side)
            total = functools.reduce(jnp.add, others, total)
        else:
            total = functools.reduce(jnp.add, reduce_scen(total, jnp.add))
        fluence = total / scen_total
    return fluence.reshape(share), weights


def solution(mesh):
    placed = (P("scen", "vox", None, None), P("vox", None), P("vox"), P("vox"), P("vox"))
    return jax.shard_map(
        body, mesh=mesh, in_specs=placed, out_specs=(P("vox"), P("scen", "vox")), check_vma=False
    )
```

```python
import functools

import jax
import jax.numpy as jnp
from jax import lax
from jax.experimental import pallas as pl
from jax.experimental.pallas import tpu as pltpu
from jax.sharding import PartitionSpec as P

ROUNDS = 2
SHARPNESS = 2.0
STEP_SIZE = 0.5
F32 = jnp.float32
BF16 = jnp.bfloat16
VMEM = pl.BlockSpec(memory_space=pltpu.VMEM)
FAR = pl.BlockSpec(memory_space=pltpu.HBM)


def exact(hot, xs):
    n = xs[0].shape[1]
    every = jnp.concatenate([y for x in xs for y in pieces(x)], axis=1)
    y = jnp.dot(hot, every, preferred_element_type=F32)
    parts = [y[:, m * n : (m + 1) * n] for m in range(3 * len(xs))]
    return [parts[m] + parts[m + 1] + parts[m + 2] for m in range(0, len(parts), 3)]


def columns(x):
    pad = -x.shape[0] % 128
    if pad:
        x = jnp.concatenate([x, jnp.zeros((pad, x.shape[1]), x.dtype)], axis=0)
    return x.T


def flat(x):
    pad = -x.shape[1] % 128
    slots = x.shape[1]
    if pad:
        x = jnp.concatenate([x, jnp.zeros((x.shape[0], pad), x.dtype)], axis=1)
    return x.T[:slots]


def pieces(x):
    high = x.astype(BF16)
    rest = x - high.astype(F32)
    mid = rest.astype(BF16)
    return high, mid, (rest - mid.astype(F32)).astype(BF16)


def products(whole, upper, lower, picked, rows):
    _, kept, side, _ = whole.shape
    pairs = lower.shape[1]
    turned, parts = {}, {}
    for _, x in picked:
        if id(x) not in turned:
            turned[id(x)] = columns(x[:kept])
            parts[id(x)] = [y.astype(F32) for y in pieces(x)]
    sub = lax.broadcasted_iota(jnp.int32, (16, side), 0)

    def on_vector_unit(k):
        wide = {}
        for n, (s, x) in enumerate(picked):
            if id(x) not in wide:
                wide[id(x)] = jnp.broadcast_to(turned[id(x)][:, k : k + 1], (side, side))
            rows[n, k : k + 1, :] = jnp.sum(whole[s, k] * wide[id(x)], axis=0, keepdims=True)

    def on_matrix_unit(m):
        left = {}
        for n, (s, x) in enumerate(picked):
            if id(x) not in left:
                stacks, firsts = [], []
                for u in range(2):
                    k = kept + 2 * m + u
                    high, mid, low = [y[k : k + 1, :] for y in parts[id(x)]]
                    stack = jnp.where(sub == 1, mid, jnp.where(sub == 2, low, 0.0))
                    stack = jnp.where(sub == 0, high, stack).astype(BF16)
                    stacks.append(jnp.concatenate([stack] * 2, axis=1))
                    firsts.append(jnp.where(sub == 8 * u, high, 0.0).astype(BF16))
                left[id(x)] = stacks, jnp.concatenate(firsts, axis=1)
            stacks, firsts = left[id(x)]
            rest = jnp.dot(firsts, lower[s, m], preferred_element_type=F32)
            for u in range(2):
                k = kept + 2 * m + u
                main = jnp.dot(stacks[u], upper[s, 2 * m + u], preferred_element_type=F32)
                total = main[:8] + rest[8 * u : 8 * u + 8]
                rows[n, k : k + 1, :] = jnp.sum(total, axis=0, keepdims=True)

    order = [((k + 0.5) / kept, on_vector_unit, k) for k in range(kept)]
    order += [((m + 0.5) / pairs, on_matrix_unit, m) for m in range(pairs)]
    for _, work, k in sorted(order, key=lambda entry: entry[0]):
        work(k)


def log_sum_exp(xs):
    top = functools.reduce(jnp.maximum, xs)
    return top + jnp.log(functools.reduce(jnp.add, [jnp.exp(x - top) for x in xs]))


def bring(source, first, sizes, to, sems):
    copies, done = [], 0
    for n, size in enumerate(sizes):
        copy = pltpu.make_async_copy(
            source.at[:, pl.ds(first + done, size)], to.at[:, pl.ds(done, size)], sems.at[n]
        )
        copy.start()
        copies.append((copy, range(done, done + size)))
        done += size
    for copy, slots in copies:
        copy.wait()
        yield slots


def whole_kernel(sizes, source, order, whole, whole_t, token, sems):
    del order
    token[...] = jnp.zeros_like(token)
    for slots in bring(source, 0, sizes, whole, sems):
        for k in slots:
            for s in range(source.shape[0]):
                whole_t[s, k] = whole[s, k].T


def split_kernel(sizes, source, order, upper, upper_t, lower, lower_t, held, sems):
    del order
    scen, slots, side, _ = source.shape
    for brought in bring(source, slots - held.shape[1], sizes, held, sems):
        for k in brought:
            for s in range(scen):
                block = held[s, k]
                for x, up, low in ((block, upper, lower), (block.T, upper_t, lower_t)):
                    high, mid, rest = pieces(x)
                    up[s, k, :side] = high
                    up[s, k, side:] = mid
                    low[s, k // 2, k % 2 * side : (k % 2 + 1) * side] = rest


def hot_kernel(
    map_far, fluence, target_far, counts,
    col_hot, col_hot_t, same, leads, target, mine, block_map, target_rows, sems
):
    copies = [
        pltpu.make_async_copy(x, y, sems.at[n])
        for n, (x, y) in enumerate(
            [(map_far, block_map), (fluence, mine), (target_far, target_rows)]
        )
    ]
    for copy in copies:
        copy.start()
    for copy in copies:
        copy.wait()
    row_blocks, slots = leads.shape
    usable = lax.broadcasted_iota(jnp.int32, (row_blocks, slots), 1) < counts[...]
    rows = lax.broadcasted_iota(jnp.int32, (row_blocks, slots), 0) == block_map[0:1, :]
    row = jnp.where(rows & usable, 1.0, 0.0).astype(F32)
    beam_blocks = col_hot_t.shape[0]
    cols = lax.broadcasted_iota(jnp.int32, (beam_blocks, slots), 0) == block_map[1:2, :]
    col = jnp.where(cols, 1.0, 0.0).astype(F32)
    col_hot_t[...] = col.astype(BF16)
    col_hot[...] = flat(col).astype(BF16)
    row_hot = flat(row).astype(BF16)
    shared = jnp.dot(row_hot, row.astype(BF16), preferred_element_type=F32)
    same[...] = shared.astype(BF16)
    before = lax.broadcasted_iota(jnp.int32, (slots, slots), 0) < lax.broadcasted_iota(
        jnp.int32, (slots, slots), 1
    )
    earlier = jnp.sum(jnp.where(before, shared, 0.0), axis=0, keepdims=True)
    leads[...] = jnp.where(earlier == 0.0, row, 0.0).astype(BF16)
    target[...] = exact(row_hot, [target_rows[...]])[0]


def join_kernel(bit, mine, other, order, joined):
    del order
    size = mine.shape[0]
    low = lax.axis_index("vox") & bit == 0
    joined[:size] = jnp.where(low, mine[...], other[...])
    joined[size:] = jnp.where(low, other[...], mine[...])


def first_kernel(whole, upper, lower, fluence, target, col_hot, same, *refs):
    *excess, score_sum, rows = refs
    scen = len(excess)
    picked = exact(col_hot[...], [fluence[...]])[0]
    products(whole, upper, lower, [(s, picked) for s in range(scen)], rows)
    scores = []
    for s, dose in enumerate(exact(same[...], [rows[s] for s in range(scen)])):
        e = dose - target[...]
        excess[s][...] = e
        scores.append(SHARPNESS * e * e)
    score_sum[...] = log_sum_exp(scores)


def second_kernel(scens, whole, upper, lower, col_hot_t, order, *refs):
    del order
    *refs, rows = refs
    n = len(scens)
    sums, refs = refs[: -3 * n], refs[-3 * n :]
    excess, weights, gradient = refs[:n], refs[n : 2 * n], refs[2 * n :]
    total = log_sum_exp([x[...] for x in sums])
    picked = []
    for m, s in enumerate(scens):
        e = excess[m][...]
        w = jnp.exp(SHARPNESS * e * e - total)
        weights[m][...] = w
        picked.append((s, 2.0 * w * e))
    products(whole, upper, lower, picked, rows)
    for m, g in enumerate(exact(col_hot_t[...], [rows[m] for m in range(n)])):
        gradient[m][...] = g


def third_kernel(
    scens, whole, upper, lower, whole_t, upper_t, lower_t, fluence, target,
    col_hot, col_hot_t, same, *refs
):
    *refs, rows, held = refs
    n = len(scens)
    grad_a, grad_b, weights, refs = refs[:n], refs[n : 2 * n], refs[2 * n : 3 * n], refs[3 * n :]
    together = len(refs[-1].shape) == 4
    others = refs[: len(refs) - n - (1 if together else n)]
    copies = refs[len(others) : len(others) + n]
    gradient = refs[len(others) + n :]
    share = copies[0].shape[0]
    mine = pl.ds(0 if share == held.shape[1] else lax.axis_index("vox") * share, share)
    for m in range(n):
        step = STEP_SIZE * (grad_a[m][...] + grad_b[m][...])
        held[m] = jnp.maximum(fluence[...] - step, 0.0)
        copies[m][...] = held[m, mine]
    picked = exact(col_hot[...], [held[m] for m in range(n)])
    products(whole_t, upper_t, lower_t, list(zip(scens, picked)), rows)
    doses = exact(same[...], [rows[m] for m in range(n)])
    picked = [2.0 * weights[m][...] * (doses[m] - target[...]) for m in range(n)]
    products(whole, upper, lower, list(zip(scens, picked)), rows)
    found = exact(col_hot_t[...], [rows[m] for m in range(n)])
    if not together:
        for m, g in enumerate(found):
            gradient[m][...] = g
        return
    parts, _, *piece = gradient[0].shape
    for m, g in enumerate([*(x[...] for x in others), *found]):
        gradient[0][:, m] = g.reshape(parts, *piece)


def place_kernel(scen_total, leads, order, *refs):
    del order
    used = jnp.sum(leads[...].astype(F32), axis=1, keepdims=True)
    *weights, placed = refs
    for s, w in enumerate(exact(leads[...], [x[...] for x in weights])):
        placed[:, s] = jnp.where(used == 0.0, 1.0 / scen_total, w)


def near(x):
    return pltpu.with_memory_space_constraint(x, pltpu.VMEM)


def far(x):
    return pltpu.with_memory_space_constraint(x, pltpu.HBM)


def swap(x, axis, bit):
    return lax.ppermute(x, axis, [(i, i ^ bit) for i in range(lax.axis_size(axis))])


def bits(axis):
    size = lax.axis_size(axis)
    if size & (size - 1) or size < 2:
        raise ValueError("axis size")
    return [1 << b for b in range(size.bit_length() - 1)]


def reduce_vox(x):
    steps = bits("vox")
    orders = [steps, steps]
    if len(steps) > 2:
        first, far, *between = steps[0], steps[-1], *steps[1:-1]
        orders = [[far, first, *between], [first, far, *between]]
    other = None
    for pair in zip(*orders):
        if other is not None:
            x = x + other
        other = lax.ppermute(
            x,
            "vox",
            [(v, v ^ pair[(v & steps[-2]) // steps[-2]]) for v in range(lax.axis_size("vox"))],
        )
    return x, other


def spread_scen(x):
    return [x] + [swap(x, "scen", n) for n in range(1, lax.axis_size("scen"))]


def swap_both(x, bit):
    scen, vox = lax.axis_size("scen"), lax.axis_size("vox")
    pairs = [(s * vox + v, (s ^ 1) * vox + (v ^ bit)) for s in range(scen) for v in range(vox)]
    return lax.ppermute(x, ("scen", "vox"), pairs)


def split(total, parts):
    return [total * (n + 1) // parts - total * n // parts for n in range(parts)]


def body(dose_blocks, block_map, block_counts, target, fluence_init):
    scen, slots, side, _ = dose_blocks.shape
    share = fluence_init.shape[0]
    parts = lax.axis_size("vox")
    beam_blocks = share * parts // side
    row_blocks = target.shape[0] // side
    scen_total = scen * lax.axis_size("scen")
    params = pltpu.CompilerParams(vmem_limit_bytes=16 * 2**20)
    passes = scen * slots * side * side
    dense = lambda *shape: jax.ShapeDtypeStruct(shape, F32)

    fluence = fluence_init.reshape(share // side, side)
    half = lambda *shape: jax.ShapeDtypeStruct(shape, BF16)
    col_hot, col_hot_t, same, leads, target, mine = pl.pallas_call(
        hot_kernel,
        name="hot",
        out_shape=(
            half(slots, beam_blocks),
            half(beam_blocks, slots),
            half(slots, slots),
            half(row_blocks, slots),
            dense(slots, side),
            dense(*fluence.shape),
        ),
        in_specs=[FAR] * 3 + [VMEM],
        out_specs=(VMEM,) * 6,
        scratch_shapes=[
            pltpu.VMEM((2, slots), jnp.int32),
            pltpu.VMEM((row_blocks, side), F32),
            pltpu.SemaphoreType.DMA((3,)),
        ],
        compiler_params=params,
    )(
        far(block_map.T),
        far(fluence),
        far(target.reshape(row_blocks, side)),
        block_counts.reshape(1, 1),
    )

    kept = slots * 2 // 5
    kept += (slots - kept) % 2
    rest = slots - kept
    steps = bits("vox")
    for n, bit in enumerate(steps):
        other = swap_both(fluence, bit)
        if n == 0:
            fluence = mine
        token = fluence
        if n == max(len(steps) - 2, 0):
            sizes = split(kept, 4)
            whole, whole_t, token = pl.pallas_call(
                functools.partial(whole_kernel, sizes),
                name="whole",
                out_shape=(pltpu.VMEM((scen, kept, side, side), F32),) * 2 + (dense(8, 128),),
                in_specs=[FAR, VMEM],
                out_specs=(VMEM,) * 3,
                scratch_shapes=[pltpu.SemaphoreType.DMA((len(sizes),))],
                compiler_params=params,
                cost_estimate=pl.CostEstimate(
                    flops=0, bytes_accessed=3 * passes, transcendentals=0
                ),
            )(far(dose_blocks), token)
        if n == len(steps) - 1:
            sizes = split(rest, 6)
            upper, upper_t, lower, lower_t = pl.pallas_call(
                functools.partial(split_kernel, sizes),
                name="split",
                out_shape=(pltpu.VMEM((scen, rest, 2 * side, side), BF16),) * 2
                + (pltpu.VMEM((scen, rest // 2, 2 * side, side), BF16),) * 2,
                in_specs=[FAR, VMEM],
                out_specs=(VMEM,) * 4,
                scratch_shapes=[
                    pltpu.VMEM((scen, rest, side, side), F32),
                    pltpu.SemaphoreType.DMA((len(sizes),)),
                ],
                compiler_params=params,
                cost_estimate=pl.CostEstimate(
                    flops=0, bytes_accessed=5 * passes, transcendentals=0
                ),
            )(far(dose_blocks), fluence)
        fluence = pl.pallas_call(
            functools.partial(join_kernel, bit),
            name="join",
            out_shape=dense(2 * fluence.shape[0], side),
            in_specs=[VMEM] * 3,
            out_specs=VMEM,
            compiler_params=params,
        )(fluence, other, token)
    blocks = [near(x) for x in (whole, upper, lower)]
    flipped = [near(x) for x in (whole_t, upper_t, lower_t)]

    for outer_round in range(ROUNDS):
        last = outer_round == ROUNDS - 1
        *excess, score_sum = pl.pallas_call(
            first_kernel,
            name="first",
            out_shape=(dense(slots, side),) * (scen + 1),
            in_specs=[VMEM] * 7,
            out_specs=(VMEM,) * (scen + 1),
            scratch_shapes=[pltpu.VMEM((scen, slots, side), F32)],
            compiler_params=params,
        )(*flipped, fluence, target, col_hot, same)
        score_sums = spread_scen(score_sum)

        groups = [[s] for s in range(scen)] if last else [list(range(scen))]
        weights, gradients, order = [], [], score_sum
        for group in groups:
            n = len(group)
            found = pl.pallas_call(
                functools.partial(second_kernel, group),
                name="second",
                out_shape=(dense(slots, side),) * n + (dense(beam_blocks, side),) * n,
                in_specs=[VMEM] * (5 + len(score_sums) + n),
                out_specs=(VMEM,) * (2 * n),
                scratch_shapes=[pltpu.VMEM((n, slots, side), F32)],
                compiler_params=params,
            )(*blocks, col_hot_t, order, *score_sums, *[excess[s] for s in group])
            order = found[-1]
            weights += found[:n]
            gradients += found[n:]
        sums = [reduce_vox(gradient) for gradient in gradients]
        copies, gradients = [], []
        for group in groups:
            n = len(group)
            together = last and group is groups[-1]
            others = gradients if together else []
            form = [(parts, scen, share // side, side)] if together else [(beam_blocks, side)] * n
            found = pl.pallas_call(
                functools.partial(third_kernel, group),
                name="third",
                out_shape=(dense(share // side if last else beam_blocks, side),) * n
                + tuple(dense(*shape) for shape in form),
                in_specs=[VMEM] * (11 + 3 * n + len(others)),
                out_specs=(VMEM,) * (n + len(form)),
                scratch_shapes=[
                    pltpu.VMEM((n, slots, side), F32),
                    pltpu.VMEM((n, beam_blocks, side), F32),
                ],
                compiler_params=params,
            )(
                *blocks, *flipped, fluence, target, col_hot, col_hot_t, same,
                *[sums[s][0] for s in group], *[sums[s][1] for s in group],
                *[weights[s] for s in group], *others,
            )
            copies += found[:n]
            gradients += found[n:]
        if not last:
            sums = [reduce_vox(gradient) for gradient in gradients]
            gradients = [a + b for a, b in sums]
        else:
            gradient, copies = lax.optimization_barrier((gradients[-1], copies))
            gradient = lax.all_to_all(gradient, "vox", split_axis=0, concat_axis=0, tiled=True)
            gradient = jnp.sum(gradient, axis=0)
            gradients = [gradient[s] for s in range(scen)]
        copies = [jnp.maximum(c - STEP_SIZE * g, 0.0) for c, g in zip(copies, gradients)]
        total = functools.reduce(jnp.add, copies)
        totals = spread_scen(total)
        if last:
            placed = pl.pallas_call(
                functools.partial(place_kernel, scen_total),
                name="place",
                out_shape=dense(row_blocks, scen, side),
                in_specs=[VMEM] * (2 + scen),
                out_specs=VMEM,
                compiler_params=params,
                cost_estimate=pl.CostEstimate(
                    flops=0, bytes_accessed=8 * scen * row_blocks * side, transcendentals=0
                ),
            )(leads, total, *weights)
            weights = jnp.swapaxes(placed, 0, 1).reshape(scen, row_blocks * side)
        fluence = functools.reduce(jnp.add, totals) / scen_total
    return fluence.reshape(share), weights


def solution(mesh):
    placed = (P("scen", "vox", None, None), P("vox", None), P("vox"), P("vox"), P("vox"))
    return jax.shard_map(
        body, mesh=mesh, in_specs=placed, out_specs=(P("vox"), P("scen", "vox")), check_vma=False
    )
```

```python
import functools

import jax
import jax.numpy as jnp
from jax import lax
from jax.experimental import pallas as pl
from jax.experimental.pallas import tpu as pltpu
from jax.sharding import PartitionSpec as P

ROUNDS = 2
SHARPNESS = 2.0
STEP_SIZE = 0.5
F32 = jnp.float32
BF16 = jnp.bfloat16
VMEM = pl.BlockSpec(memory_space=pltpu.VMEM)
FAR = pl.BlockSpec(memory_space=pltpu.HBM)


def exact(hot, xs):
    n = xs[0].shape[1]
    every = jnp.concatenate([y for x in xs for y in pieces(x)], axis=1)
    y = jnp.dot(hot, every, preferred_element_type=F32)
    parts = [y[:, m * n : (m + 1) * n] for m in range(3 * len(xs))]
    return [parts[m] + parts[m + 1] + parts[m + 2] for m in range(0, len(parts), 3)]


def columns(x):
    pad = -x.shape[0] % 128
    if pad:
        x = jnp.concatenate([x, jnp.zeros((pad, x.shape[1]), x.dtype)], axis=0)
    return x.T


def flat(x):
    pad = -x.shape[1] % 128
    slots = x.shape[1]
    if pad:
        x = jnp.concatenate([x, jnp.zeros((x.shape[0], pad), x.dtype)], axis=1)
    return x.T[:slots]


def pieces(x):
    high = x.astype(BF16)
    rest = x - high.astype(F32)
    mid = rest.astype(BF16)
    return high, mid, (rest - mid.astype(F32)).astype(BF16)


def products(whole, upper, lower, picked, rows):
    _, kept, side, _ = whole.shape
    pairs = lower.shape[1]
    turned, parts = {}, {}
    for _, x in picked:
        if id(x) not in turned:
            turned[id(x)] = columns(x[:kept])
            parts[id(x)] = [y.astype(F32) for y in pieces(x)]
    sub = lax.broadcasted_iota(jnp.int32, (16, side), 0)

    def on_vector_unit(k):
        wide = {}
        for n, (s, x) in enumerate(picked):
            if id(x) not in wide:
                wide[id(x)] = jnp.broadcast_to(turned[id(x)][:, k : k + 1], (side, side))
            rows[n, k : k + 1, :] = jnp.sum(whole[s, k] * wide[id(x)], axis=0, keepdims=True)

    def on_matrix_unit(m):
        left = {}
        for n, (s, x) in enumerate(picked):
            if id(x) not in left:
                stacks, firsts = [], []
                for u in range(2):
                    k = kept + 2 * m + u
                    high, mid, low = [y[k : k + 1, :] for y in parts[id(x)]]
                    stack = jnp.where(sub == 1, mid, jnp.where(sub == 2, low, 0.0))
                    stack = jnp.where(sub == 0, high, stack).astype(BF16)
                    stacks.append(jnp.concatenate([stack] * 2, axis=1))
                    firsts.append(jnp.where(sub == 8 * u, high, 0.0).astype(BF16))
                left[id(x)] = stacks, jnp.concatenate(firsts, axis=1)
            stacks, firsts = left[id(x)]
            rest = jnp.dot(firsts, lower[s, m], preferred_element_type=F32)
            for u in range(2):
                k = kept + 2 * m + u
                main = jnp.dot(stacks[u], upper[s, 2 * m + u], preferred_element_type=F32)
                total = main[:8] + rest[8 * u : 8 * u + 8]
                rows[n, k : k + 1, :] = jnp.sum(total, axis=0, keepdims=True)

    order = [((k + 0.5) / kept, on_vector_unit, k) for k in range(kept)]
    order += [((m + 0.5) / pairs, on_matrix_unit, m) for m in range(pairs)]
    for _, work, k in sorted(order, key=lambda entry: entry[0]):
        work(k)


def log_sum_exp(xs):
    top = functools.reduce(jnp.maximum, xs)
    return top + jnp.log(functools.reduce(jnp.add, [jnp.exp(x - top) for x in xs]))


def bring(source, first, sizes, to, sems):
    copies, done = [], 0
    for n, size in enumerate(sizes):
        copy = pltpu.make_async_copy(
            source.at[:, pl.ds(first + done, size)], to.at[:, pl.ds(done, size)], sems.at[n]
        )
        copy.start()
        copies.append((copy, range(done, done + size)))
        done += size
    yield range(0)
    for copy, slots in copies:
        copy.wait()
        yield slots


def split_kernel(sizes, source, order, upper, upper_t, lower, lower_t, held, sems):
    del order
    scen, slots, side, _ = source.shape
    for ready in bring(source, slots - held.shape[1], sizes, held, sems):
        for k in ready:
            for s in range(scen):
                block = held[s, k]
                for x, up, low in ((block, upper, lower), (block.T, upper_t, lower_t)):
                    high, mid, rest = pieces(x)
                    up[s, k, :side] = high
                    up[s, k, side:] = mid
                    low[s, k // 2, k % 2 * side : (k % 2 + 1) * side] = rest


def hot_kernel(
    sizes, map_far, fluence, target_far, counts, source,
    col_hot, col_hot_t, same, leads, target, mine, whole, whole_t, block_map, target_rows, sems
):
    copies = [
        pltpu.make_async_copy(x, y, sems.at[n])
        for n, (x, y) in enumerate(
            [(map_far, block_map), (fluence, mine), (target_far, target_rows)]
        )
    ]
    for copy in copies:
        copy.start()
    brought = bring(source, 0, sizes, whole, sems.at[pl.ds(len(copies), len(sizes))])
    next(brought)
    for copy in copies:
        copy.wait()
    row_blocks, slots = leads.shape
    usable = lax.broadcasted_iota(jnp.int32, (row_blocks, slots), 1) < counts[...]
    rows = lax.broadcasted_iota(jnp.int32, (row_blocks, slots), 0) == block_map[0:1, :]
    row = jnp.where(rows & usable, 1.0, 0.0).astype(F32)
    beam_blocks = col_hot_t.shape[0]
    cols = lax.broadcasted_iota(jnp.int32, (beam_blocks, slots), 0) == block_map[1:2, :]
    col = jnp.where(cols, 1.0, 0.0).astype(F32)
    col_hot_t[...] = col.astype(BF16)
    col_hot[...] = flat(col).astype(BF16)
    row_hot = flat(row).astype(BF16)
    shared = jnp.dot(row_hot, row.astype(BF16), preferred_element_type=F32)
    same[...] = shared.astype(BF16)
    before = lax.broadcasted_iota(jnp.int32, (slots, slots), 0) < lax.broadcasted_iota(
        jnp.int32, (slots, slots), 1
    )
    earlier = jnp.sum(jnp.where(before, shared, 0.0), axis=0, keepdims=True)
    leads[...] = jnp.where(earlier == 0.0, row, 0.0).astype(BF16)
    target[...] = exact(row_hot, [target_rows[...]])[0]
    for ready in brought:
        for k in ready:
            for s in range(source.shape[0]):
                whole_t[s, k] = whole[s, k].T


def join_kernel(bit, mine, other, joined):
    size = mine.shape[0]
    low = lax.axis_index("vox") & bit == 0
    joined[:size] = jnp.where(low, mine[...], other[...])
    joined[size:] = jnp.where(low, other[...], mine[...])


def collect_kernel(*refs):
    *found, collected = refs
    count, size = len(found), found[0].shape[0]
    here = lax.axis_index("vox") & (count - 1)
    for offset, piece in enumerate(found):
        at = pl.multiple_of((here ^ offset) * size, size)
        collected[pl.ds(at, size)] = piece[...]


def first_kernel(whole, upper, lower, fluence, target, col_hot, same, *refs):
    *excess, score_sum, rows = refs
    scen = len(excess)
    picked = exact(col_hot[...], [fluence[...]])[0]
    products(whole, upper, lower, [(s, picked) for s in range(scen)], rows)
    scores = []
    for s, dose in enumerate(exact(same[...], [rows[s] for s in range(scen)])):
        e = dose - target[...]
        excess[s][...] = e
        scores.append(SHARPNESS * e * e)
    score_sum[...] = log_sum_exp(scores)


def second_kernel(scens, whole, upper, lower, col_hot_t, order, *refs):
    del order
    *refs, rows = refs
    n = len(scens)
    sums, refs = refs[: -3 * n], refs[-3 * n :]
    excess, weights, gradient = refs[:n], refs[n : 2 * n], refs[2 * n :]
    total = log_sum_exp([x[...] for x in sums])
    picked = []
    for m, s in enumerate(scens):
        e = excess[m][...]
        w = jnp.exp(SHARPNESS * e * e - total)
        weights[m][...] = w
        picked.append((s, 2.0 * w * e))
    products(whole, upper, lower, picked, rows)
    for m, g in enumerate(exact(col_hot_t[...], [rows[m] for m in range(n)])):
        gradient[m][...] = g


def third_kernel(
    scens, whole, upper, lower, whole_t, upper_t, lower_t, fluence, target,
    col_hot, col_hot_t, same, *refs
):
    *refs, rows, held = refs
    n = len(scens)
    grad_a, grad_b, weights, refs = refs[:n], refs[n : 2 * n], refs[2 * n : 3 * n], refs[3 * n :]
    together = len(refs[-1].shape) == 4
    others = refs[: len(refs) - n - (1 if together else n)]
    copies = refs[len(others) : len(others) + n]
    gradient = refs[len(others) + n :]
    share = copies[0].shape[0]
    mine = pl.ds(0 if share == held.shape[1] else lax.axis_index("vox") * share, share)
    for m in range(n):
        step = STEP_SIZE * (grad_a[m][...] + grad_b[m][...])
        held[m] = jnp.maximum(fluence[...] - step, 0.0)
        copies[m][...] = held[m, mine]
    picked = exact(col_hot[...], [held[m] for m in range(n)])
    products(whole_t, upper_t, lower_t, list(zip(scens, picked)), rows)
    doses = exact(same[...], [rows[m] for m in range(n)])
    picked = [2.0 * weights[m][...] * (doses[m] - target[...]) for m in range(n)]
    products(whole, upper, lower, list(zip(scens, picked)), rows)
    found = exact(col_hot_t[...], [rows[m] for m in range(n)])
    if not together:
        for m, g in enumerate(found):
            gradient[m][...] = g
        return
    parts, _, *piece = gradient[0].shape
    for m, g in enumerate([*(x[...] for x in others), *found]):
        gradient[0][:, m] = g.reshape(parts, *piece)


def place_kernel(scen_total, leads, order, *refs):
    del order
    used = jnp.sum(leads[...].astype(F32), axis=1, keepdims=True)
    *weights, placed = refs
    for s, w in enumerate(exact(leads[...], [x[...] for x in weights])):
        placed[:, s] = jnp.where(used == 0.0, 1.0 / scen_total, w)


def near(x):
    return pltpu.with_memory_space_constraint(x, pltpu.VMEM)


def far(x):
    return pltpu.with_memory_space_constraint(x, pltpu.HBM)


def swap(x, axis, bit):
    return lax.ppermute(x, axis, [(i, i ^ bit) for i in range(lax.axis_size(axis))])


def bits(axis):
    size = lax.axis_size(axis)
    if size & (size - 1) or size < 2:
        raise ValueError("axis size")
    return [1 << b for b in range(size.bit_length() - 1)]


def reduce_vox(x):
    steps = bits("vox")
    orders = [steps, steps]
    if len(steps) > 2:
        first, far, *between = steps[0], steps[-1], *steps[1:-1]
        orders = [[far, first, *between], [first, far, *between]]
    other = None
    for pair in zip(*orders):
        if other is not None:
            x = x + other
        other = lax.ppermute(
            x,
            "vox",
            [(v, v ^ pair[(v & steps[-2]) // steps[-2]]) for v in range(lax.axis_size("vox"))],
        )
    return x, other


def spread_scen(x):
    return [x] + [swap(x, "scen", n) for n in range(1, lax.axis_size("scen"))]


def swap_both(x, bit):
    scen, vox = lax.axis_size("scen"), lax.axis_size("vox")
    pairs = [(s * vox + v, (s ^ 1) * vox + (v ^ bit)) for s in range(scen) for v in range(vox)]
    return lax.ppermute(x, ("scen", "vox"), pairs)


def split(total, parts):
    return [total * (n + 1) // parts - total * n // parts for n in range(parts)]


def body(dose_blocks, block_map, block_counts, target, fluence_init):
    scen, slots, side, _ = dose_blocks.shape
    share = fluence_init.shape[0]
    parts = lax.axis_size("vox")
    beam_blocks = share * parts // side
    row_blocks = target.shape[0] // side
    scen_total = scen * lax.axis_size("scen")
    params = pltpu.CompilerParams(vmem_limit_bytes=16 * 2**20)
    passes = scen * slots * side * side
    dense = lambda *shape: jax.ShapeDtypeStruct(shape, F32)

    fluence = fluence_init.reshape(share // side, side)
    half = lambda *shape: jax.ShapeDtypeStruct(shape, BF16)
    kept = slots * 2 // 5
    kept += (slots - kept) % 2
    rest = slots - kept
    sizes = split(kept, 4)
    col_hot, col_hot_t, same, leads, target, mine, whole, whole_t = pl.pallas_call(
        functools.partial(hot_kernel, sizes),
        name="hot",
        out_shape=(
            half(slots, beam_blocks),
            half(beam_blocks, slots),
            half(slots, slots),
            half(row_blocks, slots),
            dense(slots, side),
            dense(*fluence.shape),
            pltpu.VMEM((scen, kept, side, side), F32),
            pltpu.VMEM((scen, kept, side, side), F32),
        ),
        in_specs=[FAR] * 3 + [VMEM, FAR],
        out_specs=(VMEM,) * 8,
        scratch_shapes=[
            pltpu.VMEM((2, slots), jnp.int32),
            pltpu.VMEM((row_blocks, side), F32),
            pltpu.SemaphoreType.DMA((3 + len(sizes),)),
        ],
        compiler_params=params,
        cost_estimate=pl.CostEstimate(flops=0, bytes_accessed=3 * passes, transcendentals=0),
    )(
        far(block_map.T),
        far(fluence),
        far(target.reshape(row_blocks, side)),
        block_counts.reshape(1, 1),
        far(dose_blocks),
    )

    neighbours = min(4, parts)
    order = fluence
    found = [mine] + [swap_both(fluence, n) for n in range(1, neighbours)]
    fluence = pl.pallas_call(
        collect_kernel,
        name="collect",
        out_shape=dense(neighbours * mine.shape[0], side),
        in_specs=[VMEM] * neighbours,
        out_specs=VMEM,
        compiler_params=params,
    )(*found)
    for bit in bits("vox"):
        if bit < neighbours:
            continue
        other = swap_both(fluence, bit)
        order = fluence
        fluence = pl.pallas_call(
            functools.partial(join_kernel, bit),
            name="join",
            out_shape=dense(2 * fluence.shape[0], side),
            in_specs=[VMEM] * 2,
            out_specs=VMEM,
            compiler_params=params,
        )(fluence, other)
    sizes = split(rest, 6)
    upper, upper_t, lower, lower_t = pl.pallas_call(
        functools.partial(split_kernel, sizes),
        name="split",
        out_shape=(pltpu.VMEM((scen, rest, 2 * side, side), BF16),) * 2
        + (pltpu.VMEM((scen, rest // 2, 2 * side, side), BF16),) * 2,
        in_specs=[FAR, VMEM],
        out_specs=(VMEM,) * 4,
        scratch_shapes=[
            pltpu.VMEM((scen, rest, side, side), F32),
            pltpu.SemaphoreType.DMA((len(sizes),)),
        ],
        compiler_params=params,
        cost_estimate=pl.CostEstimate(flops=0, bytes_accessed=5 * passes, transcendentals=0),
    )(far(dose_blocks), order)
    blocks = [near(x) for x in (whole, upper, lower)]
    flipped = [near(x) for x in (whole_t, upper_t, lower_t)]

    for outer_round in range(ROUNDS):
        last = outer_round == ROUNDS - 1
        *excess, score_sum = pl.pallas_call(
            first_kernel,
            name="first",
            out_shape=(dense(slots, side),) * (scen + 1),
            in_specs=[VMEM] * 7,
            out_specs=(VMEM,) * (scen + 1),
            scratch_shapes=[pltpu.VMEM((scen, slots, side), F32)],
            compiler_params=params,
        )(*flipped, fluence, target, col_hot, same)
        score_sums = spread_scen(score_sum)

        groups = [[s] for s in range(scen)] if last else [list(range(scen))]
        weights, gradients, order = [], [], score_sum
        for group in groups:
            n = len(group)
            found = pl.pallas_call(
                functools.partial(second_kernel, group),
                name="second",
                out_shape=(dense(slots, side),) * n + (dense(beam_blocks, side),) * n,
                in_specs=[VMEM] * (5 + len(score_sums) + n),
                out_specs=(VMEM,) * (2 * n),
                scratch_shapes=[pltpu.VMEM((n, slots, side), F32)],
                compiler_params=params,
            )(*blocks, col_hot_t, order, *score_sums, *[excess[s] for s in group])
            order = found[-1]
            weights += found[:n]
            gradients += found[n:]
        sums = [reduce_vox(gradient) for gradient in gradients]
        copies, gradients = [], []
        for group in groups:
            n = len(group)
            together = last and group is groups[-1]
            others = gradients if together else []
            form = [(parts, scen, share // side, side)] if together else [(beam_blocks, side)] * n
            found = pl.pallas_call(
                functools.partial(third_kernel, group),
                name="third",
                out_shape=(dense(share // side if last else beam_blocks, side),) * n
                + tuple(dense(*shape) for shape in form),
                in_specs=[VMEM] * (11 + 3 * n + len(others)),
                out_specs=(VMEM,) * (n + len(form)),
                scratch_shapes=[
                    pltpu.VMEM((n, slots, side), F32),
                    pltpu.VMEM((n, beam_blocks, side), F32),
                ],
                compiler_params=params,
            )(
                *blocks, *flipped, fluence, target, col_hot, col_hot_t, same,
                *[sums[s][0] for s in group], *[sums[s][1] for s in group],
                *[weights[s] for s in group], *others,
            )
            copies += found[:n]
            gradients += found[n:]
        if not last:
            sums = [reduce_vox(gradient) for gradient in gradients]
            gradients = [a + b for a, b in sums]
        else:
            gradient, copies = lax.optimization_barrier((gradients[-1], copies))
            gradient = lax.all_to_all(gradient, "vox", split_axis=0, concat_axis=0, tiled=True)
            gradient = jnp.sum(gradient, axis=0)
            gradients = [gradient[s] for s in range(scen)]
        copies = [jnp.maximum(c - STEP_SIZE * g, 0.0) for c, g in zip(copies, gradients)]
        total = functools.reduce(jnp.add, copies)
        totals = spread_scen(total)
        if last:
            placed = pl.pallas_call(
                functools.partial(place_kernel, scen_total),
                name="place",
                out_shape=dense(row_blocks, scen, side),
                in_specs=[VMEM] * (2 + scen),
                out_specs=VMEM,
                compiler_params=params,
                cost_estimate=pl.CostEstimate(
                    flops=0, bytes_accessed=8 * scen * row_blocks * side, transcendentals=0
                ),
            )(leads, total, *weights)
            weights = jnp.swapaxes(placed, 0, 1).reshape(scen, row_blocks * side)
        fluence = functools.reduce(jnp.add, totals) / scen_total
    return fluence.reshape(share), weights


def solution(mesh):
    placed = (P("scen", "vox", None, None), P("vox", None), P("vox"), P("vox"), P("vox"))
    return jax.shard_map(
        body, mesh=mesh, in_specs=placed, out_specs=(P("vox"), P("scen", "vox")), check_vma=False
    )
```

```python
import functools

import jax
import jax.numpy as jnp
from jax import lax
from jax.experimental import pallas as pl
from jax.experimental.pallas import tpu as pltpu
from jax.sharding import PartitionSpec as P

ROUNDS = 2
SHARPNESS = 2.0
STEP_SIZE = 0.5
F32 = jnp.float32
BF16 = jnp.bfloat16
VMEM = pl.BlockSpec(memory_space=pltpu.VMEM)
FAR = pl.BlockSpec(memory_space=pltpu.HBM)


def exact(hot, xs):
    n = xs[0].shape[1]
    every = jnp.concatenate([y for x in xs for y in pieces(x)], axis=1)
    y = jnp.dot(hot, every, preferred_element_type=F32)
    parts = [y[:, m * n : (m + 1) * n] for m in range(3 * len(xs))]
    return [parts[m] + parts[m + 1] + parts[m + 2] for m in range(0, len(parts), 3)]


def columns(x):
    pad = -x.shape[0] % 128
    if pad:
        x = jnp.concatenate([x, jnp.zeros((pad, x.shape[1]), x.dtype)], axis=0)
    return x.T


def flat(x):
    pad = -x.shape[1] % 128
    slots = x.shape[1]
    if pad:
        x = jnp.concatenate([x, jnp.zeros((x.shape[0], pad), x.dtype)], axis=1)
    return x.T[:slots]


def pieces(x):
    high = x.astype(BF16)
    rest = x - high.astype(F32)
    mid = rest.astype(BF16)
    return high, mid, (rest - mid.astype(F32)).astype(BF16)


def products(whole, upper, lower, picked, rows):
    _, kept, side, _ = whole.shape
    pairs = lower.shape[1]
    turned, parts = {}, {}
    for _, x in picked:
        if id(x) not in turned:
            turned[id(x)] = columns(x[:kept])
            parts[id(x)] = [y.astype(F32) for y in pieces(x)]
    sub = lax.broadcasted_iota(jnp.int32, (16, side), 0)

    def on_vector_unit(k):
        wide = {}
        for n, (s, x) in enumerate(picked):
            if id(x) not in wide:
                wide[id(x)] = jnp.broadcast_to(turned[id(x)][:, k : k + 1], (side, side))
            rows[n, k : k + 1, :] = jnp.sum(whole[s, k] * wide[id(x)], axis=0, keepdims=True)

    def on_matrix_unit(m):
        left = {}
        for n, (s, x) in enumerate(picked):
            if id(x) not in left:
                stacks, firsts = [], []
                for u in range(2):
                    k = kept + 2 * m + u
                    high, mid, low = [y[k : k + 1, :] for y in parts[id(x)]]
                    stack = jnp.where(sub == 1, mid, jnp.where(sub == 2, low, 0.0))
                    stack = jnp.where(sub == 0, high, stack).astype(BF16)
                    stacks.append(jnp.concatenate([stack] * 2, axis=1))
                    firsts.append(jnp.where(sub == 8 * u, high, 0.0).astype(BF16))
                left[id(x)] = stacks, jnp.concatenate(firsts, axis=1)
            stacks, firsts = left[id(x)]
            rest = jnp.dot(firsts, lower[s, m], preferred_element_type=F32)
            for u in range(2):
                k = kept + 2 * m + u
                main = jnp.dot(stacks[u], upper[s, 2 * m + u], preferred_element_type=F32)
                total = main[:8] + rest[8 * u : 8 * u + 8]
                rows[n, k : k + 1, :] = jnp.sum(total, axis=0, keepdims=True)

    order = [((k + 0.5) / kept, on_vector_unit, k) for k in range(kept)]
    order += [((m + 0.5) / pairs, on_matrix_unit, m) for m in range(pairs)]
    for _, work, k in sorted(order, key=lambda entry: entry[0]):
        work(k)


def log_sum_exp(xs):
    top = functools.reduce(jnp.maximum, xs)
    return top + jnp.log(functools.reduce(jnp.add, [jnp.exp(x - top) for x in xs]))


def bring(source, first, sizes, to, sems):
    copies, done = [], 0
    for n, size in enumerate(sizes):
        copy = pltpu.make_async_copy(
            source.at[:, pl.ds(first + done, size)], to.at[:, pl.ds(done, size)], sems.at[n]
        )
        copy.start()
        copies.append((copy, range(done, done + size)))
        done += size
    yield range(0)
    for copy, slots in copies:
        copy.wait()
        yield slots


def split_kernel(sizes, source, order, upper, upper_t, lower, lower_t, held, sems):
    del order
    scen, slots, side, _ = source.shape
    for ready in bring(source, slots - held.shape[1], sizes, held, sems):
        for k in ready:
            for s in range(scen):
                block = held[s, k]
                for x, up, low in ((block, upper, lower), (block.T, upper_t, lower_t)):
                    high, mid, rest = pieces(x)
                    up[s, k, :side] = high
                    up[s, k, side:] = mid
                    low[s, k // 2, k % 2 * side : (k % 2 + 1) * side] = rest


def hot_kernel(
    sizes, map_far, fluence, target_far, counts, source,
    col_hot, col_hot_t, same, leads, target, mine, whole, whole_t, block_map, target_rows, sems
):
    copies = [
        pltpu.make_async_copy(x, y, sems.at[n])
        for n, (x, y) in enumerate(
            [(map_far, block_map), (fluence, mine), (target_far, target_rows)]
        )
    ]
    for copy in copies:
        copy.start()
    brought = bring(source, 0, sizes, whole, sems.at[pl.ds(len(copies), len(sizes))])
    next(brought)
    for copy in copies:
        copy.wait()
    row_blocks, slots = leads.shape
    usable = lax.broadcasted_iota(jnp.int32, (row_blocks, slots), 1) < counts[...]
    rows = lax.broadcasted_iota(jnp.int32, (row_blocks, slots), 0) == block_map[0:1, :]
    row = jnp.where(rows & usable, 1.0, 0.0).astype(F32)
    beam_blocks = col_hot_t.shape[0]
    cols = lax.broadcasted_iota(jnp.int32, (beam_blocks, slots), 0) == block_map[1:2, :]
    col = jnp.where(cols, 1.0, 0.0).astype(F32)
    col_hot_t[...] = col.astype(BF16)
    col_hot[...] = flat(col).astype(BF16)
    row_hot = flat(row).astype(BF16)
    shared = jnp.dot(row_hot, row.astype(BF16), preferred_element_type=F32)
    same[...] = shared.astype(BF16)
    before = lax.broadcasted_iota(jnp.int32, (slots, slots), 0) < lax.broadcasted_iota(
        jnp.int32, (slots, slots), 1
    )
    earlier = jnp.sum(jnp.where(before, shared, 0.0), axis=0, keepdims=True)
    leads[...] = jnp.where(earlier == 0.0, row, 0.0).astype(BF16)
    target[...] = exact(row_hot, [target_rows[...]])[0]
    for ready in brought:
        for k in ready:
            for s in range(source.shape[0]):
                whole_t[s, k] = whole[s, k].T


def join_kernel(bit, mine, other, joined):
    size = mine.shape[0]
    low = lax.axis_index("vox") & bit == 0
    joined[:size] = jnp.where(low, mine[...], other[...])
    joined[size:] = jnp.where(low, other[...], mine[...])


def collect_kernel(*refs):
    *found, collected = refs
    count, size = len(found), found[0].shape[0]
    here = lax.axis_index("vox") & (count - 1)
    for offset, piece in enumerate(found):
        at = pl.multiple_of((here ^ offset) * size, size)
        collected[pl.ds(at, size)] = piece[...]


def first_kernel(whole, upper, lower, fluence, target, col_hot, same, *refs):
    *excess, score_sum, rows = refs
    scen = len(excess)
    picked = exact(col_hot[...], [fluence[...]])[0]
    products(whole, upper, lower, [(s, picked) for s in range(scen)], rows)
    scores = []
    for s, dose in enumerate(exact(same[...], [rows[s] for s in range(scen)])):
        e = dose - target[...]
        excess[s][...] = e
        scores.append(SHARPNESS * e * e)
    score_sum[...] = log_sum_exp(scores)


def second_kernel(scens, whole, upper, lower, col_hot_t, order, *refs):
    del order
    *refs, rows = refs
    n = len(scens)
    sums, refs = refs[: -3 * n], refs[-3 * n :]
    excess, weights, gradient = refs[:n], refs[n : 2 * n], refs[2 * n :]
    total = log_sum_exp([x[...] for x in sums])
    picked = []
    for m, s in enumerate(scens):
        e = excess[m][...]
        w = jnp.exp(SHARPNESS * e * e - total)
        weights[m][...] = w
        picked.append((s, 2.0 * w * e))
    products(whole, upper, lower, picked, rows)
    for m, g in enumerate(exact(col_hot_t[...], [rows[m] for m in range(n)])):
        gradient[m][...] = g


def third_kernel(
    scens, whole, upper, lower, whole_t, upper_t, lower_t, fluence, target,
    col_hot, col_hot_t, same, *refs
):
    *refs, rows, held = refs
    n = len(scens)
    grad_a, grad_b, weights, refs = refs[:n], refs[n : 2 * n], refs[2 * n : 3 * n], refs[3 * n :]
    together = len(refs[-1].shape) == 4
    others = refs[: len(refs) - n - (1 if together else n)]
    copies = refs[len(others) : len(others) + n]
    gradient = refs[len(others) + n :]
    share = copies[0].shape[0]
    mine = pl.ds(0 if share == held.shape[1] else lax.axis_index("vox") * share, share)
    for m in range(n):
        step = STEP_SIZE * (grad_a[m][...] + grad_b[m][...])
        held[m] = jnp.maximum(fluence[...] - step, 0.0)
        copies[m][...] = held[m, mine]
    picked = exact(col_hot[...], [held[m] for m in range(n)])
    products(whole_t, upper_t, lower_t, list(zip(scens, picked)), rows)
    doses = exact(same[...], [rows[m] for m in range(n)])
    picked = [2.0 * weights[m][...] * (doses[m] - target[...]) for m in range(n)]
    products(whole, upper, lower, list(zip(scens, picked)), rows)
    found = exact(col_hot_t[...], [rows[m] for m in range(n)])
    if not together:
        for m, g in enumerate(found):
            gradient[m][...] = g
        return
    parts, _, *piece = gradient[0].shape
    for m, g in enumerate([*(x[...] for x in others), *found]):
        gradient[0][:, m] = g.reshape(parts, *piece)


def place_kernel(scen_total, leads, order, *refs):
    del order
    used = jnp.sum(leads[...].astype(F32), axis=1, keepdims=True)
    *weights, placed = refs
    for s, w in enumerate(exact(leads[...], [x[...] for x in weights])):
        placed[:, s] = jnp.where(used == 0.0, 1.0 / scen_total, w)


def near(x):
    return pltpu.with_memory_space_constraint(x, pltpu.VMEM)


def far(x):
    return pltpu.with_memory_space_constraint(x, pltpu.HBM)


def swap(x, axis, bit):
    return lax.ppermute(x, axis, [(i, i ^ bit) for i in range(lax.axis_size(axis))])


def bits(axis):
    size = lax.axis_size(axis)
    if size & (size - 1) or size < 2:
        raise ValueError("axis size")
    return [1 << b for b in range(size.bit_length() - 1)]


def reduce_vox(x):
    steps = bits("vox")
    orders = [steps, steps]
    if len(steps) > 2:
        first, far, *between = steps[0], steps[-1], *steps[1:-1]
        orders = [[far, first, *between], [first, far, *between]]
    other = None
    for pair in zip(*orders):
        if other is not None:
            x = x + other
        other = lax.ppermute(
            x,
            "vox",
            [(v, v ^ pair[(v & steps[-2]) // steps[-2]]) for v in range(lax.axis_size("vox"))],
        )
    return x, other


def reduce_scen(x, combine):
    steps = bits("scen")
    x = [x, swap(x, "scen", steps[0])]
    for bit in steps[1:]:
        both = combine(x)
        x = [both, swap(both, "scen", bit ^ 1)]
    return x


def spread_scen(x):
    return [x] + [swap(x, "scen", n) for n in range(1, lax.axis_size("scen"))]


def swap_both(x, bit):
    scen, vox = lax.axis_size("scen"), lax.axis_size("vox")
    pairs = [(s * vox + v, (s ^ 1) * vox + (v ^ bit)) for s in range(scen) for v in range(vox)]
    return lax.ppermute(x, ("scen", "vox"), pairs)


def split(total, parts):
    return [total * (n + 1) // parts - total * n // parts for n in range(parts)]


def body(dose_blocks, block_map, block_counts, target, fluence_init):
    scen, slots, side, _ = dose_blocks.shape
    share = fluence_init.shape[0]
    parts = lax.axis_size("vox")
    beam_blocks = share * parts // side
    row_blocks = target.shape[0] // side
    scen_total = scen * lax.axis_size("scen")
    params = pltpu.CompilerParams(vmem_limit_bytes=16 * 2**20)
    passes = scen * slots * side * side
    dense = lambda *shape: jax.ShapeDtypeStruct(shape, F32)

    fluence = fluence_init.reshape(share // side, side)
    half = lambda *shape: jax.ShapeDtypeStruct(shape, BF16)
    kept = slots * 2 // 5
    kept += (slots - kept) % 2
    rest = slots - kept
    sizes = split(kept, 4)
    col_hot, col_hot_t, same, leads, target, mine, whole, whole_t = pl.pallas_call(
        functools.partial(hot_kernel, sizes),
        name="hot",
        out_shape=(
            half(slots, beam_blocks),
            half(beam_blocks, slots),
            half(slots, slots),
            half(row_blocks, slots),
            dense(slots, side),
            dense(*fluence.shape),
            pltpu.VMEM((scen, kept, side, side), F32),
            pltpu.VMEM((scen, kept, side, side), F32),
        ),
        in_specs=[FAR] * 3 + [VMEM, FAR],
        out_specs=(VMEM,) * 8,
        scratch_shapes=[
            pltpu.VMEM((2, slots), jnp.int32),
            pltpu.VMEM((row_blocks, side), F32),
            pltpu.SemaphoreType.DMA((3 + len(sizes),)),
        ],
        compiler_params=params,
        cost_estimate=pl.CostEstimate(flops=0, bytes_accessed=3 * passes, transcendentals=0),
    )(
        far(block_map.T),
        far(fluence),
        far(target.reshape(row_blocks, side)),
        block_counts.reshape(1, 1),
        far(dose_blocks),
    )

    neighbours = min(4, parts)
    order = fluence
    found = [mine] + [swap_both(fluence, n) for n in range(1, neighbours)]
    fluence = pl.pallas_call(
        collect_kernel,
        name="collect",
        out_shape=dense(neighbours * mine.shape[0], side),
        in_specs=[VMEM] * neighbours,
        out_specs=VMEM,
        compiler_params=params,
    )(*found)
    for bit in bits("vox"):
        if bit < neighbours:
            continue
        other = swap_both(fluence, bit)
        order = fluence
        fluence = pl.pallas_call(
            functools.partial(join_kernel, bit),
            name="join",
            out_shape=dense(2 * fluence.shape[0], side),
            in_specs=[VMEM] * 2,
            out_specs=VMEM,
            compiler_params=params,
        )(fluence, other)
    sizes = split(rest, 6)
    upper, upper_t, lower, lower_t = pl.pallas_call(
        functools.partial(split_kernel, sizes),
        name="split",
        out_shape=(pltpu.VMEM((scen, rest, 2 * side, side), BF16),) * 2
        + (pltpu.VMEM((scen, rest // 2, 2 * side, side), BF16),) * 2,
        in_specs=[FAR, VMEM],
        out_specs=(VMEM,) * 4,
        scratch_shapes=[
            pltpu.VMEM((scen, rest, side, side), F32),
            pltpu.SemaphoreType.DMA((len(sizes),)),
        ],
        compiler_params=params,
        cost_estimate=pl.CostEstimate(flops=0, bytes_accessed=5 * passes, transcendentals=0),
    )(far(dose_blocks), order)
    blocks = [near(x) for x in (whole, upper, lower)]
    flipped = [near(x) for x in (whole_t, upper_t, lower_t)]

    for outer_round in range(ROUNDS):
        last = outer_round == ROUNDS - 1
        *excess, score_sum = pl.pallas_call(
            first_kernel,
            name="first",
            out_shape=(dense(slots, side),) * (scen + 1),
            in_specs=[VMEM] * 7,
            out_specs=(VMEM,) * (scen + 1),
            scratch_shapes=[pltpu.VMEM((scen, slots, side), F32)],
            compiler_params=params,
        )(*flipped, fluence, target, col_hot, same)
        score_sums = spread_scen(score_sum)

        groups = [[s] for s in range(scen)] if last else [list(range(scen))]
        weights, gradients, order = [], [], score_sum
        for group in groups:
            n = len(group)
            found = pl.pallas_call(
                functools.partial(second_kernel, group),
                name="second",
                out_shape=(dense(slots, side),) * n + (dense(beam_blocks, side),) * n,
                in_specs=[VMEM] * (5 + len(score_sums) + n),
                out_specs=(VMEM,) * (2 * n),
                scratch_shapes=[pltpu.VMEM((n, slots, side), F32)],
                compiler_params=params,
            )(*blocks, col_hot_t, order, *score_sums, *[excess[s] for s in group])
            order = found[-1]
            weights += found[:n]
            gradients += found[n:]
        sums = [reduce_vox(gradient) for gradient in gradients]
        groups = [[s] for s in range(scen)]
        copies, gradients = [], []
        for group in groups:
            n = len(group)
            together = last and group is groups[-1]
            others = gradients if together else []
            form = [(parts, scen, share // side, side)] if together else [(beam_blocks, side)] * n
            found = pl.pallas_call(
                functools.partial(third_kernel, group),
                name="third",
                out_shape=(dense(share // side if last else beam_blocks, side),) * n
                + tuple(dense(*shape) for shape in form),
                in_specs=[VMEM] * (11 + 3 * n + len(others)),
                out_specs=(VMEM,) * (n + len(form)),
                scratch_shapes=[
                    pltpu.VMEM((n, slots, side), F32),
                    pltpu.VMEM((n, beam_blocks, side), F32),
                ],
                compiler_params=params,
            )(
                *blocks, *flipped, fluence, target, col_hot, col_hot_t, same,
                *[sums[s][0] for s in group], *[sums[s][1] for s in group],
                *[weights[s] for s in group], *others,
            )
            copies += found[:n]
            gradients += found[n:]
        if not last:
            sums = [reduce_vox(gradient) for gradient in gradients]
            gradients = [a + b for a, b in sums]
        else:
            gradient, copies = lax.optimization_barrier((gradients[-1], copies))
            gradient = lax.all_to_all(gradient, "vox", split_axis=0, concat_axis=0, tiled=True)
            gradient = jnp.sum(gradient, axis=0)
            gradients = [gradient[s] for s in range(scen)]
        copies = [jnp.maximum(c - STEP_SIZE * g, 0.0) for c, g in zip(copies, gradients)]
        total = functools.reduce(jnp.add, copies)
        totals = spread_scen(total) if last else reduce_scen(total, sum)
        if last:
            placed = pl.pallas_call(
                functools.partial(place_kernel, scen_total),
                name="place",
                out_shape=dense(row_blocks, scen, side),
                in_specs=[VMEM] * (2 + scen),
                out_specs=VMEM,
                compiler_params=params,
                cost_estimate=pl.CostEstimate(
                    flops=0, bytes_accessed=8 * scen * row_blocks * side, transcendentals=0
                ),
            )(leads, total, *weights)
            weights = jnp.swapaxes(placed, 0, 1).reshape(scen, row_blocks * side)
        fluence = functools.reduce(jnp.add, totals) / scen_total
    return fluence.reshape(share), weights


def solution(mesh):
    placed = (P("scen", "vox", None, None), P("vox", None), P("vox"), P("vox"), P("vox"))
    return jax.shard_map(
        body, mesh=mesh, in_specs=placed, out_specs=(P("vox"), P("scen", "vox")), check_vma=False
    )
```

```python
import functools

import jax
import jax.numpy as jnp
from jax import lax
from jax.experimental import pallas as pl
from jax.experimental.pallas import tpu as pltpu
from jax.sharding import PartitionSpec as P

ROUNDS = 2
SHARPNESS = 2.0
STEP_SIZE = 0.5
F32 = jnp.float32
BF16 = jnp.bfloat16
VMEM = pl.BlockSpec(memory_space=pltpu.VMEM)
FAR = pl.BlockSpec(memory_space=pltpu.HBM)


def exact(hot, xs):
    n = xs[0].shape[1]
    every = jnp.concatenate([y for x in xs for y in pieces(x)], axis=1)
    y = jnp.dot(hot, every, preferred_element_type=F32)
    parts = [y[:, m * n : (m + 1) * n] for m in range(3 * len(xs))]
    return [parts[m] + parts[m + 1] + parts[m + 2] for m in range(0, len(parts), 3)]


def columns(x):
    pad = -x.shape[0] % 128
    if pad:
        x = jnp.concatenate([x, jnp.zeros((pad, x.shape[1]), x.dtype)], axis=0)
    return x.T


def flat(x):
    pad = -x.shape[1] % 128
    slots = x.shape[1]
    if pad:
        x = jnp.concatenate([x, jnp.zeros((x.shape[0], pad), x.dtype)], axis=1)
    return x.T[:slots]


def pieces(x):
    high = x.astype(BF16)
    rest = x - high.astype(F32)
    mid = rest.astype(BF16)
    return high, mid, (rest - mid.astype(F32)).astype(BF16)


def products(whole, upper, lower, picked, rows):
    _, kept, side, _ = whole.shape
    pairs = lower.shape[1]
    turned, parts = {}, {}
    for _, x in picked:
        if id(x) not in turned:
            turned[id(x)] = columns(x[:kept])
            parts[id(x)] = [y.astype(F32) for y in pieces(x)]
    sub = lax.broadcasted_iota(jnp.int32, (16, side), 0)

    def on_vector_unit(k):
        wide = {}
        for n, (s, x) in enumerate(picked):
            if id(x) not in wide:
                wide[id(x)] = jnp.broadcast_to(turned[id(x)][:, k : k + 1], (side, side))
            rows[n, k : k + 1, :] = jnp.sum(whole[s, k] * wide[id(x)], axis=0, keepdims=True)

    def on_matrix_unit(m):
        left = {}
        for n, (s, x) in enumerate(picked):
            if id(x) not in left:
                stacks, firsts = [], []
                for u in range(2):
                    k = kept + 2 * m + u
                    high, mid, low = [y[k : k + 1, :] for y in parts[id(x)]]
                    stack = jnp.where(sub == 1, mid, jnp.where(sub == 2, low, 0.0))
                    stack = jnp.where(sub == 0, high, stack).astype(BF16)
                    stacks.append(jnp.concatenate([stack] * 2, axis=1))
                    firsts.append(jnp.where(sub == 8 * u, high, 0.0).astype(BF16))
                left[id(x)] = stacks, jnp.concatenate(firsts, axis=1)
            stacks, firsts = left[id(x)]
            rest = jnp.dot(firsts, lower[s, m], preferred_element_type=F32)
            for u in range(2):
                k = kept + 2 * m + u
                main = jnp.dot(stacks[u], upper[s, 2 * m + u], preferred_element_type=F32)
                total = main[:8] + rest[8 * u : 8 * u + 8]
                rows[n, k : k + 1, :] = jnp.sum(total, axis=0, keepdims=True)

    order = [((k + 0.5) / kept, on_vector_unit, k) for k in range(kept)]
    order += [((m + 0.5) / pairs, on_matrix_unit, m) for m in range(pairs)]
    for _, work, k in sorted(order, key=lambda entry: entry[0]):
        work(k)


def log_sum_exp(xs):
    top = functools.reduce(jnp.maximum, xs)
    return top + jnp.log(functools.reduce(jnp.add, [jnp.exp(x - top) for x in xs]))


def bring(source, first, sizes, to, sems):
    copies, done = [], 0
    for n, size in enumerate(sizes):
        copy = pltpu.make_async_copy(
            source.at[:, pl.ds(first + done, size)], to.at[:, pl.ds(done, size)], sems.at[n]
        )
        copy.start()
        copies.append((copy, range(done, done + size)))
        done += size
    yield range(0)
    for copy, slots in copies:
        copy.wait()
        yield slots


def split_kernel(sizes, source, order, upper, upper_t, lower, lower_t, held, sems):
    del order
    scen, slots, side, _ = source.shape
    for ready in bring(source, slots - held.shape[1], sizes, held, sems):
        for k in ready:
            for s in range(scen):
                block = held[s, k]
                for x, up, low in ((block, upper, lower), (block.T, upper_t, lower_t)):
                    high, mid, rest = pieces(x)
                    up[s, k, :side] = high
                    up[s, k, side:] = mid
                    low[s, k // 2, k % 2 * side : (k % 2 + 1) * side] = rest


def hot_kernel(
    sizes, map_far, fluence, target_far, counts, source,
    col_hot, col_hot_t, same, leads, target, mine, whole, whole_t, block_map, target_rows, sems
):
    copies = [
        pltpu.make_async_copy(x, y, sems.at[n])
        for n, (x, y) in enumerate(
            [(map_far, block_map), (fluence, mine), (target_far, target_rows)]
        )
    ]
    for copy in copies:
        copy.start()
    brought = bring(source, 0, sizes, whole, sems.at[pl.ds(len(copies), len(sizes))])
    next(brought)
    for copy in copies:
        copy.wait()
    row_blocks, slots = leads.shape
    usable = lax.broadcasted_iota(jnp.int32, (row_blocks, slots), 1) < counts[...]
    rows = lax.broadcasted_iota(jnp.int32, (row_blocks, slots), 0) == block_map[0:1, :]
    row = jnp.where(rows & usable, 1.0, 0.0).astype(F32)
    beam_blocks = col_hot_t.shape[0]
    cols = lax.broadcasted_iota(jnp.int32, (beam_blocks, slots), 0) == block_map[1:2, :]
    col = jnp.where(cols, 1.0, 0.0).astype(F32)
    col_hot_t[...] = col.astype(BF16)
    col_hot[...] = flat(col).astype(BF16)
    row_hot = flat(row).astype(BF16)
    shared = jnp.dot(row_hot, row.astype(BF16), preferred_element_type=F32)
    same[...] = shared.astype(BF16)
    before = lax.broadcasted_iota(jnp.int32, (slots, slots), 0) < lax.broadcasted_iota(
        jnp.int32, (slots, slots), 1
    )
    earlier = jnp.sum(jnp.where(before, shared, 0.0), axis=0, keepdims=True)
    leads[...] = jnp.where(earlier == 0.0, row, 0.0).astype(BF16)
    target[...] = exact(row_hot, [target_rows[...]])[0]
    for ready in brought:
        for k in ready:
            for s in range(source.shape[0]):
                whole_t[s, k] = whole[s, k].T


def join_kernel(bit, mine, other, joined):
    size = mine.shape[0]
    low = lax.axis_index("vox") & bit == 0
    joined[:size] = jnp.where(low, mine[...], other[...])
    joined[size:] = jnp.where(low, other[...], mine[...])


def collect_kernel(*refs):
    *found, collected = refs
    count, size = len(found), found[0].shape[0]
    here = lax.axis_index("vox") & (count - 1)
    for offset, piece in enumerate(found):
        at = pl.multiple_of((here ^ offset) * size, size)
        collected[pl.ds(at, size)] = piece[...]


def first_kernel(whole, upper, lower, fluence, target, col_hot, same, *refs):
    *excess, score_sum, rows = refs
    scen = len(excess)
    picked = exact(col_hot[...], [fluence[...]])[0]
    products(whole, upper, lower, [(s, picked) for s in range(scen)], rows)
    scores = []
    for s, dose in enumerate(exact(same[...], [rows[s] for s in range(scen)])):
        e = dose - target[...]
        excess[s][...] = e
        scores.append(SHARPNESS * e * e)
    score_sum[...] = log_sum_exp(scores)


def second_kernel(scens, whole, upper, lower, col_hot_t, order, *refs):
    del order
    *refs, rows = refs
    n = len(scens)
    sums, refs = refs[: -3 * n], refs[-3 * n :]
    excess, weights, gradient = refs[:n], refs[n : 2 * n], refs[2 * n :]
    total = log_sum_exp([x[...] for x in sums])
    picked = []
    for m, s in enumerate(scens):
        e = excess[m][...]
        w = jnp.exp(SHARPNESS * e * e - total)
        weights[m][...] = w
        picked.append((s, 2.0 * w * e))
    products(whole, upper, lower, picked, rows)
    for m, g in enumerate(exact(col_hot_t[...], [rows[m] for m in range(n)])):
        gradient[m][...] = g


def third_kernel(
    scens, whole, upper, lower, whole_t, upper_t, lower_t, fluence, target,
    col_hot, col_hot_t, same, *refs
):
    *refs, rows, held = refs
    n = len(scens)
    grad_a, grad_b, weights, refs = refs[:n], refs[n : 2 * n], refs[2 * n : 3 * n], refs[3 * n :]
    together = len(refs[-1].shape) == 4
    others = refs[: len(refs) - n - (1 if together else n)]
    copies = refs[len(others) : len(others) + n]
    gradient = refs[len(others) + n :]
    share = copies[0].shape[0]
    mine = pl.ds(0 if share == held.shape[1] else lax.axis_index("vox") * share, share)
    for m in range(n):
        step = STEP_SIZE * (grad_a[m][...] + grad_b[m][...])
        held[m] = jnp.maximum(fluence[...] - step, 0.0)
        copies[m][...] = held[m, mine]
    picked = exact(col_hot[...], [held[m] for m in range(n)])
    products(whole_t, upper_t, lower_t, list(zip(scens, picked)), rows)
    doses = exact(same[...], [rows[m] for m in range(n)])
    picked = [2.0 * weights[m][...] * (doses[m] - target[...]) for m in range(n)]
    products(whole, upper, lower, list(zip(scens, picked)), rows)
    found = exact(col_hot_t[...], [rows[m] for m in range(n)])
    if not together:
        for m, g in enumerate(found):
            gradient[m][...] = g
        return
    parts, _, *piece = gradient[0].shape
    for m, g in enumerate([*(x[...] for x in others), *found]):
        gradient[0][:, m] = g.reshape(parts, *piece)


def place_kernel(scen_total, leads, order, *refs):
    del order
    used = jnp.sum(leads[...].astype(F32), axis=1, keepdims=True)
    *weights, placed = refs
    for s, w in enumerate(exact(leads[...], [x[...] for x in weights])):
        placed[:, s] = jnp.where(used == 0.0, 1.0 / scen_total, w)


def near(x):
    return pltpu.with_memory_space_constraint(x, pltpu.VMEM)


def far(x):
    return pltpu.with_memory_space_constraint(x, pltpu.HBM)


def swap(x, axis, bit):
    return lax.ppermute(x, axis, [(i, i ^ bit) for i in range(lax.axis_size(axis))])


def bits(axis):
    size = lax.axis_size(axis)
    if size & (size - 1) or size < 2:
        raise ValueError("axis size")
    return [1 << b for b in range(size.bit_length() - 1)]


def reduce_vox(x):
    steps = bits("vox")
    orders = [steps, steps]
    if len(steps) > 2:
        first, far, *between = steps[0], steps[-1], *steps[1:-1]
        orders = [[far, first, *between], [first, far, *between]]
    other = None
    for pair in zip(*orders):
        if other is not None:
            x = x + other
        other = lax.ppermute(
            x,
            "vox",
            [(v, v ^ pair[(v & steps[-2]) // steps[-2]]) for v in range(lax.axis_size("vox"))],
        )
    return x, other


def reduce_scen(x, combine):
    steps = bits("scen")
    x = [x, swap(x, "scen", steps[0])]
    for bit in steps[1:]:
        both = combine(x)
        x = [both, swap(both, "scen", bit ^ 1)]
    return x


def spread_scen(x):
    return [x] + [swap(x, "scen", n) for n in range(1, lax.axis_size("scen"))]


def swap_both(x, bit):
    scen, vox = lax.axis_size("scen"), lax.axis_size("vox")
    pairs = [(s * vox + v, (s ^ 1) * vox + (v ^ bit)) for s in range(scen) for v in range(vox)]
    return lax.ppermute(x, ("scen", "vox"), pairs)


def split(total, parts):
    return [total * (n + 1) // parts - total * n // parts for n in range(parts)]


def body(dose_blocks, block_map, block_counts, target, fluence_init):
    scen, slots, side, _ = dose_blocks.shape
    share = fluence_init.shape[0]
    parts = lax.axis_size("vox")
    beam_blocks = share * parts // side
    row_blocks = target.shape[0] // side
    scen_total = scen * lax.axis_size("scen")
    params = pltpu.CompilerParams(vmem_limit_bytes=16 * 2**20)
    passes = scen * slots * side * side
    dense = lambda *shape: jax.ShapeDtypeStruct(shape, F32)

    fluence = fluence_init.reshape(share // side, side)
    half = lambda *shape: jax.ShapeDtypeStruct(shape, BF16)
    kept = slots * 2 // 5
    kept += (slots - kept) % 2
    rest = slots - kept
    sizes = split(kept, 4)
    col_hot, col_hot_t, same, leads, target, mine, whole, whole_t = pl.pallas_call(
        functools.partial(hot_kernel, sizes),
        name="hot",
        out_shape=(
            half(slots, beam_blocks),
            half(beam_blocks, slots),
            half(slots, slots),
            half(row_blocks, slots),
            dense(slots, side),
            dense(*fluence.shape),
            pltpu.VMEM((scen, kept, side, side), F32),
            pltpu.VMEM((scen, kept, side, side), F32),
        ),
        in_specs=[FAR] * 3 + [VMEM, FAR],
        out_specs=(VMEM,) * 8,
        scratch_shapes=[
            pltpu.VMEM((2, slots), jnp.int32),
            pltpu.VMEM((row_blocks, side), F32),
            pltpu.SemaphoreType.DMA((3 + len(sizes),)),
        ],
        compiler_params=params,
        cost_estimate=pl.CostEstimate(flops=0, bytes_accessed=3 * passes, transcendentals=0),
    )(
        far(block_map.T),
        far(fluence),
        far(target.reshape(row_blocks, side)),
        block_counts.reshape(1, 1),
        far(dose_blocks),
    )

    neighbours = min(4, parts)
    order = fluence
    found = [mine] + [swap_both(fluence, n) for n in range(1, neighbours)]
    fluence = pl.pallas_call(
        collect_kernel,
        name="collect",
        out_shape=dense(neighbours * mine.shape[0], side),
        in_specs=[VMEM] * neighbours,
        out_specs=VMEM,
        compiler_params=params,
    )(*found)
    for bit in bits("vox"):
        if bit < neighbours:
            continue
        other = swap_both(fluence, bit)
        order = fluence
        fluence = pl.pallas_call(
            functools.partial(join_kernel, bit),
            name="join",
            out_shape=dense(2 * fluence.shape[0], side),
            in_specs=[VMEM] * 2,
            out_specs=VMEM,
            compiler_params=params,
        )(fluence, other)
    sizes = split(rest, 6)
    upper, upper_t, lower, lower_t = pl.pallas_call(
        functools.partial(split_kernel, sizes),
        name="split",
        out_shape=(pltpu.VMEM((scen, rest, 2 * side, side), BF16),) * 2
        + (pltpu.VMEM((scen, rest // 2, 2 * side, side), BF16),) * 2,
        in_specs=[FAR, VMEM],
        out_specs=(VMEM,) * 4,
        scratch_shapes=[
            pltpu.VMEM((scen, rest, side, side), F32),
            pltpu.SemaphoreType.DMA((len(sizes),)),
        ],
        compiler_params=params,
        cost_estimate=pl.CostEstimate(flops=0, bytes_accessed=5 * passes, transcendentals=0),
    )(far(dose_blocks), order)
    blocks = [near(x) for x in (whole, upper, lower)]
    flipped = [near(x) for x in (whole_t, upper_t, lower_t)]

    for outer_round in range(ROUNDS):
        last = outer_round == ROUNDS - 1
        *excess, score_sum = pl.pallas_call(
            first_kernel,
            name="first",
            out_shape=(dense(slots, side),) * (scen + 1),
            in_specs=[VMEM] * 7,
            out_specs=(VMEM,) * (scen + 1),
            scratch_shapes=[pltpu.VMEM((scen, slots, side), F32)],
            compiler_params=params,
        )(*flipped, fluence, target, col_hot, same)
        score_sums = spread_scen(score_sum) if last else reduce_scen(score_sum, log_sum_exp)

        groups = [[s] for s in range(scen)] if last else [list(range(scen))]
        weights, gradients, order = [], [], score_sum
        for group in groups:
            n = len(group)
            found = pl.pallas_call(
                functools.partial(second_kernel, group),
                name="second",
                out_shape=(dense(slots, side),) * n + (dense(beam_blocks, side),) * n,
                in_specs=[VMEM] * (5 + len(score_sums) + n),
                out_specs=(VMEM,) * (2 * n),
                scratch_shapes=[pltpu.VMEM((n, slots, side), F32)],
                compiler_params=params,
            )(*blocks, col_hot_t, order, *score_sums, *[excess[s] for s in group])
            order = found[-1]
            weights += found[:n]
            gradients += found[n:]
        sums = [reduce_vox(gradient) for gradient in gradients]
        groups = [[s] for s in range(scen)]
        copies, gradients = [], []
        for group in groups:
            n = len(group)
            together = last and group is groups[-1]
            others = gradients if together else []
            form = [(parts, scen, share // side, side)] if together else [(beam_blocks, side)] * n
            found = pl.pallas_call(
                functools.partial(third_kernel, group),
                name="third",
                out_shape=(dense(share // side if last else beam_blocks, side),) * n
                + tuple(dense(*shape) for shape in form),
                in_specs=[VMEM] * (11 + 3 * n + len(others)),
                out_specs=(VMEM,) * (n + len(form)),
                scratch_shapes=[
                    pltpu.VMEM((n, slots, side), F32),
                    pltpu.VMEM((n, beam_blocks, side), F32),
                ],
                compiler_params=params,
            )(
                *blocks, *flipped, fluence, target, col_hot, col_hot_t, same,
                *[sums[s][0] for s in group], *[sums[s][1] for s in group],
                *[weights[s] for s in group], *others,
            )
            copies += found[:n]
            gradients += found[n:]
        if not last:
            sums = [reduce_vox(gradient) for gradient in gradients]
            gradients = [a + b for a, b in sums]
        else:
            gradient, copies = lax.optimization_barrier((gradients[-1], copies))
            gradient = lax.all_to_all(gradient, "vox", split_axis=0, concat_axis=0, tiled=True)
            gradient = jnp.sum(gradient, axis=0)
            gradients = [gradient[s] for s in range(scen)]
        copies = [jnp.maximum(c - STEP_SIZE * g, 0.0) for c, g in zip(copies, gradients)]
        total = functools.reduce(jnp.add, copies)
        totals = spread_scen(total) if last else reduce_scen(total, sum)
        if last:
            placed = pl.pallas_call(
                functools.partial(place_kernel, scen_total),
                name="place",
                out_shape=dense(row_blocks, scen, side),
                in_specs=[VMEM] * (2 + scen),
                out_specs=VMEM,
                compiler_params=params,
                cost_estimate=pl.CostEstimate(
                    flops=0, bytes_accessed=8 * scen * row_blocks * side, transcendentals=0
                ),
            )(leads, total, *weights)
            weights = jnp.swapaxes(placed, 0, 1).reshape(scen, row_blocks * side)
        fluence = functools.reduce(jnp.add, totals) / scen_total
    return fluence.reshape(share), weights


def solution(mesh):
    placed = (P("scen", "vox", None, None), P("vox", None), P("vox"), P("vox"), P("vox"))
    return jax.shard_map(
        body, mesh=mesh, in_specs=placed, out_specs=(P("vox"), P("scen", "vox")), check_vma=False
    )
```

```python
import functools

import jax
import jax.numpy as jnp
from jax import lax
from jax.experimental import pallas as pl
from jax.experimental.pallas import tpu as pltpu
from jax.sharding import PartitionSpec as P

ROUNDS = 2
SHARPNESS = 2.0
STEP_SIZE = 0.5
F32 = jnp.float32
BF16 = jnp.bfloat16
VMEM = pl.BlockSpec(memory_space=pltpu.VMEM)
FAR = pl.BlockSpec(memory_space=pltpu.HBM)


def exact(hot, xs):
    n = xs[0].shape[1]
    every = jnp.concatenate([y for x in xs for y in pieces(x)], axis=1)
    y = jnp.dot(hot, every, preferred_element_type=F32)
    parts = [y[:, m * n : (m + 1) * n] for m in range(3 * len(xs))]
    return [parts[m] + parts[m + 1] + parts[m + 2] for m in range(0, len(parts), 3)]


def columns(x):
    pad = -x.shape[0] % 128
    if pad:
        x = jnp.concatenate([x, jnp.zeros((pad, x.shape[1]), x.dtype)], axis=0)
    return x.T


def flat(x):
    pad = -x.shape[1] % 128
    slots = x.shape[1]
    if pad:
        x = jnp.concatenate([x, jnp.zeros((x.shape[0], pad), x.dtype)], axis=1)
    return x.T[:slots]


def pieces(x):
    high = x.astype(BF16)
    rest = x - high.astype(F32)
    mid = rest.astype(BF16)
    return high, mid, (rest - mid.astype(F32)).astype(BF16)


def products(whole, upper, lower, picked, rows):
    _, kept, side, _ = whole.shape
    pairs = lower.shape[1]
    turned, parts = {}, {}
    for _, x in picked:
        if id(x) not in turned:
            turned[id(x)] = columns(x[:kept])
            parts[id(x)] = [y.astype(F32) for y in pieces(x)]
    sub = lax.broadcasted_iota(jnp.int32, (16, side), 0)

    def on_vector_unit(k):
        wide = {}
        for n, (s, x) in enumerate(picked):
            if id(x) not in wide:
                wide[id(x)] = jnp.broadcast_to(turned[id(x)][:, k : k + 1], (side, side))
            rows[n, k : k + 1, :] = jnp.sum(whole[s, k] * wide[id(x)], axis=0, keepdims=True)

    def on_matrix_unit(m):
        left = {}
        for n, (s, x) in enumerate(picked):
            if id(x) not in left:
                stacks, firsts = [], []
                for u in range(2):
                    k = kept + 2 * m + u
                    high, mid, low = [y[k : k + 1, :] for y in parts[id(x)]]
                    stack = jnp.where(sub == 1, mid, jnp.where(sub == 2, low, 0.0))
                    stack = jnp.where(sub == 0, high, stack).astype(BF16)
                    stacks.append(jnp.concatenate([stack] * 2, axis=1))
                    firsts.append(jnp.where(sub == 8 * u, high, 0.0).astype(BF16))
                left[id(x)] = stacks, jnp.concatenate(firsts, axis=1)
            stacks, firsts = left[id(x)]
            rest = jnp.dot(firsts, lower[s, m], preferred_element_type=F32)
            for u in range(2):
                k = kept + 2 * m + u
                main = jnp.dot(stacks[u], upper[s, 2 * m + u], preferred_element_type=F32)
                total = main[0:1] + rest[8 * u : 8 * u + 1]
                rows[n, k : k + 1, :] = total + main[1:2] + main[2:3]

    order = [((k + 0.5) / kept, on_vector_unit, k) for k in range(kept)]
    order += [((m + 0.5) / pairs, on_matrix_unit, m) for m in range(pairs)]
    for _, work, k in sorted(order, key=lambda entry: entry[0]):
        work(k)


def log_sum_exp(xs):
    top = functools.reduce(jnp.maximum, xs)
    return top + jnp.log(functools.reduce(jnp.add, [jnp.exp(x - top) for x in xs]))


def bring(source, first, sizes, to, sems):
    copies, done = [], 0
    for n, size in enumerate(sizes):
        copy = pltpu.make_async_copy(
            source.at[:, pl.ds(first + done, size)], to.at[:, pl.ds(done, size)], sems.at[n]
        )
        copy.start()
        copies.append((copy, range(done, done + size)))
        done += size
    yield range(0)
    for copy, slots in copies:
        copy.wait()
        yield slots


def split_kernel(sizes, source, order, upper, upper_t, lower, lower_t, held, sems):
    del order
    scen, slots, side, _ = source.shape
    for ready in bring(source, slots - held.shape[1], sizes, held, sems):
        for k in ready:
            for s in range(scen):
                block = held[s, k]
                for x, up, low in ((block, upper, lower), (block.T, upper_t, lower_t)):
                    high, mid, rest = pieces(x)
                    up[s, k, :side] = high
                    up[s, k, side:] = mid
                    low[s, k // 2, k % 2 * side : (k % 2 + 1) * side] = rest


def hot_kernel(
    sizes, map_far, fluence, target_far, counts, source,
    col_hot, col_hot_t, same, leads, target, mine, whole, whole_t, block_map, target_rows, sems
):
    copies = [
        pltpu.make_async_copy(x, y, sems.at[n])
        for n, (x, y) in enumerate(
            [(map_far, block_map), (fluence, mine), (target_far, target_rows)]
        )
    ]
    for copy in copies:
        copy.start()
    brought = bring(source, 0, sizes, whole, sems.at[pl.ds(len(copies), len(sizes))])
    next(brought)
    for copy in copies:
        copy.wait()
    row_blocks, slots = leads.shape
    usable = lax.broadcasted_iota(jnp.int32, (row_blocks, slots), 1) < counts[...]
    rows = lax.broadcasted_iota(jnp.int32, (row_blocks, slots), 0) == block_map[0:1, :]
    row = jnp.where(rows & usable, 1.0, 0.0).astype(F32)
    beam_blocks = col_hot_t.shape[0]
    cols = lax.broadcasted_iota(jnp.int32, (beam_blocks, slots), 0) == block_map[1:2, :]
    col = jnp.where(cols, 1.0, 0.0).astype(F32)
    col_hot_t[...] = col.astype(BF16)
    col_hot[...] = flat(col).astype(BF16)
    row_hot = flat(row).astype(BF16)
    shared = jnp.dot(row_hot, row.astype(BF16), preferred_element_type=F32)
    same[...] = shared.astype(BF16)
    before = lax.broadcasted_iota(jnp.int32, (slots, slots), 0) < lax.broadcasted_iota(
        jnp.int32, (slots, slots), 1
    )
    earlier = jnp.sum(jnp.where(before, shared, 0.0), axis=0, keepdims=True)
    leads[...] = jnp.where(earlier == 0.0, row, 0.0).astype(BF16)
    target[...] = exact(row_hot, [target_rows[...]])[0]
    for ready in brought:
        for k in ready:
            for s in range(source.shape[0]):
                whole_t[s, k] = whole[s, k].T


def join_kernel(bit, mine, other, joined):
    size = mine.shape[0]
    low = lax.axis_index("vox") & bit == 0
    joined[:size] = jnp.where(low, mine[...], other[...])
    joined[size:] = jnp.where(low, other[...], mine[...])


def collect_kernel(*refs):
    *found, collected = refs
    count, size = len(found), found[0].shape[0]
    here = lax.axis_index("vox") & (count - 1)
    for offset, piece in enumerate(found):
        at = pl.multiple_of((here ^ offset) * size, size)
        collected[pl.ds(at, size)] = piece[...]


def first_kernel(whole, upper, lower, fluence, target, col_hot, same, *refs):
    *excess, score_sum, rows = refs
    scen = len(excess)
    picked = exact(col_hot[...], [fluence[...]])[0]
    products(whole, upper, lower, [(s, picked) for s in range(scen)], rows)
    scores = []
    for s, dose in enumerate(exact(same[...], [rows[s] for s in range(scen)])):
        e = dose - target[...]
        excess[s][...] = e
        scores.append(SHARPNESS * e * e)
    score_sum[...] = log_sum_exp(scores)


def second_kernel(scens, whole, upper, lower, col_hot_t, order, *refs):
    del order
    *refs, rows = refs
    n = len(scens)
    sums, refs = refs[: -3 * n], refs[-3 * n :]
    excess, weights, gradient = refs[:n], refs[n : 2 * n], refs[2 * n :]
    total = log_sum_exp([x[...] for x in sums])
    picked = []
    for m, s in enumerate(scens):
        e = excess[m][...]
        w = jnp.exp(SHARPNESS * e * e - total)
        weights[m][...] = w
        picked.append((s, 2.0 * w * e))
    products(whole, upper, lower, picked, rows)
    for m, g in enumerate(exact(col_hot_t[...], [rows[m] for m in range(n)])):
        gradient[m][...] = g


def third_kernel(
    scens, whole, upper, lower, whole_t, upper_t, lower_t, fluence, target,
    col_hot, col_hot_t, same, *refs
):
    *refs, rows, held = refs
    n = len(scens)
    grad_a, grad_b, weights, refs = refs[:n], refs[n : 2 * n], refs[2 * n : 3 * n], refs[3 * n :]
    together = len(refs[-1].shape) == 4
    others = refs[: len(refs) - n - (1 if together else n)]
    copies = refs[len(others) : len(others) + n]
    gradient = refs[len(others) + n :]
    share = copies[0].shape[0]
    mine = pl.ds(0 if share == held.shape[1] else lax.axis_index("vox") * share, share)
    for m in range(n):
        step = STEP_SIZE * (grad_a[m][...] + grad_b[m][...])
        held[m] = jnp.maximum(fluence[...] - step, 0.0)
        copies[m][...] = held[m, mine]
    picked = exact(col_hot[...], [held[m] for m in range(n)])
    products(whole_t, upper_t, lower_t, list(zip(scens, picked)), rows)
    doses = exact(same[...], [rows[m] for m in range(n)])
    picked = [2.0 * weights[m][...] * (doses[m] - target[...]) for m in range(n)]
    products(whole, upper, lower, list(zip(scens, picked)), rows)
    found = exact(col_hot_t[...], [rows[m] for m in range(n)])
    if not together:
        for m, g in enumerate(found):
            gradient[m][...] = g
        return
    parts, _, *piece = gradient[0].shape
    for m, g in enumerate([*(x[...] for x in others), *found]):
        gradient[0][:, m] = g.reshape(parts, *piece)


def place_kernel(scen_total, leads, order, *refs):
    del order
    used = jnp.sum(leads[...].astype(F32), axis=1, keepdims=True)
    *weights, placed = refs
    for s, w in enumerate(exact(leads[...], [x[...] for x in weights])):
        placed[:, s] = jnp.where(used == 0.0, 1.0 / scen_total, w)


def near(x):
    return pltpu.with_memory_space_constraint(x, pltpu.VMEM)


def far(x):
    return pltpu.with_memory_space_constraint(x, pltpu.HBM)


def swap(x, axis, bit):
    return lax.ppermute(x, axis, [(i, i ^ bit) for i in range(lax.axis_size(axis))])


def bits(axis):
    size = lax.axis_size(axis)
    if size & (size - 1) or size < 2:
        raise ValueError("axis size")
    return [1 << b for b in range(size.bit_length() - 1)]


def reduce_vox(x):
    steps = bits("vox")
    orders = [steps, steps]
    if len(steps) > 2:
        first, far, *between = steps[0], steps[-1], *steps[1:-1]
        orders = [[far, first, *between], [first, far, *between]]
    other = None
    for pair in zip(*orders):
        if other is not None:
            x = x + other
        other = lax.ppermute(
            x,
            "vox",
            [(v, v ^ pair[(v & steps[-2]) // steps[-2]]) for v in range(lax.axis_size("vox"))],
        )
    return x, other


def reduce_scen(x, combine):
    steps = bits("scen")
    x = [x, swap(x, "scen", steps[0])]
    for bit in steps[1:]:
        both = combine(x)
        x = [both, swap(both, "scen", bit ^ 1)]
    return x


def spread_scen(x):
    return [x] + [swap(x, "scen", n) for n in range(1, lax.axis_size("scen"))]


def swap_both(x, bit):
    scen, vox = lax.axis_size("scen"), lax.axis_size("vox")
    pairs = [(s * vox + v, (s ^ 1) * vox + (v ^ bit)) for s in range(scen) for v in range(vox)]
    return lax.ppermute(x, ("scen", "vox"), pairs)


def split(total, parts):
    return [total * (n + 1) // parts - total * n // parts for n in range(parts)]


def body(dose_blocks, block_map, block_counts, target, fluence_init):
    scen, slots, side, _ = dose_blocks.shape
    share = fluence_init.shape[0]
    parts = lax.axis_size("vox")
    beam_blocks = share * parts // side
    row_blocks = target.shape[0] // side
    scen_total = scen * lax.axis_size("scen")
    params = pltpu.CompilerParams(vmem_limit_bytes=16 * 2**20)
    passes = scen * slots * side * side
    dense = lambda *shape: jax.ShapeDtypeStruct(shape, F32)

    fluence = fluence_init.reshape(share // side, side)
    half = lambda *shape: jax.ShapeDtypeStruct(shape, BF16)
    kept = slots * 2 // 5
    kept += (slots - kept) % 2
    rest = slots - kept
    sizes = split(kept, 4)
    col_hot, col_hot_t, same, leads, target, mine, whole, whole_t = pl.pallas_call(
        functools.partial(hot_kernel, sizes),
        name="hot",
        out_shape=(
            half(slots, beam_blocks),
            half(beam_blocks, slots),
            half(slots, slots),
            half(row_blocks, slots),
            dense(slots, side),
            dense(*fluence.shape),
            pltpu.VMEM((scen, kept, side, side), F32),
            pltpu.VMEM((scen, kept, side, side), F32),
        ),
        in_specs=[FAR] * 3 + [VMEM, FAR],
        out_specs=(VMEM,) * 8,
        scratch_shapes=[
            pltpu.VMEM((2, slots), jnp.int32),
            pltpu.VMEM((row_blocks, side), F32),
            pltpu.SemaphoreType.DMA((3 + len(sizes),)),
        ],
        compiler_params=params,
        cost_estimate=pl.CostEstimate(flops=0, bytes_accessed=3 * passes, transcendentals=0),
    )(
        far(block_map.T),
        far(fluence),
        far(target.reshape(row_blocks, side)),
        block_counts.reshape(1, 1),
        far(dose_blocks),
    )

    neighbours = min(4, parts)
    order = fluence
    found = [mine] + [swap_both(fluence, n) for n in range(1, neighbours)]
    fluence = pl.pallas_call(
        collect_kernel,
        name="collect",
        out_shape=dense(neighbours * mine.shape[0], side),
        in_specs=[VMEM] * neighbours,
        out_specs=VMEM,
        compiler_params=params,
    )(*found)
    for bit in bits("vox"):
        if bit < neighbours:
            continue
        other = swap_both(fluence, bit)
        order = fluence
        fluence = pl.pallas_call(
            functools.partial(join_kernel, bit),
            name="join",
            out_shape=dense(2 * fluence.shape[0], side),
            in_specs=[VMEM] * 2,
            out_specs=VMEM,
            compiler_params=params,
        )(fluence, other)
    sizes = split(rest, 6)
    upper, upper_t, lower, lower_t = pl.pallas_call(
        functools.partial(split_kernel, sizes),
        name="split",
        out_shape=(pltpu.VMEM((scen, rest, 2 * side, side), BF16),) * 2
        + (pltpu.VMEM((scen, rest // 2, 2 * side, side), BF16),) * 2,
        in_specs=[FAR, VMEM],
        out_specs=(VMEM,) * 4,
        scratch_shapes=[
            pltpu.VMEM((scen, rest, side, side), F32),
            pltpu.SemaphoreType.DMA((len(sizes),)),
        ],
        compiler_params=params,
        cost_estimate=pl.CostEstimate(flops=0, bytes_accessed=5 * passes, transcendentals=0),
    )(far(dose_blocks), order)
    blocks = [near(x) for x in (whole, upper, lower)]
    flipped = [near(x) for x in (whole_t, upper_t, lower_t)]

    for outer_round in range(ROUNDS):
        last = outer_round == ROUNDS - 1
        *excess, score_sum = pl.pallas_call(
            first_kernel,
            name="first",
            out_shape=(dense(slots, side),) * (scen + 1),
            in_specs=[VMEM] * 7,
            out_specs=(VMEM,) * (scen + 1),
            scratch_shapes=[pltpu.VMEM((scen, slots, side), F32)],
            compiler_params=params,
        )(*flipped, fluence, target, col_hot, same)
        score_sums = spread_scen(score_sum)

        groups = [[s] for s in range(scen)] if last else [list(range(scen))]
        weights, gradients, order = [], [], score_sum
        for group in groups:
            n = len(group)
            found = pl.pallas_call(
                functools.partial(second_kernel, group),
                name="second",
                out_shape=(dense(slots, side),) * n + (dense(beam_blocks, side),) * n,
                in_specs=[VMEM] * (5 + len(score_sums) + n),
                out_specs=(VMEM,) * (2 * n),
                scratch_shapes=[pltpu.VMEM((n, slots, side), F32)],
                compiler_params=params,
            )(*blocks, col_hot_t, order, *score_sums, *[excess[s] for s in group])
            order = found[-1]
            weights += found[:n]
            gradients += found[n:]
        sums = [reduce_vox(gradient) for gradient in gradients]
        groups = [[s] for s in range(scen)]
        copies, gradients = [], []
        for group in groups:
            n = len(group)
            together = last and group is groups[-1]
            others = gradients if together else []
            form = [(parts, scen, share // side, side)] if together else [(beam_blocks, side)] * n
            found = pl.pallas_call(
                functools.partial(third_kernel, group),
                name="third",
                out_shape=(dense(share // side if last else beam_blocks, side),) * n
                + tuple(dense(*shape) for shape in form),
                in_specs=[VMEM] * (11 + 3 * n + len(others)),
                out_specs=(VMEM,) * (n + len(form)),
                scratch_shapes=[
                    pltpu.VMEM((n, slots, side), F32),
                    pltpu.VMEM((n, beam_blocks, side), F32),
                ],
                compiler_params=params,
            )(
                *blocks, *flipped, fluence, target, col_hot, col_hot_t, same,
                *[sums[s][0] for s in group], *[sums[s][1] for s in group],
                *[weights[s] for s in group], *others,
            )
            copies += found[:n]
            gradients += found[n:]
        if not last:
            sums = [reduce_vox(gradient) for gradient in gradients]
            gradients = [a + b for a, b in sums]
        else:
            gradient, copies = lax.optimization_barrier((gradients[-1], copies))
            gradient = lax.all_to_all(gradient, "vox", split_axis=0, concat_axis=0, tiled=True)
            gradient = jnp.sum(gradient, axis=0)
            gradients = [gradient[s] for s in range(scen)]
        copies = [jnp.maximum(c - STEP_SIZE * g, 0.0) for c, g in zip(copies, gradients)]
        total = functools.reduce(jnp.add, copies)
        totals = spread_scen(total) if last else reduce_scen(total, sum)
        if last:
            placed = pl.pallas_call(
                functools.partial(place_kernel, scen_total),
                name="place",
                out_shape=dense(row_blocks, scen, side),
                in_specs=[VMEM] * (2 + scen),
                out_specs=VMEM,
                compiler_params=params,
                cost_estimate=pl.CostEstimate(
                    flops=0, bytes_accessed=8 * scen * row_blocks * side, transcendentals=0
                ),
            )(leads, total, *weights)
            weights = jnp.swapaxes(placed, 0, 1).reshape(scen, row_blocks * side)
        fluence = functools.reduce(jnp.add, totals) / scen_total
    return fluence.reshape(share), weights


def solution(mesh):
    placed = (P("scen", "vox", None, None), P("vox", None), P("vox"), P("vox"), P("vox"))
    return jax.shard_map(
        body, mesh=mesh, in_specs=placed, out_specs=(P("vox"), P("scen", "vox")), check_vma=False
    )
```
